32 devices in a mesh: trade: 4 (over z), path: 8 (over y, x, core).
Axes of the slice: x: 2, y: 2, z: 4, core: 2. Of those that a mesh axis runs over, the one named last changes fastest.
Arguments:
- start_state: float32 [4096, 32], P('path'), may hold values from -6 to 6
- shocks: float32 [2, 4096, 32], P(None, 'path'), may hold values from -6 to 6
- loadings: float32 [32, 32768], P(None, 'trade'), may hold values from -1 to 1
- strikes: float32 [32768], P('trade'), may hold values from -0.5 to 1
- notionals: float32 [32768], P('trade'), may hold values from -1 to 1
- trade_set: int32 [32768], P('trade'), may hold values from 0 to 1023
- live_counts: int32 [4], replicated, may hold values from 1 to 8192, 24576 in all
- weights: int32 [4096], P('path'), may hold values from 1 to 16
- thresholds: int32 [1024], P('trade'), may hold values from 0 to 8
Outputs:
- exposure: float32 [2, 1024, 4096], P(None, 'trade', 'path')
- expected: float32 [2, 1024], P(None, 'trade')
The draws below stay inside these ranges and needn't reach their ends.
Inputs may be any that keep to these rules, and one draw needn't show every extreme that they name: The live slots of group g are its first live_counts[g] slots; the counts sum to 24576 and some group is full.
All inputs are finite; a program needn't handle non-finite values.
Results may differ from the reference program's by a relative error of at most 0.0003.
Values sent between devices are 32-bit elements; how exact they have to be, the bound alone decides.
No kernel may reach another device: no remote copies, remote signals or barrier semaphores. Data moves between devices by JAX's collectives and lax.ppermute only.
A program may use at most 128 MiB of HBM per device.

```python
import math
import jax
import jax.numpy as jnp
import numpy as np
from jax import lax

NF = 32
DATES = 2
TR_DEV = 8192
GROUPS = 4
PATHS = 4096
TRADES = 32768
NSETS = 1024
LIVE = 24576


def place_ends(array, stream_key, low, top_value):
    spot = [jax.random.randint(jax.random.fold_in(stream_key, axis), (), 0, length) for axis, length in enumerate(array.shape)]
    longest = array.shape.index(max(array.shape))
    neighbour = spot[:longest] + [(spot[longest] + 1) % array.shape[longest]] + spot[longest + 1:]
    return array.at[tuple(spot)].set(low).at[tuple(neighbour)].set(top_value)


def level_of(rng, dims, split, low, top_value):
    def one(dim, shards_of):
        draws = jax.random.uniform(jax.random.fold_in(jax.random.fold_in(rng, 6), dim), (shards_of,), jnp.float32, low / len(split), top_value / len(split))
        return jnp.repeat(jnp.exp(draws), dims[dim] // shards_of).reshape((-1,) + (1,) * (len(dims) - dim - 1))

    level = one(*split[0])
    for cut in split[1:]:
        level = level * one(*cut)
    return level


def split_up(amount, total, limit, lean):
    loads = [(1 << 20) // math.isqrt(standing ** lean) + 1 for standing in range(2, amount + 1)]
    rest, given = total - limit - (amount - 1), [1] * (amount - 1)
    while rest > 0:
        movable = [i for i in range(amount - 1) if given[i] < limit]
        pool, remaining = sum([loads[i] for i in movable]), rest
        for i in movable:
            extra = min(limit - given[i], max(1, remaining * loads[i] // pool), rest)
            given[i] = given[i] + extra
            rest = rest - extra
    return np.array([limit] + given)


def uneven(stream_key, number_of, total, bound, slope):
    if number_of == 2:
        one = jax.random.randint(stream_key, (), max(1, total - bound), min(bound, total - 1) + 1)
        return jnp.stack([one, total - one])
    sizes = jnp.asarray(split_up(number_of, total, bound, slope), jnp.int32)
    couples = (number_of - 1) // 2
    donor, taker = sizes[1:1 + 2 * couples:2], sizes[2:2 + 2 * couples:2]
    slack = jnp.minimum(donor - 1, bound - taker)
    shifted = jax.random.randint(jax.random.fold_in(stream_key, 1), (couples,), 0, 1 << 20) % (slack + 1)
    sizes = sizes.at[1:1 + 2 * couples:2].set(donor - shifted).at[2:2 + 2 * couples:2].set(taker + shifted)
    return sizes[jax.random.permutation(jax.random.fold_in(stream_key, 2), number_of)]


def normal_values(stream_key, dims, width, most, shards=(), kind=jnp.bfloat16):
    entries = jax.random.normal(stream_key, dims, jnp.float32) * width
    if len(shards) > 0:
        entries = level_of(stream_key, dims, shards, -0.22, 0.18) * entries
    return jnp.clip(entries, min=-most, max=most).astype(kind)


def setup_inputs(seed: int = 0) -> dict:
    keys = jax.random.split(jax.random.key(seed), 10)
    return {
        "start_state": normal_values(keys[0], (PATHS, NF), 1.0, 6.0, ((0, 8),), jnp.float32),
        "shocks": normal_values(keys[1], (DATES, PATHS, NF), 1.0, 6.0, ((1, 8),), jnp.float32),
        "loadings": normal_values(keys[2], (NF, TRADES), NF ** -0.5, 1.0, ((1, 4),), jnp.float32),
        "strikes": jnp.clip(-0.5 + 1.5 * jax.random.uniform(keys[3], (TRADES,), jnp.float32) ** level_of(keys[3], (TRADES,), ((0, 4),), -0.2, 0.2), -0.5, 1.0),
        "notionals": jnp.clip(jax.random.uniform(keys[4], (TRADES,), jnp.float32, -1.0, 1.0) * level_of(keys[4], (TRADES,), ((0, 4),), -0.4, 0.0), -1.0, 1.0),
        "trade_set": place_ends(jax.random.randint(keys[5], (TRADES,), 0, NSETS), jax.random.fold_in(keys[5], 1), 0, NSETS - 1).astype(jnp.int32),
        "live_counts": uneven(keys[6], GROUPS, LIVE, TR_DEV, 2).astype(jnp.int32),
        "weights": place_ends(jax.random.randint(keys[7], (PATHS,), 1, 17), jax.random.fold_in(keys[7], 1), 1, 16).astype(jnp.int32),
        "thresholds": place_ends(jax.random.randint(keys[8], (NSETS,), 0, 9), jax.random.fold_in(keys[8], 1), 0, 8).astype(jnp.int32),
    }


HIGHEST_PREC = lax.Precision.HIGHEST
ROOT_HALF = 0.7071067811865476

def make_basis(state):
    return jnp.concatenate([state, (state * state - 1.0) * ROOT_HALF], axis=1)

def reference(start_state, shocks, loadings, strikes, notionals, trade_set, live_counts, weights, thresholds):
    weight_vals = weights.astype(jnp.float32)
    states = [start_state]
    for date_idx in range(DATES):
        states.append(0.8 * states[-1] + 0.6 * shocks[date_idx])
    slots = jnp.arange(TRADES, dtype=jnp.int32)
    owners = slots // TR_DEV
    live = (slots % TR_DEV < live_counts[owners]).astype(jnp.float32)
    scaled = notionals * live
    limits = 0.25 * thresholds.astype(jnp.float32)
    exposures = []
    expects = []
    for date_idx in range(DATES):
        basis_vals = make_basis(states[date_idx])
        weighted = basis_vals * weight_vals[:, None]
        gram_total = jnp.dot(weighted.T, basis_vals, precision=HIGHEST_PREC)
        future = states[date_idx + 1]

        def block_step(netted, block_idx):
            begin = (block_idx * TR_DEV).astype(jnp.int32)
            load_block = lax.dynamic_slice_in_dim(loadings, begin, TR_DEV, 1)
            strike_block = lax.dynamic_slice_in_dim(strikes, begin, TR_DEV, 0)
            scale_block = lax.dynamic_slice_in_dim(scaled, begin, TR_DEV, 0)
            set_block = lax.dynamic_slice_in_dim(trade_set, begin, TR_DEV, 0)
            cashflow = scale_block * jnp.maximum(jnp.dot(future, load_block, precision=HIGHEST_PREC) - strike_block, 0.0)
            moment = jnp.dot(weighted.T, cashflow, precision=HIGHEST_PREC)
            coeffs = jnp.linalg.solve(gram_total, moment)
            values = jnp.dot(coeffs.T, basis_vals.T, precision=HIGHEST_PREC)
            netted = netted + jax.ops.segment_sum(values, set_block, num_segments=NSETS)
            return (netted, None)
        netted, _ = lax.scan(block_step, jnp.zeros((NSETS, PATHS), jnp.float32), jnp.arange(GROUPS, dtype=jnp.int32))
        clamped = jnp.maximum(netted - limits[:, None], 0.0)
        exposures.append(clamped)
        expects.append(jnp.dot(clamped, weight_vals, precision=HIGHEST_PREC) / jnp.sum(weight_vals))
    return (jnp.stack(exposures), jnp.stack(expects))
```

```python
import functools

import jax
import jax.numpy as jnp
from jax import lax
from jax.experimental import pallas as pl
from jax.experimental.pallas import tpu as pltpu
from jax.sharding import PartitionSpec as P

HIGHEST_PREC = lax.Precision.HIGHEST
ROOT_HALF = 0.7071067811865476
F32 = jnp.float32
BF16 = jnp.bfloat16
TILE = 512
DEPTH = 256
VMEM_BYTES = 56 * 1024 * 1024
NN = (((1,), (0,)), ((), ()))
NT = (((1,), (1,)), ((), ()))


def mm(a, b, dims=NN):
    return lax.dot_general(a, b, dims, preferred_element_type=F32)


def mm_full(a, b, dims=NN):
    return lax.dot_general(a, b, dims, preferred_element_type=F32, precision=HIGHEST_PREC)


def split2(x):
    hi = x.astype(BF16)
    return hi, (x - hi.astype(F32)).astype(BF16)


def split3(x):
    hi = x.astype(BF16)
    rest = x - hi.astype(F32)
    mid = rest.astype(BF16)
    return hi, mid, (rest - mid.astype(F32)).astype(BF16)


def basis_rows(state):
    return jnp.concatenate([state, (state * state - 1.0) * ROOT_HALF], axis=0)


def moment_kernel(
    counts_ref, start_ref, shocks_ref, weights_ref, load_ref, strike_ref, notional_ref, set_ref,
    net_ref, states_scr, wide_scr, load_scr,
):
    factors, paths = start_ref.shape
    dates = shocks_ref.shape[0]
    slots = load_ref.shape[1]
    sets = net_ref.shape[0]
    filled = counts_ref[lax.axis_index("trade")]

    weight_row = weights_ref[...].astype(F32)
    state = start_ref[...]
    ones = jnp.where(lax.broadcasted_iota(jnp.int32, (DEPTH - 6 * factors, paths), 0) < 3, 1.0, 0.0)
    for date in range(dates):
        hi, lo = split2(basis_rows(state) * weight_row)
        wide_scr[date] = jnp.concatenate([hi, lo], axis=0)
        state = 0.8 * state + 0.6 * shocks_ref[date]
        hi, mid, low = split3(state)
        hi, mid, low = hi.astype(F32), mid.astype(F32), low.astype(F32)
        stacked = jnp.concatenate([hi, hi, mid, mid, hi, low, ones], axis=0)
        states_scr[pl.ds(date * paths, paths), :] = stacked.T.astype(BF16)
    net_ref[...] = jnp.zeros_like(net_ref)
    load_scr[...] = jnp.zeros_like(load_scr)

    def step(index, carry):
        cols = pl.ds(pl.multiple_of(index * TILE, TILE), TILE)
        hi, mid, low = split3(load_ref[:, cols])
        for part, piece in enumerate((hi, mid, hi, mid, low, hi)):
            load_scr[pl.ds(part * factors, factors), :] = piece
        s_hi, s_mid, s_low = split3(-strike_ref[:, cols])
        rows = lax.broadcasted_iota(jnp.int32, (16, TILE), 0)
        strike_rows = jnp.where(
            rows == 0, s_hi.astype(F32), jnp.where(rows == 1, s_mid.astype(F32), jnp.where(rows == 2, s_low.astype(F32), 0.0))
        )
        load_scr[pl.ds(6 * factors, 16), :] = strike_rows.astype(BF16)
        slot_ids = index * TILE + lax.broadcasted_iota(jnp.int32, (1, TILE), 1)
        scaled = jnp.where(slot_ids < filled, notional_ref[:, cols], 0.0)
        his, los = [], []
        for date in range(dates):
            pay = mm(states_scr[pl.ds(date * paths, paths), :], load_scr[...])
            hi, lo = split2(jnp.maximum(pay, 0.0))
            wide = 2 * factors
            both = mm(wide_scr[date], hi)
            moment = both[:wide] + both[wide:] + mm(wide_scr[date, :wide], lo)
            hi, lo = split2(moment * scaled)
            his.append(hi)
            los.append(lo)
        stacked = jnp.concatenate(his + los, axis=0)
        one_hot = jnp.where(
            lax.broadcasted_iota(jnp.int32, (sets, TILE), 0) == set_ref[:, cols], 1.0, 0.0
        ).astype(BF16)
        summed = mm(one_hot, stacked, NT)
        half = summed.shape[1] // 2
        net_ref[...] += summed[:, :half] + summed[:, half:]
        return carry

    lax.fori_loop(0, slots // TILE, step, 0)


def inverse_kernel(start_ref, shock_ref, weights_ref, inverse_ref):
    blocks, factors, _ = start_ref.shape
    dates = inverse_ref.shape[0]
    wide = 2 * factors
    sub = lax.broadcasted_iota(jnp.int32, (wide, wide), 0)
    lane = lax.broadcasted_iota(jnp.int32, (wide, wide), 1)

    def step(block, grams):
        weight_row = weights_ref[block].astype(F32)
        state = start_ref[block]
        results = []
        for date in range(dates):
            if date > 0:
                state = 0.8 * state + 0.6 * shock_ref[date - 1, block]
            basis = basis_rows(state)
            results.append(grams[date] + mm_full(basis * weight_row, basis, NT))
        return tuple(results)

    grams = lax.fori_loop(0, blocks, step, tuple(jnp.zeros((wide, wide), F32) for _ in range(dates)))
    work = list(grams)
    for k in range(wide):
        for date in range(dates):
            mat = work[date]
            row = mat[k : k + 1, :]
            col = mat[:, k : k + 1]
            pivot = 1.0 / mat[k : k + 1, k : k + 1]
            row = jnp.where(lane[:1] == k, 1.0, row) * pivot
            work[date] = jnp.where(sub == k, row, jnp.where(lane == k, 0.0, mat) - col * row)
    eye = jnp.where(sub == lane, 1.0, 0.0)
    for date in range(dates):
        approx = work[date]
        inverse_ref[date] = approx + mm_full(approx, eye - mm_full(grams[date], approx))


def exposure_kernel(
    totals_ref, inverse_ref, start_ref, shock_ref, weights_ref, limits_ref, exposure_ref, expected_ref
):
    blocks, factors, paths = start_ref.shape
    dates = inverse_ref.shape[0]
    wide = 2 * factors
    mine = lax.axis_index("path")
    limits = 0.25 * limits_ref[...].astype(F32)
    coeffs = []
    for date in range(dates):
        hi, lo = split2(mm_full(totals_ref[:, date * wide : (date + 1) * wide], inverse_ref[date]))
        coeffs.append(jnp.concatenate([hi, hi, lo], axis=1))

    def netted(block):
        state = start_ref[block]
        results = []
        for date in range(dates):
            if date > 0:
                state = 0.8 * state + 0.6 * shock_ref[date - 1, block]
            hi, lo = split2(basis_rows(state))
            value = mm(coeffs[date], jnp.concatenate([hi, lo, hi], axis=0))
            results.append(jnp.maximum(value - limits, 0.0))
        return results

    own = netted(mine)
    for date in range(dates):
        exposure_ref[date] = own[date]

    def step(block, carry):
        weight_row = weights_ref[block].astype(F32)
        sums, total = carry
        results = []
        parts = netted(block)
        for date in range(dates):
            product = parts[date] * weight_row
            partial = sums[date]
            for c in range(paths // 128):
                partial = partial + product[:, c * 128 : (c + 1) * 128]
            results.append(partial)
        return (tuple(results), total + jnp.sum(weight_row, keepdims=True))

    sets = limits.shape[0]
    sums, total = lax.fori_loop(
        0, blocks, step,
        (tuple(jnp.zeros((sets, 128), F32) for _ in range(dates)), jnp.zeros((1, 1), F32)),
    )
    for date in range(dates):
        expected_ref[date : date + 1, :] = jnp.sum(sums[date].T, axis=0, keepdims=True) / total


def body(
    start_state, shocks, loadings, strikes, notionals, trade_set, live_counts, weights, thresholds
):
    paths, factors = start_state.shape
    dates = shocks.shape[0]
    slots = loadings.shape[1]
    owned = thresholds.shape[0]
    groups = lax.axis_size("trade")
    ranks = lax.axis_size("path")
    sets = owned * groups
    wide = 2 * factors

    start_t = start_state.T
    shocks_t = jnp.swapaxes(shocks, 1, 2)
    weights_row = weights[None, :]
    vmem = pl.BlockSpec(memory_space=pltpu.VMEM)
    smem = pl.BlockSpec(memory_space=pltpu.SMEM)
    params = pltpu.CompilerParams(vmem_limit_bytes=VMEM_BYTES)

    all_start = lax.all_gather(start_t, "path")
    all_shocks = [lax.all_gather(shocks_t[date], "path") for date in range(dates - 1)]
    all_shocks = jnp.stack(all_shocks) if len(all_shocks) > 1 else all_shocks[0][None]
    all_weights = lax.all_gather(weights_row, "path")

    net = pl.pallas_call(
        moment_kernel,
        out_shape=jax.ShapeDtypeStruct((sets, dates * wide), F32),
        in_specs=[smem] + [vmem] * 7,
        out_specs=vmem,
        scratch_shapes=[
            pltpu.VMEM((dates * paths, DEPTH), BF16),
            pltpu.VMEM((dates, 2 * wide, paths), BF16),
            pltpu.VMEM((DEPTH, TILE), BF16),
        ],
        compiler_params=params,
        cost_estimate=pl.CostEstimate(flops=16 * 10**9, bytes_accessed=4 * 10**6, transcendentals=0),
        name="net_moments",
    )(
        live_counts, start_t, shocks_t, weights_row, loadings, strikes[None, :], notionals[None, :],
        trade_set[None, :],
    )
    share = lax.psum_scatter(net, ("trade", "path"), scatter_dimension=0, tiled=True)

    inverse = pl.pallas_call(
        inverse_kernel,
        out_shape=jax.ShapeDtypeStruct((dates, wide, wide), F32),
        in_specs=[vmem] * 3,
        out_specs=vmem,
        compiler_params=params,
        cost_estimate=pl.CostEstimate(flops=8 * 10**9, bytes_accessed=10**6, transcendentals=0),
        name="gram_inverse",
    )(all_start, all_shocks, all_weights)

    totals = lax.all_gather(share, "path", axis=0, tiled=True)

    exposure, expected = pl.pallas_call(
        exposure_kernel,
        out_shape=(
            jax.ShapeDtypeStruct((dates, owned, paths), F32),
            jax.ShapeDtypeStruct((dates, owned), F32),
        ),
        in_specs=[vmem] * 6,
        out_specs=(vmem, vmem),
        compiler_params=params,
        cost_estimate=pl.CostEstimate(flops=2 * 10**9, bytes_accessed=2 * 10**6, transcendentals=0),
        name="set_exposure",
    )(totals, inverse, all_start, all_shocks, all_weights, thresholds[:, None])
    return (exposure, expected)


def solution(mesh):
    placed = (
        P("path", None),
        P(None, "path", None),
        P(None, "trade"),
        P("trade"),
        P("trade"),
        P("trade"),
        P(),
        P("path"),
        P("trade"),
    )
    return jax.shard_map(
        body,
        mesh=mesh,
        in_specs=placed,
        out_specs=(P(None, "trade", "path"), P(None, "trade")),
        check_vma=False,
    )
```

```python
import functools

import jax
import jax.numpy as jnp
from jax import lax
from jax.experimental import pallas as pl
from jax.experimental.pallas import tpu as pltpu
from jax.sharding import PartitionSpec as P

HIGHEST_PREC = lax.Precision.HIGHEST
ROOT_HALF = 0.7071067811865476
F32 = jnp.float32
BF16 = jnp.bfloat16
TILE = 512
DEPTH = 256
MIB = 1024 * 1024
NN = (((1,), (0,)), ((), ()))
NT = (((1,), (1,)), ((), ()))


def mm(a, b, dims=NN):
    return lax.dot_general(a, b, dims, preferred_element_type=F32)


def mm_full(a, b, dims=NN):
    return lax.dot_general(a, b, dims, preferred_element_type=F32, precision=HIGHEST_PREC)


def split2(x):
    hi = x.astype(BF16)
    return hi, (x - hi.astype(F32)).astype(BF16)


def split3(x):
    hi = x.astype(BF16)
    rest = x - hi.astype(F32)
    mid = rest.astype(BF16)
    return hi, mid, (rest - mid.astype(F32)).astype(BF16)


def basis_rows(state):
    return jnp.concatenate([state, (state * state - 1.0) * ROOT_HALF], axis=0)


def moment_kernel(
    counts_ref, start_ref, shocks_ref, weights_ref, load_ref, strike_ref, notional_ref, set_ref,
    keep_ref, send_ref, states_scr, wide_scr, load_scr, net_ref,
    *, groups, ranks,
):
    factors, paths = start_ref.shape
    dates = shocks_ref.shape[0]
    slots = load_ref.shape[1]
    sets = net_ref.shape[0]
    group, rank = lax.axis_index("trade"), lax.axis_index("path")
    filled = counts_ref[group]
    rows_bits = log2(sets // (groups * ranks))

    weight_row = weights_ref[...].astype(F32)
    state = start_ref[...]
    ones = jnp.where(lax.broadcasted_iota(jnp.int32, (DEPTH - 6 * factors, paths), 0) < 3, 1.0, 0.0)
    for date in range(dates):
        hi, lo = split2(basis_rows(state) * weight_row)
        wide_scr[date] = jnp.concatenate([hi, lo], axis=0)
        state = 0.8 * state + 0.6 * shocks_ref[date]
        hi, mid, low = split3(state)
        hi, mid, low = hi.astype(F32), mid.astype(F32), low.astype(F32)
        stacked = jnp.concatenate([hi, hi, mid, mid, hi, low, ones], axis=0)
        states_scr[pl.ds(date * paths, paths), :] = stacked.T.astype(BF16)
    net_ref[...] = jnp.zeros_like(net_ref)
    load_scr[...] = jnp.zeros_like(load_scr)

    def step(index, carry):
        cols = pl.ds(pl.multiple_of(index * TILE, TILE), TILE)
        hi, mid, low = split3(load_ref[:, cols])
        for part, piece in enumerate((hi, mid, hi, mid, low, hi)):
            load_scr[pl.ds(part * factors, factors), :] = piece
        s_hi, s_mid, s_low = split3(-strike_ref[:, cols])
        rows = lax.broadcasted_iota(jnp.int32, (16, TILE), 0)
        strike_rows = jnp.where(
            rows == 0, s_hi.astype(F32), jnp.where(rows == 1, s_mid.astype(F32), jnp.where(rows == 2, s_low.astype(F32), 0.0))
        )
        load_scr[pl.ds(6 * factors, 16), :] = strike_rows.astype(BF16)
        slot_ids = index * TILE + lax.broadcasted_iota(jnp.int32, (1, TILE), 1)
        scaled = jnp.where(slot_ids < filled, notional_ref[:, cols], 0.0)
        his, los = [], []
        for date in range(dates):
            pay = mm(states_scr[pl.ds(date * paths, paths), :], load_scr[...])
            hi, lo = split2(jnp.maximum(pay, 0.0))
            wide = 2 * factors
            both = mm(wide_scr[date], hi)
            moment = both[:wide] + both[wide:] + mm(wide_scr[date, :wide], lo)
            hi, lo = split2(moment * scaled)
            his.append(hi)
            los.append(lo)
        stacked = jnp.concatenate(his + los, axis=0)
        set_ids = set_ref[:, cols]
        to_rank = ((set_ids >> rows_bits) & (ranks - 1)) ^ rank
        to_group = (set_ids >> (rows_bits + log2(ranks))) ^ group
        places = (to_rank & 1) * (ranks // 2) + (to_rank >> 1)
        places = ((places * groups + to_group) << rows_bits) + (set_ids & ((1 << rows_bits) - 1))
        one_hot = jnp.where(
            lax.broadcasted_iota(jnp.int32, (sets, TILE), 0) == places, 1.0, 0.0
        ).astype(BF16)
        summed = mm(one_hot, stacked, NT)
        half = summed.shape[1] // 2
        net_ref[...] += summed[:, :half] + summed[:, half:]
        return carry

    lax.fori_loop(0, slots // TILE, step, 0)
    keep_ref[...] = net_ref[: sets // 2]
    send_ref[...] = net_ref[sets // 2 :]


def add_kernel(count, *refs):
    outs = refs[count:]
    rows = outs[0].shape[0]
    for part, out in enumerate(outs):
        cut = pl.ds(part * rows, rows)
        total = refs[0][cut, :]
        for ref in refs[1:count]:
            total = total + ref[cut, :]
        out[...] = total


def states_of(ref, factors, dates):
    state = ref[:factors, :]
    yield state
    for date in range(1, dates):
        state = 0.8 * state + 0.6 * ref[date * factors : (date + 1) * factors, :]
        yield state


def weights_of(ref, factors, dates):
    return ref[dates * factors : dates * factors + 1, :]


def inverse_kernel(factors, dates, *refs):
    blocks, inverse_ref = refs[:-1], refs[-1]
    wide = 2 * factors
    sub = lax.broadcasted_iota(jnp.int32, (wide, wide), 0)
    lane = lax.broadcasted_iota(jnp.int32, (wide, wide), 1)
    grams = [jnp.zeros((wide, wide), F32) for _ in range(dates)]
    for block in blocks:
        weight_row = weights_of(block, factors, dates)
        for date, state in enumerate(states_of(block, factors, dates)):
            basis = basis_rows(state)
            grams[date] = grams[date] + mm_full(basis * weight_row, basis, NT)
    work = list(grams)
    for k in range(wide):
        for date in range(dates):
            mat = work[date]
            row = mat[k : k + 1, :]
            col = mat[:, k : k + 1]
            pivot = 1.0 / mat[k : k + 1, k : k + 1]
            row = jnp.where(lane[:1] == k, 1.0, row) * pivot
            work[date] = jnp.where(sub == k, row, jnp.where(lane == k, 0.0, mat) - col * row)
    eye = jnp.where(sub == lane, 1.0, 0.0)
    for date in range(dates):
        approx = work[date]
        inverse_ref[date] = approx + mm_full(approx, eye - mm_full(grams[date], approx))


def exposure_kernel(factors, dates, ranks, *refs):
    shares, blocks = refs[:ranks], refs[ranks : 2 * ranks]
    inverse_ref, limits_ref, exposure_ref, expected_ref, totals_scr = refs[2 * ranks :]
    wide = 2 * factors
    paths = blocks[0].shape[1]
    rank = lax.axis_index("path")
    rows = shares[0].shape[0]
    for away, share in enumerate(shares):
        totals_scr[pl.ds(pl.multiple_of((rank ^ away) * rows, rows), rows), :] = share[...]
    limits = 0.25 * limits_ref[...].astype(F32)
    coeffs = []
    for date in range(dates):
        hi, lo = split2(mm_full(totals_scr[:, date * wide : (date + 1) * wide], inverse_ref[date]))
        coeffs.append(jnp.concatenate([hi, hi, lo], axis=1))
    sums = [jnp.zeros((limits.shape[0], 128), F32) for _ in range(dates)]
    total = jnp.zeros((1, 1), F32)
    for away, block in enumerate(blocks):
        weight_row = weights_of(block, factors, dates)
        total = total + jnp.sum(weight_row, keepdims=True)
        for date, state in enumerate(states_of(block, factors, dates)):
            hi, lo = split2(basis_rows(state))
            value = mm(coeffs[date], jnp.concatenate([hi, lo, hi], axis=0))
            value = jnp.maximum(value - limits, 0.0)
            if away == 0:
                exposure_ref[date] = value
            product = value * weight_row
            for c in range(paths // 128):
                sums[date] = sums[date] + product[:, c * 128 : (c + 1) * 128]
    for date in range(dates):
        expected_ref[date : date + 1, :] = jnp.sum(sums[date].T, axis=0, keepdims=True) / total


def log2(n):
    assert n & (n - 1) == 0
    return n.bit_length() - 1


def swap(x, axis, away):
    return lax.ppermute(x, axis, [(i, i ^ away) for i in range(lax.axis_size(axis))])


def added(arrays, parts):
    rows, cols = arrays[0].shape
    vmem = pl.BlockSpec(memory_space=pltpu.VMEM)
    return pl.pallas_call(
        functools.partial(add_kernel, len(arrays)),
        out_shape=[jax.ShapeDtypeStruct((rows // parts, cols), F32)] * parts,
        in_specs=[vmem] * len(arrays),
        out_specs=[vmem] * parts,
        compiler_params=pltpu.CompilerParams(vmem_limit_bytes=4 * MIB),
        name="add_parts",
    )(*arrays)


def body(
    start_state, shocks, loadings, strikes, notionals, trade_set, live_counts, weights, thresholds
):
    paths, factors = start_state.shape
    dates = shocks.shape[0]
    slots = loadings.shape[1]
    owned = thresholds.shape[0]
    groups = lax.axis_size("trade")
    ranks = lax.axis_size("path")
    sets = owned * groups
    wide = 2 * factors

    start_t = start_state.T
    shocks_t = jnp.swapaxes(shocks, 1, 2)
    weights_row = weights[None, :]
    vmem = pl.BlockSpec(memory_space=pltpu.VMEM)
    smem = pl.BlockSpec(memory_space=pltpu.SMEM)

    packed = jnp.concatenate(
        [start_t]
        + [shocks_t[date] for date in range(dates - 1)]
        + [jnp.broadcast_to(weights_row.astype(F32), (8, paths))],
        axis=0,
    )
    blocks = [packed] + [swap(packed, "path", away) for away in range(1, ranks)]

    keep, send = pl.pallas_call(
        functools.partial(moment_kernel, groups=groups, ranks=ranks),
        out_shape=[jax.ShapeDtypeStruct((sets // 2, dates * wide), F32)] * 2,
        in_specs=[smem] + [vmem] * 7,
        out_specs=[vmem] * 2,
        scratch_shapes=[
            pltpu.VMEM((dates * paths, DEPTH), BF16),
            pltpu.VMEM((dates, 2 * wide, paths), BF16),
            pltpu.VMEM((DEPTH, TILE), BF16),
            pltpu.VMEM((sets, dates * wide), F32),
        ],
        compiler_params=pltpu.CompilerParams(vmem_limit_bytes=20 * MIB),
        cost_estimate=pl.CostEstimate(flops=16 * 10**9, bytes_accessed=4 * 10**6, transcendentals=0),
        name="net_moments",
    )(
        live_counts, start_t, shocks_t, weights_row, loadings, strikes[None, :], notionals[None, :],
        trade_set[None, :],
    )
    got = swap(send, "path", 1)
    chips = added([keep, got], ranks // 2)
    got = [swap(chips[away], "path", 2 * away) for away in range(1, ranks // 2)]
    by_group = added([chips[0]] + got, groups)
    got = [swap(by_group[away], "trade", away) for away in range(1, groups)]
    (share,) = added([by_group[0]] + got, 1)
    shares = [share] + [swap(share, "path", away) for away in range(1, ranks)]

    inverse = pl.pallas_call(
        functools.partial(inverse_kernel, factors, dates),
        out_shape=jax.ShapeDtypeStruct((dates, wide, wide), F32),
        in_specs=[vmem] * ranks,
        out_specs=vmem,
        compiler_params=pltpu.CompilerParams(vmem_limit_bytes=8 * MIB),
        cost_estimate=pl.CostEstimate(flops=8 * 10**9, bytes_accessed=10**6, transcendentals=0),
        name="gram_inverse",
    )(*blocks)

    exposure, expected = pl.pallas_call(
        functools.partial(exposure_kernel, factors, dates, ranks),
        out_shape=(
            jax.ShapeDtypeStruct((dates, owned, paths), F32),
            jax.ShapeDtypeStruct((dates, owned), F32),
        ),
        in_specs=[vmem] * (2 * ranks + 2),
        out_specs=(vmem, vmem),
        scratch_shapes=[pltpu.VMEM((owned, dates * wide), F32)],
        compiler_params=pltpu.CompilerParams(vmem_limit_bytes=16 * MIB),
        cost_estimate=pl.CostEstimate(flops=2 * 10**9, bytes_accessed=2 * 10**6, transcendentals=0),
        name="set_exposure",
    )(*shares, *blocks, inverse, thresholds[:, None])
    return (exposure, expected)


def solution(mesh):
    placed = (
        P("path", None),
        P(None, "path", None),
        P(None, "trade"),
        P("trade"),
        P("trade"),
        P("trade"),
        P(),
        P("path"),
        P("trade"),
    )
    return jax.shard_map(
        body,
        mesh=mesh,
        in_specs=placed,
        out_specs=(P(None, "trade", "path"), P(None, "trade")),
        check_vma=False,
    )
```

```python
import functools

import jax
import jax.numpy as jnp
from jax import lax
from jax.experimental import pallas as pl
from jax.experimental.pallas import tpu as pltpu
from jax.sharding import PartitionSpec as P

HIGHEST_PREC = lax.Precision.HIGHEST
ROOT_HALF = 0.7071067811865476
F32 = jnp.float32
BF16 = jnp.bfloat16
TILE = 512
DEPTH = 256
MIB = 1024 * 1024
NN = (((1,), (0,)), ((), ()))
NT = (((1,), (1,)), ((), ()))


def mm(a, b, dims=NN):
    return lax.dot_general(a, b, dims, preferred_element_type=F32)


def mm_full(a, b, dims=NN):
    return lax.dot_general(a, b, dims, preferred_element_type=F32, precision=HIGHEST_PREC)


def split2(x):
    hi = x.astype(BF16)
    return hi, (x - hi.astype(F32)).astype(BF16)


def split3(x):
    hi = x.astype(BF16)
    rest = x - hi.astype(F32)
    mid = rest.astype(BF16)
    return hi, mid, (rest - mid.astype(F32)).astype(BF16)


def basis_rows(state):
    return jnp.concatenate([state, (state * state - 1.0) * ROOT_HALF], axis=0)


def moment_kernel(
    counts_ref, start_ref, shocks_ref, weights_ref, load_ref, strike_ref, notional_ref, set_ref,
    net_ref, states_scr, wide_scr, load_scr,
    *, groups, ranks,
):
    factors, paths = start_ref.shape
    dates = shocks_ref.shape[0]
    slots = load_ref.shape[1]
    sets = net_ref.shape[0]
    filled = counts_ref[lax.axis_index("trade")]
    rows_bits = log2(sets // (groups * ranks))

    weight_row = weights_ref[...].astype(F32)
    state = start_ref[...]
    ones = jnp.where(lax.broadcasted_iota(jnp.int32, (DEPTH - 6 * factors, paths), 0) < 3, 1.0, 0.0)
    for date in range(dates):
        hi, lo = split2(basis_rows(state) * weight_row)
        wide_scr[date] = jnp.concatenate([hi, lo], axis=0)
        state = 0.8 * state + 0.6 * shocks_ref[date]
        hi, mid, low = split3(state)
        hi, mid, low = hi.astype(F32), mid.astype(F32), low.astype(F32)
        stacked = jnp.concatenate([hi, hi, mid, mid, hi, low, ones], axis=0)
        states_scr[pl.ds(date * paths, paths), :] = stacked.T.astype(BF16)
    net_ref[...] = jnp.zeros_like(net_ref)
    load_scr[...] = jnp.zeros_like(load_scr)

    def step(index, carry):
        cols = pl.ds(pl.multiple_of(index * TILE, TILE), TILE)
        hi, mid, low = split3(load_ref[:, cols])
        for part, piece in enumerate((hi, mid, hi, mid, low, hi)):
            load_scr[pl.ds(part * factors, factors), :] = piece
        s_hi, s_mid, s_low = split3(-strike_ref[:, cols])
        rows = lax.broadcasted_iota(jnp.int32, (16, TILE), 0)
        strike_rows = jnp.where(
            rows == 0, s_hi.astype(F32), jnp.where(rows == 1, s_mid.astype(F32), jnp.where(rows == 2, s_low.astype(F32), 0.0))
        )
        load_scr[pl.ds(6 * factors, 16), :] = strike_rows.astype(BF16)
        slot_ids = index * TILE + lax.broadcasted_iota(jnp.int32, (1, TILE), 1)
        scaled = jnp.where(slot_ids < filled, notional_ref[:, cols], 0.0)
        his, los = [], []
        for date in range(dates):
            pay = mm(states_scr[pl.ds(date * paths, paths), :], load_scr[...])
            hi, lo = split2(jnp.maximum(pay, 0.0))
            wide = 2 * factors
            both = mm(wide_scr[date], hi)
            moment = both[:wide] + both[wide:] + mm(wide_scr[date, :wide], lo)
            hi, lo = split2(moment * scaled)
            his.append(hi)
            los.append(lo)
        stacked = jnp.concatenate(his + los, axis=0)
        set_ids = set_ref[:, cols]
        to_rank = (set_ids >> rows_bits) & (ranks - 1)
        to_group = set_ids >> (rows_bits + log2(ranks))
        places = ((to_rank * groups + to_group) << rows_bits) + (set_ids & ((1 << rows_bits) - 1))
        one_hot = jnp.where(
            lax.broadcasted_iota(jnp.int32, (sets, TILE), 0) == places, 1.0, 0.0
        ).astype(BF16)
        summed = mm(one_hot, stacked, NT)
        half = summed.shape[1] // 2
        net_ref[...] += summed[:, :half] + summed[:, half:]
        return carry

    lax.fori_loop(0, slots // TILE, step, 0)


def add_kernel(parts_ref, total_ref):
    total = parts_ref[0]
    for part in range(1, parts_ref.shape[0]):
        total = total + parts_ref[part]
    total_ref[...] = total


def states_of(ref, factors, dates):
    state = ref[:factors, :]
    yield state
    for date in range(1, dates):
        state = 0.8 * state + 0.6 * ref[date * factors : (date + 1) * factors, :]
        yield state


def weights_of(ref, factors, dates):
    return ref[dates * factors : dates * factors + 1, :]


def inverse_kernel(factors, dates, blocks_ref, inverse_ref):
    wide = 2 * factors
    sub = lax.broadcasted_iota(jnp.int32, (wide, wide), 0)
    lane = lax.broadcasted_iota(jnp.int32, (wide, wide), 1)
    grams = [jnp.zeros((wide, wide), F32) for _ in range(dates)]
    for block in range(blocks_ref.shape[0]):
        weight_row = weights_of(blocks_ref.at[block], factors, dates)
        for date, state in enumerate(states_of(blocks_ref.at[block], factors, dates)):
            basis = basis_rows(state)
            grams[date] = grams[date] + mm_full(basis * weight_row, basis, NT)
    work = list(grams)
    for k in range(wide):
        for date in range(dates):
            mat = work[date]
            row = mat[k : k + 1, :]
            col = mat[:, k : k + 1]
            pivot = 1.0 / mat[k : k + 1, k : k + 1]
            row = jnp.where(lane[:1] == k, 1.0, row) * pivot
            work[date] = jnp.where(sub == k, row, jnp.where(lane == k, 0.0, mat) - col * row)
    eye = jnp.where(sub == lane, 1.0, 0.0)
    for date in range(dates):
        approx = work[date]
        inverse_ref[date] = approx + mm_full(approx, eye - mm_full(grams[date], approx))


def exposure_kernel(
    factors, dates, totals_ref, own_ref, blocks_ref, inverse_ref, limits_ref, exposure_ref, expected_ref
):
    wide = 2 * factors
    paths = own_ref.shape[1]
    limits = 0.25 * limits_ref[...].astype(F32)
    coeffs = []
    for date in range(dates):
        hi, lo = split2(mm_full(totals_ref[:, date * wide : (date + 1) * wide], inverse_ref[date]))
        coeffs.append(jnp.concatenate([hi, hi, lo], axis=1))

    def exposures(block_ref):
        for date, state in enumerate(states_of(block_ref, factors, dates)):
            hi, lo = split2(basis_rows(state))
            value = mm(coeffs[date], jnp.concatenate([hi, lo, hi], axis=0))
            yield jnp.maximum(value - limits, 0.0)

    for date, value in enumerate(exposures(own_ref)):
        exposure_ref[date] = value
    sums = [jnp.zeros((limits.shape[0], 128), F32) for _ in range(dates)]
    total = jnp.zeros((1, 1), F32)
    for block in range(blocks_ref.shape[0]):
        weight_row = weights_of(blocks_ref.at[block], factors, dates)
        total = total + jnp.sum(weight_row, keepdims=True)
        for date, value in enumerate(exposures(blocks_ref.at[block])):
            product = value * weight_row
            for c in range(paths // 128):
                sums[date] = sums[date] + product[:, c * 128 : (c + 1) * 128]
    for date in range(dates):
        expected_ref[date : date + 1, :] = jnp.sum(sums[date].T, axis=0, keepdims=True) / total


def log2(n):
    assert n & (n - 1) == 0
    return n.bit_length() - 1


def scatter_sum(parts, axis):
    parts = lax.all_to_all(parts, axis, 0, 0)
    vmem = pl.BlockSpec(memory_space=pltpu.VMEM)
    return pl.pallas_call(
        add_kernel,
        out_shape=jax.ShapeDtypeStruct(parts.shape[1:], F32),
        in_specs=[vmem],
        out_specs=vmem,
        compiler_params=pltpu.CompilerParams(vmem_limit_bytes=4 * MIB),
        name="add_parts",
    )(parts)


def gather(x, axis):
    return lax.all_to_all(jnp.broadcast_to(x, (lax.axis_size(axis), *x.shape)), axis, 0, 0)


def body(
    start_state, shocks, loadings, strikes, notionals, trade_set, live_counts, weights, thresholds
):
    paths, factors = start_state.shape
    dates = shocks.shape[0]
    slots = loadings.shape[1]
    owned = thresholds.shape[0]
    groups = lax.axis_size("trade")
    ranks = lax.axis_size("path")
    sets = owned * groups
    wide = 2 * factors

    start_t = start_state.T
    shocks_t = jnp.swapaxes(shocks, 1, 2)
    weights_row = weights[None, :]
    vmem = pl.BlockSpec(memory_space=pltpu.VMEM)
    smem = pl.BlockSpec(memory_space=pltpu.SMEM)

    packed = jnp.concatenate(
        [start_t]
        + [shocks_t[date] for date in range(dates - 1)]
        + [jnp.broadcast_to(weights_row.astype(F32), (8, paths))],
        axis=0,
    )
    blocks = gather(packed, "path")

    net = pl.pallas_call(
        functools.partial(moment_kernel, groups=groups, ranks=ranks),
        out_shape=jax.ShapeDtypeStruct((sets, dates * wide), F32),
        in_specs=[smem] + [vmem] * 7,
        out_specs=vmem,
        scratch_shapes=[
            pltpu.VMEM((dates * paths, DEPTH), BF16),
            pltpu.VMEM((dates, 2 * wide, paths), BF16),
            pltpu.VMEM((DEPTH, TILE), BF16),
        ],
        compiler_params=pltpu.CompilerParams(vmem_limit_bytes=58 * MIB),
        cost_estimate=pl.CostEstimate(flops=16 * 10**9, bytes_accessed=4 * 10**6, transcendentals=0),
        name="net_moments",
    )(
        live_counts, start_t, shocks_t, weights_row, loadings, strikes[None, :], notionals[None, :],
        trade_set[None, :],
    )
    by_group = scatter_sum(net.reshape(ranks, sets // ranks, dates * wide), "path")
    share = scatter_sum(by_group.reshape(groups, owned // ranks, dates * wide), "trade")
    totals = gather(share, "path").reshape(owned, dates * wide)

    inverse = pl.pallas_call(
        functools.partial(inverse_kernel, factors, dates),
        out_shape=jax.ShapeDtypeStruct((dates, wide, wide), F32),
        in_specs=[vmem],
        out_specs=vmem,
        compiler_params=pltpu.CompilerParams(vmem_limit_bytes=8 * MIB),
        cost_estimate=pl.CostEstimate(flops=8 * 10**9, bytes_accessed=10**6, transcendentals=0),
        name="gram_inverse",
    )(blocks)

    exposure, expected = pl.pallas_call(
        functools.partial(exposure_kernel, factors, dates),
        out_shape=(
            jax.ShapeDtypeStruct((dates, owned, paths), F32),
            jax.ShapeDtypeStruct((dates, owned), F32),
        ),
        in_specs=[vmem] * 5,
        out_specs=(vmem, vmem),
        compiler_params=pltpu.CompilerParams(vmem_limit_bytes=16 * MIB),
        cost_estimate=pl.CostEstimate(flops=2 * 10**9, bytes_accessed=2 * 10**6, transcendentals=0),
        name="set_exposure",
    )(totals, packed, blocks, inverse, thresholds[:, None])
    return (exposure, expected)


def solution(mesh):
    placed = (
        P("path", None),
        P(None, "path", None),
        P(None, "trade"),
        P("trade"),
        P("trade"),
        P("trade"),
        P(),
        P("path"),
        P("trade"),
    )
    return jax.shard_map(
        body,
        mesh=mesh,
        in_specs=placed,
        out_specs=(P(None, "trade", "path"), P(None, "trade")),
        check_vma=False,
    )
```

```python
import functools

import jax
import jax.numpy as jnp
from jax import lax
from jax.experimental import pallas as pl
from jax.experimental.pallas import tpu as pltpu
from jax.sharding import PartitionSpec as P

HIGHEST_PREC = lax.Precision.HIGHEST
ROOT_HALF = 0.7071067811865476
F32 = jnp.float32
BF16 = jnp.bfloat16
TILE = 512
DEPTH = 256
PAD = 8
MIB = 1024 * 1024
NN = (((1,), (0,)), ((), ()))
NT = (((1,), (1,)), ((), ()))
VMEM = pl.BlockSpec(memory_space=pltpu.VMEM)
SMEM = pl.BlockSpec(memory_space=pltpu.SMEM)


def mm(a, b, dims=NN):
    return lax.dot_general(a, b, dims, preferred_element_type=F32)


def mm_full(a, b, dims=NN):
    return lax.dot_general(a, b, dims, preferred_element_type=F32, precision=HIGHEST_PREC)


def split2(x):
    hi = x.astype(BF16)
    return hi, (x - hi.astype(F32)).astype(BF16)


def split3(x):
    hi = x.astype(BF16)
    rest = x - hi.astype(F32)
    mid = rest.astype(BF16)
    return hi, mid, (rest - mid.astype(F32)).astype(BF16)


def log2(n):
    assert n & (n - 1) == 0
    return n.bit_length() - 1


def basis_rows(state):
    return jnp.concatenate([state, (state * state - 1.0) * ROOT_HALF], axis=0)


def pick(core, first, second):
    return jnp.where(core == 0, first, second)


def states_of(ref, factors):
    state = ref[:factors, :]
    return state, 0.8 * state + 0.6 * ref[factors : 2 * factors, :]


def weights_of(ref, factors):
    return ref[2 * factors : 2 * factors + 1, :]


def prepare(block_ref, states_scr, wide_scr, load_scr, factors):
    core = lax.axis_index("path") & 1
    first, second = states_of(block_ref, factors)
    third = 0.8 * second + 0.6 * block_ref[2 * factors + PAD :, :]
    hi, lo = split2(basis_rows(pick(core, first, second)) * weights_of(block_ref, factors))
    wide_scr[...] = jnp.concatenate([hi, lo], axis=0)
    hi, mid, low = split3(pick(core, second, third))
    hi, mid, low = hi.astype(F32), mid.astype(F32), low.astype(F32)
    paths = block_ref.shape[1]
    ones = jnp.where(lax.broadcasted_iota(jnp.int32, (DEPTH - 6 * factors, paths), 0) < 3, 1.0, 0.0)
    states_scr[...] = jnp.concatenate([hi, hi, mid, mid, hi, low, ones], axis=0).T.astype(BF16)
    load_scr[...] = jnp.zeros_like(load_scr)


def path_moments(cols, load_ref, strike_ref, states_scr, wide_scr, load_scr, slot):
    factors = load_ref.shape[0]
    wide = 2 * factors
    hi, mid, low = split3(load_ref[:, cols])
    for part, piece in enumerate((hi, mid, hi, mid, low, hi)):
        load_scr[slot, pl.ds(part * factors, factors), :] = piece
    s_hi, s_mid, s_low = split3(-strike_ref[:, cols])
    rows = lax.broadcasted_iota(jnp.int32, (16, TILE), 0)
    strike_rows = jnp.where(rows == 1, s_mid.astype(F32), jnp.where(rows == 2, s_low.astype(F32), 0.0))
    strike_rows = jnp.where(rows == 0, s_hi.astype(F32), strike_rows)
    load_scr[slot, pl.ds(6 * factors, 16), :] = strike_rows.astype(BF16)
    hi, lo = split2(jnp.maximum(mm(states_scr[...], load_scr[slot]), 0.0))
    both = mm(wide_scr[...], hi)
    return both[:wide] + both[wide:] + mm(wide_scr[:wide], lo)


def tile_at(index):
    return pl.ds(pl.multiple_of(index * TILE, TILE), TILE)


def first_kernel(block_ref, load_ref, strike_ref, moment_ref, states_scr, wide_scr, load_scr):
    prepare(block_ref, states_scr, wide_scr, load_scr, load_ref.shape[0])

    def step(pair, carry):
        for slot in range(2):
            cols = tile_at(2 * pair + slot)
            moment_ref[:, cols] = path_moments(cols, load_ref, strike_ref, states_scr, wide_scr, load_scr, slot)
        return carry

    lax.fori_loop(0, load_ref.shape[1] // (2 * TILE), step, 0)


def second_kernel(groups, counts_ref, block_ref, moment_ref, load_ref, strike_ref, notional_ref, set_ref, *refs):
    outs, (net_scr, states_scr, wide_scr, load_scr) = refs[:groups], refs[groups:]
    group = lax.axis_index("trade")
    filled = counts_ref[group]
    sets = net_scr.shape[0]
    owned = sets // groups
    bits = log2(owned)
    prepare(block_ref, states_scr, wide_scr, load_scr, load_ref.shape[0])
    net_scr[...] = jnp.zeros_like(net_scr)

    def step(pair, carry):
        for slot in range(2):
            index = 2 * pair + slot
            cols = tile_at(index)
            moment = moment_ref[:, cols]
            moment = moment + path_moments(cols, load_ref, strike_ref, states_scr, wide_scr, load_scr, slot)
            slot_ids = index * TILE + lax.broadcasted_iota(jnp.int32, (1, TILE), 1)
            hi, lo = split2(moment * jnp.where(slot_ids < filled, notional_ref[:, cols], 0.0))
            places = set_ref[:, cols] ^ (group << bits)
            one_hot = lax.broadcasted_iota(jnp.int16, (sets, TILE), 0) == places.astype(jnp.int16)
            one_hot = jnp.where(one_hot, jnp.ones((), BF16), jnp.zeros((), BF16))
            net_scr[...] += mm(one_hot, jnp.concatenate([hi, lo], axis=0), NT)
        return carry

    lax.fori_loop(0, load_ref.shape[1] // (2 * TILE), step, 0)
    wide = net_scr.shape[1] // 2
    half = owned // 2
    for away, out in enumerate(outs):
        net = net_scr[away * owned : (away + 1) * owned, :]
        net = net[:, :wide] + net[:, wide:]
        out[...] = jnp.concatenate([net[:half], net[half:]], axis=1)


def inverse_kernel(factors, *refs):
    blocks, inverse_ref = refs[:-1], refs[-1]
    core = lax.axis_index("path") & 1
    wide = 2 * factors
    sub = lax.broadcasted_iota(jnp.int32, (wide, wide), 0)
    lane = lax.broadcasted_iota(jnp.int32, (wide, wide), 1)
    gram = jnp.zeros((wide, wide), F32)
    for block in path_blocks(blocks):
        basis = basis_rows(pick(core, *states_of(block, factors)))
        gram = gram + mm_full(basis * weights_of(block, factors), basis, NT)
    mat = gram
    for k in range(wide):
        row = mat[k : k + 1, :]
        col = mat[:, k : k + 1]
        pivot = 1.0 / mat[k : k + 1, k : k + 1]
        row = jnp.where(lane[:1] == k, 1.0, row) * pivot
        mat = jnp.where(sub == k, row, jnp.where(lane == k, 0.0, mat) - col * row)
    eye = jnp.where(sub == lane, 1.0, 0.0)
    mat = mat + mm_full(mat, eye - mm_full(gram, mat))
    zero = jnp.zeros_like(mat)
    upper = jnp.concatenate([mat, zero], axis=1)
    inverse_ref[...] = jnp.concatenate([upper, jnp.concatenate([zero, mat], axis=1)], axis=0)


def path_blocks(refs):
    for ref in refs:
        if len(ref.shape) == 2:
            yield ref
        else:
            for index in range(ref.shape[0]):
                yield ref.at[index]


def sum_kernel(*refs):
    total = refs[0][...]
    for ref in refs[1:-1]:
        total = total + ref[...]
    refs[-1][...] = total


def coeff_kernel(*refs):
    total = refs[0][...]
    for ref in refs[1:-2]:
        total = total + ref[...]
    refs[-1][...] = mm_full(total, refs[-2][...])


def exposure_kernel(factors, mine_ref, other_ref, limits_ref, *refs):
    blocks, (exposure_ref, expected_ref) = refs[:-2], refs[-2:]
    core = lax.axis_index("path") & 1
    wide = 2 * factors
    paths = blocks[0].shape[1]
    limits = 0.25 * limits_ref[...].astype(F32)
    mine, other = mine_ref[...], other_ref[...]
    coeffs = []
    for packed in (pick(core, mine, other), pick(core, other, mine)):
        hi, lo = split2(jnp.concatenate([packed[:, :wide], packed[:, wide:]], axis=0))
        coeffs.append(jnp.concatenate([hi, hi, lo], axis=1))
    sums = [jnp.zeros((limits.shape[0], 128), F32) for _ in coeffs]
    total = jnp.zeros((1, 1), F32)
    for number, block in enumerate(path_blocks(blocks)):
        weight_row = weights_of(block, factors)
        total = total + jnp.sum(weight_row, keepdims=True)
        for date, state in enumerate(states_of(block, factors)):
            hi, lo = split2(basis_rows(state))
            value = jnp.maximum(mm(coeffs[date], jnp.concatenate([hi, lo, hi], axis=0)) - limits, 0.0)
            if number == 0:
                exposure_ref[date] = value
            product = value * weight_row
            for c in range(paths // 128):
                sums[date] = sums[date] + product[:, c * 128 : (c + 1) * 128]
    for date, partial in enumerate(sums):
        expected_ref[date : date + 1, :] = jnp.sum(partial.T, axis=0, keepdims=True) / total


def swap(x, axis, away):
    return lax.ppermute(x, axis, [(i, i ^ away) for i in range(lax.axis_size(axis))])


def run(kernel, name, out, specs, args, mib, scratch=(), gflops=0.0):
    return pl.pallas_call(
        kernel,
        out_shape=out,
        in_specs=specs,
        out_specs=jax.tree.map(lambda _: VMEM, out),
        scratch_shapes=list(scratch),
        compiler_params=pltpu.CompilerParams(vmem_limit_bytes=mib * MIB),
        cost_estimate=pl.CostEstimate(flops=int(gflops * 1e9), bytes_accessed=10**5, transcendentals=0),
        name=name,
    )(*args)


def body(
    start_state, shocks, loadings, strikes, notionals, trade_set, live_counts, weights, thresholds
):
    paths, factors = start_state.shape
    dates = shocks.shape[0]
    slots = loadings.shape[1]
    owned = thresholds.shape[0]
    groups = lax.axis_size("trade")
    ranks = lax.axis_size("path")
    sets = owned * groups
    wide = 2 * factors
    assert dates == 2

    shocks_t = jnp.swapaxes(shocks, 1, 2)
    weight_rows = jnp.broadcast_to(weights.astype(F32), (PAD, paths))
    short = jnp.concatenate([start_state.T, shocks_t[0], weight_rows], axis=0)
    whole = jnp.concatenate([start_state.T, shocks_t[0], weight_rows, shocks_t[1]], axis=0)
    other = swap(whole, "path", 1)
    across = jnp.stack([swap(short, "path", 2 * away) for away in range(1, ranks // 2)])

    shape = jax.ShapeDtypeStruct
    scratch = [
        pltpu.VMEM((paths, DEPTH), BF16),
        pltpu.VMEM((2 * wide, paths), BF16),
        pltpu.VMEM((2, DEPTH, TILE), BF16),
    ]
    strike_row, notional_row, set_row = strikes[None, :], notionals[None, :], trade_set[None, :]
    moment = run(
        first_kernel, "own_path_moments", shape((wide, slots), F32), [VMEM] * 3,
        (whole, loadings, strike_row), 48, scratch, 8.0,
    )
    other, across = lax.optimization_barrier((other, across))
    others = swap(across, "path", 1)
    nets = run(
        functools.partial(second_kernel, groups), "other_path_moments",
        [shape((owned // 2, 2 * wide), F32)] * groups, [SMEM] + [VMEM] * 6,
        (live_counts, other, moment, loadings, strike_row, notional_row, set_row), 48,
        [pltpu.VMEM((sets, 2 * wide), F32)] + scratch, 12.0,
    )
    got = [swap(nets[away], "trade", away) for away in range(1, groups)]
    blocks = (whole, other, across, others)
    inverse = run(
        functools.partial(inverse_kernel, factors), "gram_inverse", shape((2 * wide, 2 * wide), F32),
        [VMEM] * 4, blocks, 8, (), 6.0,
    )
    part = run(
        sum_kernel, "group_sum", shape((owned // 2, 2 * wide), F32), [VMEM] * groups, [nets[0]] + got, 4
    )
    got = [swap(part, "path", 2 * away) for away in range(1, ranks // 2)]
    mine = run(
        coeff_kernel, "set_coeffs", shape((owned // 2, 2 * wide), F32), [VMEM] * (ranks // 2 + 1),
        [part] + got + [inverse], 4,
    )
    partner = swap(mine, "path", 1)
    exposure, expected = run(
        functools.partial(exposure_kernel, factors), "set_exposure",
        (shape((dates, owned, paths), F32), shape((dates, owned), F32)), [VMEM] * 7,
        (mine, partner, thresholds[:, None], *blocks), 16, (), 2.0,
    )
    return (exposure, expected)


def solution(mesh):
    placed = (
        P("path", None),
        P(None, "path", None),
        P(None, "trade"),
        P("trade"),
        P("trade"),
        P("trade"),
        P(),
        P("path"),
        P("trade"),
    )
    return jax.shard_map(
        body,
        mesh=mesh,
        in_specs=placed,
        out_specs=(P(None, "trade", "path"), P(None, "trade")),
        check_vma=False,
    )
```

```python
import functools

import jax
import jax.numpy as jnp
from jax import lax
from jax.experimental import pallas as pl
from jax.experimental.pallas import tpu as pltpu
from jax.sharding import PartitionSpec as P

HIGHEST_PREC = lax.Precision.HIGHEST
ROOT_HALF = 0.7071067811865476
F32 = jnp.float32
BF16 = jnp.bfloat16
TILE = 512
DEPTH = 256
PAD = 8
MIB = 1024 * 1024
NN = (((1,), (0,)), ((), ()))
NT = (((1,), (1,)), ((), ()))
VMEM = pl.BlockSpec(memory_space=pltpu.VMEM)
SMEM = pl.BlockSpec(memory_space=pltpu.SMEM)
ANY = pl.BlockSpec(memory_space=pl.ANY)


def mm(a, b, dims=NN):
    return lax.dot_general(a, b, dims, preferred_element_type=F32)


def mm_full(a, b, dims=NN):
    return lax.dot_general(a, b, dims, preferred_element_type=F32, precision=HIGHEST_PREC)


def split2(x):
    hi = x.astype(BF16)
    return hi, (x - hi.astype(F32)).astype(BF16)


def split3(x):
    hi = x.astype(BF16)
    rest = x - hi.astype(F32)
    mid = rest.astype(BF16)
    return hi, mid, (rest - mid.astype(F32)).astype(BF16)


def log2(n):
    assert n & (n - 1) == 0
    return n.bit_length() - 1


def basis_rows(state):
    return jnp.concatenate([state, (state * state - 1.0) * ROOT_HALF], axis=0)


def pick(core, first, second):
    return jnp.where(core == 0, first, second)


def states_of(ref, factors):
    state = ref[:factors, :]
    return state, 0.8 * state + 0.6 * ref[factors : 2 * factors, :]


def weights_of(ref, factors):
    return ref[2 * factors : 2 * factors + 1, :]


def pack_kernel(start_ref, shocks_ref, weights_ref, short_ref, whole_ref):
    factors = start_ref.shape[0]
    for ref in (short_ref, whole_ref):
        ref[:factors, :] = start_ref[...]
        ref[factors : 2 * factors, :] = shocks_ref[0]
        ref[2 * factors : 2 * factors + PAD, :] = jnp.broadcast_to(weights_ref[...].astype(F32), (PAD, ref.shape[1]))
    whole_ref[2 * factors + PAD :, :] = shocks_ref[1]


def prepare(blocks, states_scr, wide_scr, load_scr, factors):
    core = lax.axis_index("path") & 1
    load_scr[...] = jnp.zeros_like(load_scr)
    for number, block_ref in enumerate(blocks):
        paths = block_ref.shape[1]
        mine = pl.ds(number * paths, paths)
        first, second = states_of(block_ref, factors)
        third = 0.8 * second + 0.6 * block_ref[2 * factors + PAD :, :]
        hi, lo = split2(basis_rows(pick(core, first, second)) * weights_of(block_ref, factors))
        wide_scr[:, mine] = jnp.concatenate([hi, lo], axis=0)
        hi, mid, low = split3(pick(core, second, third))
        hi, mid, low = hi.astype(F32), mid.astype(F32), low.astype(F32)
        ones = jnp.where(lax.broadcasted_iota(jnp.int32, (DEPTH - 6 * factors, paths), 0) < 3, 1.0, 0.0)
        stacked = jnp.concatenate([hi, hi, mid, mid, hi, low, ones], axis=0)
        states_scr[mine, :] = stacked.T.astype(BF16)


def path_moments(cols, load_ref, strike_ref, states_scr, wide_scr, load_scr, slot):
    factors = load_ref.shape[0]
    wide = 2 * factors
    hi, mid, low = split3(load_ref[:, cols])
    for part, piece in enumerate((hi, mid, hi, mid, low, hi)):
        load_scr[slot, pl.ds(part * factors, factors), :] = piece
    s_hi, s_mid, s_low = split3(-strike_ref[:, cols])
    rows = lax.broadcasted_iota(jnp.int32, (16, TILE), 0)
    strike_rows = jnp.where(rows == 1, s_mid.astype(F32), jnp.where(rows == 2, s_low.astype(F32), 0.0))
    strike_rows = jnp.where(rows == 0, s_hi.astype(F32), strike_rows)
    load_scr[slot, pl.ds(6 * factors, 16), :] = strike_rows.astype(BF16)
    hi, lo = split2(jnp.maximum(mm(states_scr[...], load_scr[slot]), 0.0))
    both = mm(wide_scr[...], hi)
    return both[:wide] + both[wide:] + mm(wide_scr[:wide], lo)


def tile_at(index):
    return pl.ds(pl.multiple_of(index * TILE, TILE), TILE)


def copies(sources, targets, sems):
    return [pltpu.make_async_copy(src, dst, sems.at[i]) for i, (src, dst) in enumerate(zip(sources, targets))]


def moment_kernel(
    groups, counts_ref, own_ref, other_ref, load_hbm, strike_hbm, notional_hbm, set_hbm, *refs
):
    outs = refs[:groups]
    load_ref, strike_ref, notional_ref, set_ref, sems, net_scr, *scratch = refs[groups:]
    moves = copies(
        (load_hbm, strike_hbm, notional_hbm, set_hbm), (load_ref, strike_ref, notional_ref, set_ref), sems
    )
    for move in moves:
        move.start()
    group = lax.axis_index("trade")
    filled = counts_ref[group]
    owned = net_scr.shape[0]
    bits = log2(owned)
    rows = 16
    prepare((own_ref, other_ref), *scratch, load_ref.shape[0])
    net_scr[...] = jnp.zeros_like(net_scr)
    for move in moves:
        move.wait()

    def step(pair, carry):
        for slot in range(2):
            index = 2 * pair + slot
            cols = tile_at(index)
            moment = path_moments(cols, load_ref, strike_ref, *scratch, slot)
            slot_ids = index * TILE + lax.broadcasted_iota(jnp.int32, (1, TILE), 1)
            hi, lo = split2(moment * jnp.where(slot_ids < filled, notional_ref[:, cols], 0.0))
            both = jnp.concatenate([hi, lo], axis=0)
            both = both.reshape(both.shape[0] // rows, rows, TILE)
            sets = set_ref[:, cols]
            to_group = jnp.broadcast_to((sets >> bits) ^ group, (rows, TILE))
            parts = []
            for away in range(groups):
                mask = jnp.where(to_group == away, 1.0, 0.0).astype(BF16)
                parts.append((both * mask[None]).reshape(-1, TILE))
            one_hot = lax.broadcasted_iota(jnp.int32, (owned, TILE), 0) == (sets & (owned - 1))
            one_hot = jnp.where(one_hot, 1.0, 0.0).astype(BF16)
            net_scr[...] += mm(one_hot, jnp.concatenate(parts, axis=0), NT)
        return carry

    lax.fori_loop(0, load_ref.shape[1] // (2 * TILE), step, 0)
    wide = net_scr.shape[1] // (2 * groups)
    half = owned // 2
    for away, out in enumerate(outs):
        net = net_scr[:, 2 * wide * away : 2 * wide * (away + 1)]
        net = net[:, :wide] + net[:, wide:]
        out[...] = jnp.concatenate([net[:half], net[half:]], axis=1)


def inverse_kernel(factors, *refs):
    blocks, inverse_ref = refs[:-1], refs[-1]
    core = lax.axis_index("path") & 1
    wide = 2 * factors
    sub = lax.broadcasted_iota(jnp.int32, (wide, wide), 0)
    lane = lax.broadcasted_iota(jnp.int32, (wide, wide), 1)
    gram = jnp.zeros((wide, wide), F32)
    for block in path_blocks(blocks):
        basis = basis_rows(pick(core, *states_of(block, factors)))
        gram = gram + mm_full(basis * weights_of(block, factors), basis, NT)
    mat = gram
    for k in range(wide):
        row = mat[k : k + 1, :]
        col = mat[:, k : k + 1]
        pivot = 1.0 / mat[k : k + 1, k : k + 1]
        row = jnp.where(lane[:1] == k, 1.0, row) * pivot
        mat = jnp.where(sub == k, row, jnp.where(lane == k, 0.0, mat) - col * row)
    eye = jnp.where(sub == lane, 1.0, 0.0)
    mat = mat + mm_full(mat, eye - mm_full(gram, mat))
    zero = jnp.zeros_like(mat)
    upper = jnp.concatenate([mat, zero], axis=1)
    inverse_ref[...] = jnp.concatenate([upper, jnp.concatenate([zero, mat], axis=1)], axis=0)


def path_blocks(refs):
    for ref in refs:
        if len(ref.shape) == 2:
            yield ref
        else:
            for index in range(ref.shape[0]):
                yield ref.at[index]


def sum_kernel(*refs):
    total = refs[0][...]
    for ref in refs[1:-1]:
        total = total + ref[...]
    refs[-1][...] = total


def coeff_kernel(*refs):
    total = refs[0][...]
    for ref in refs[1:-2]:
        total = total + ref[...]
    refs[-1][...] = mm_full(total, refs[-2][...])


def exposure_kernel(factors, mine_ref, other_ref, limits_ref, *refs):
    blocks, (exposure_ref, expected_ref) = refs[:-2], refs[-2:]
    core = lax.axis_index("path") & 1
    wide = 2 * factors
    paths = blocks[0].shape[1]
    limits = 0.25 * limits_ref[...].astype(F32)
    mine, other = mine_ref[...], other_ref[...]
    coeffs = []
    for packed in (pick(core, mine, other), pick(core, other, mine)):
        hi, lo = split2(jnp.concatenate([packed[:, :wide], packed[:, wide:]], axis=0))
        coeffs.append(jnp.concatenate([hi, hi, lo], axis=1))
    sums = [jnp.zeros((limits.shape[0], 128), F32) for _ in coeffs]
    total = jnp.zeros((1, 1), F32)
    for number, block in enumerate(path_blocks(blocks)):
        weight_row = weights_of(block, factors)
        total = total + jnp.sum(weight_row, keepdims=True)
        for date, state in enumerate(states_of(block, factors)):
            hi, lo = split2(basis_rows(state))
            value = jnp.maximum(mm(coeffs[date], jnp.concatenate([hi, lo, hi], axis=0)) - limits, 0.0)
            if number == 0:
                exposure_ref[date] = value
            product = value * weight_row
            for c in range(paths // 128):
                sums[date] = sums[date] + product[:, c * 128 : (c + 1) * 128]
    for date, partial in enumerate(sums):
        expected_ref[date : date + 1, :] = jnp.sum(partial.T, axis=0, keepdims=True) / total


def swap(x, axis, away):
    return lax.ppermute(x, axis, [(i, i ^ away) for i in range(lax.axis_size(axis))])


def run(kernel, name, out, specs, args, mib, scratch=(), gflops=0.0):
    return pl.pallas_call(
        kernel,
        out_shape=out,
        in_specs=specs,
        out_specs=jax.tree.map(lambda _: VMEM, out),
        scratch_shapes=list(scratch),
        compiler_params=pltpu.CompilerParams(vmem_limit_bytes=mib * MIB),
        cost_estimate=pl.CostEstimate(flops=int(gflops * 1e9), bytes_accessed=10**5, transcendentals=0),
        name=name,
    )(*args)


def body(
    start_state, shocks, loadings, strikes, notionals, trade_set, live_counts, weights, thresholds
):
    paths, factors = start_state.shape
    dates = shocks.shape[0]
    slots = loadings.shape[1]
    owned = thresholds.shape[0]
    groups = lax.axis_size("trade")
    ranks = lax.axis_size("path")
    wide = 2 * factors
    assert dates == 2

    shape = jax.ShapeDtypeStruct
    short, whole = run(
        pack_kernel, "pack_states",
        [shape(((dates - 1) * factors + factors + PAD, paths), F32), shape(((dates + 1) * factors + PAD, paths), F32)],
        [VMEM] * 3, (start_state.T, jnp.swapaxes(shocks, 1, 2), weights[None, :]), 58,
    )
    other = swap(whole, "path", 1)
    across = [swap(short, "path", 2 * away) for away in range(1, ranks // 2)]

    strike_row, notional_row, set_row = strikes[None, :], notionals[None, :], trade_set[None, :]
    nets = run(
        functools.partial(moment_kernel, groups), "net_moments",
        [shape((owned // 2, 2 * wide), F32)] * groups, [SMEM, VMEM, VMEM] + [ANY] * 4,
        (live_counts, whole, other, loadings, strike_row, notional_row, set_row), 56,
        [
            pltpu.VMEM((factors, slots), F32),
            pltpu.VMEM((1, slots), F32),
            pltpu.VMEM((1, slots), F32),
            pltpu.VMEM((1, slots), jnp.int32),
            pltpu.SemaphoreType.DMA((4,)),
            pltpu.VMEM((owned, 2 * wide * groups), F32),
            pltpu.VMEM((2 * paths, DEPTH), BF16),
            pltpu.VMEM((2 * wide, 2 * paths), BF16),
            pltpu.VMEM((2, DEPTH, TILE), BF16),
        ],
        20.0,
    )
    *across, net = lax.optimization_barrier((*across, nets[0]))
    others = swap(jnp.stack(across), "path", 1)
    got = [swap(nets[away], "trade", away) for away in range(1, groups)]
    blocks = (whole, other, *across, others)
    inverse = run(
        functools.partial(inverse_kernel, factors), "gram_inverse", shape((2 * wide, 2 * wide), F32),
        [VMEM] * len(blocks), blocks, 8, (), 6.0,
    )
    inverse, net = lax.optimization_barrier((inverse, net))
    part = run(
        sum_kernel, "group_sum", shape((owned // 2, 2 * wide), F32), [VMEM] * groups, [net] + got, 4
    )
    got = [swap(part, "path", 2 * away) for away in range(1, ranks // 2)]
    mine = run(
        coeff_kernel, "set_coeffs", shape((owned // 2, 2 * wide), F32), [VMEM] * (ranks // 2 + 1),
        [part] + got + [inverse], 4,
    )
    partner = swap(mine, "path", 1)
    exposure, expected = run(
        functools.partial(exposure_kernel, factors), "set_exposure",
        (shape((dates, owned, paths), F32), shape((dates, owned), F32)), [VMEM] * (3 + len(blocks)),
        (mine, partner, thresholds[:, None], *blocks), 16, (), 2.0,
    )
    return (exposure, expected)


def solution(mesh):
    placed = (
        P("path", None),
        P(None, "path", None),
        P(None, "trade"),
        P("trade"),
        P("trade"),
        P("trade"),
        P(),
        P("path"),
        P("trade"),
    )
    return jax.shard_map(
        body,
        mesh=mesh,
        in_specs=placed,
        out_specs=(P(None, "trade", "path"), P(None, "trade")),
        check_vma=False,
    )
```

```python
import functools

import jax
import jax.numpy as jnp
from jax import lax
from jax.experimental import pallas as pl
from jax.experimental.pallas import tpu as pltpu
from jax.sharding import PartitionSpec as P

HIGHEST_PREC = lax.Precision.HIGHEST
ROOT_HALF = 0.7071067811865476
F32 = jnp.float32
BF16 = jnp.bfloat16
TILE = 512
CHUNK = 512
SLOTS = 2
DEPTH = 256
PAD = 8
MIB = 1024 * 1024
NN = (((1,), (0,)), ((), ()))
NT = (((1,), (1,)), ((), ()))
VMEM = pl.BlockSpec(memory_space=pltpu.VMEM)
SMEM = pl.BlockSpec(memory_space=pltpu.SMEM)
ANY = pl.BlockSpec(memory_space=pl.ANY)


def mm(a, b, dims=NN):
    return lax.dot_general(a, b, dims, preferred_element_type=F32)


def mm_full(a, b, dims=NN):
    return lax.dot_general(a, b, dims, preferred_element_type=F32, precision=HIGHEST_PREC)


def split2(x):
    hi = x.astype(BF16)
    return hi, (x - hi.astype(F32)).astype(BF16)


def split3(x):
    hi = x.astype(BF16)
    rest = x - hi.astype(F32)
    mid = rest.astype(BF16)
    return hi, mid, (rest - mid.astype(F32)).astype(BF16)


def log2(n):
    assert n & (n - 1) == 0
    return n.bit_length() - 1


def basis_rows(state):
    return jnp.concatenate([state, (state * state - 1.0) * ROOT_HALF], axis=0)


def pick(core, first, second):
    return jnp.where(core == 0, first, second)


def states_of(ref, factors):
    state = ref[:factors, :]
    return state, 0.8 * state + 0.6 * ref[factors : 2 * factors, :]


def weights_of(ref, factors):
    return ref[2 * factors : 2 * factors + 1, :]


def pack_kernel(start_ref, shocks_ref, weights_ref, short_ref, whole_ref):
    factors = start_ref.shape[0]
    for ref in (short_ref, whole_ref):
        ref[:factors, :] = start_ref[...]
        ref[factors : 2 * factors, :] = shocks_ref[0]
        ref[2 * factors : 2 * factors + PAD, :] = jnp.broadcast_to(weights_ref[...].astype(F32), (PAD, ref.shape[1]))
    whole_ref[2 * factors + PAD :, :] = shocks_ref[1]


def prepare(blocks, states_scr, wide_scr, load_scr, factors):
    core = lax.axis_index("path") & 1
    load_scr[...] = jnp.zeros_like(load_scr)
    for number, block_ref in enumerate(blocks):
        paths = block_ref.shape[1]
        mine = pl.ds(number * paths, paths)
        first, second = states_of(block_ref, factors)
        third = 0.8 * second + 0.6 * block_ref[2 * factors + PAD :, :]
        hi, lo = split2(basis_rows(pick(core, first, second)) * weights_of(block_ref, factors))
        wide_scr[:, mine] = jnp.concatenate([hi, lo], axis=0)
        hi, mid, low = split3(pick(core, second, third))
        hi, mid, low = hi.astype(F32), mid.astype(F32), low.astype(F32)
        ones = jnp.where(lax.broadcasted_iota(jnp.int32, (DEPTH - 6 * factors, paths), 0) < 3, 1.0, 0.0)
        stacked = jnp.concatenate([hi, hi, mid, mid, hi, low, ones], axis=0)
        states_scr[mine, :] = stacked.T.astype(BF16)


def load_rows(cols, load_ref, strike_ref, load_scr, slot):
    factors = load_ref.shape[0]
    hi, mid, low = split3(load_ref[:, cols])
    for part, piece in enumerate((hi, mid, hi, mid, low, hi)):
        load_scr[slot, pl.ds(part * factors, factors), :] = piece
    s_hi, s_mid, s_low = split3(-strike_ref[:, cols])
    rows = lax.broadcasted_iota(jnp.int32, (16, TILE), 0)
    strike_rows = jnp.where(rows == 1, s_mid.astype(F32), jnp.where(rows == 2, s_low.astype(F32), 0.0))
    strike_rows = jnp.where(rows == 0, s_hi.astype(F32), strike_rows)
    load_scr[slot, pl.ds(6 * factors, 16), :] = strike_rows.astype(BF16)


def chunk_moments(pay, rows, wide_scr):
    wide = wide_scr.shape[0] // 2
    hi, lo = split2(jnp.maximum(pay, 0.0))
    both = mm(wide_scr[:, rows], hi)
    return both[:wide] + (both[wide:] + mm(wide_scr[:wide, rows], lo))


def tile_at(index):
    return pl.ds(pl.multiple_of(index * TILE, TILE), TILE)


def copies(sources, targets, sems):
    return [pltpu.make_async_copy(src, dst, sems.at[i]) for i, (src, dst) in enumerate(zip(sources, targets))]


def moment_kernel(
    groups, counts_ref, own_ref, other_ref, load_hbm, strike_hbm, notional_hbm, set_hbm, *refs
):
    outs = refs[:groups]
    load_ref, strike_ref, notional_ref, set_ref, sems, net_scr, *scratch = refs[groups:]
    moves = copies(
        (load_hbm, strike_hbm, notional_hbm, set_hbm), (load_ref, strike_ref, notional_ref, set_ref), sems
    )
    for move in moves:
        move.start()
    group = lax.axis_index("trade")
    filled = counts_ref[group]
    owned = net_scr.shape[0]
    bits = log2(owned)
    rows = 16
    prepare((own_ref, other_ref), *scratch, load_ref.shape[0])
    net_scr[...] = jnp.zeros_like(net_scr)
    for move in moves:
        move.wait()

    states_scr, wide_scr, load_scr = scratch
    chunks = [pl.ds(start, CHUNK) for start in range(0, states_scr.shape[0], CHUNK)]

    def add_tile(index, moment):
        cols = tile_at(index)
        slot_ids = index * TILE + lax.broadcasted_iota(jnp.int32, (1, TILE), 1)
        hi, lo = split2(moment * jnp.where(slot_ids < filled, notional_ref[:, cols], 0.0))
        both = jnp.concatenate([hi, lo], axis=0)
        both = both.reshape(both.shape[0] // rows, rows, TILE)
        sets = set_ref[:, cols]
        to_group = jnp.broadcast_to((sets >> bits) ^ group, (rows, TILE))
        parts = []
        for away in range(groups):
            mask = jnp.where(to_group == away, 1.0, 0.0).astype(BF16)
            parts.append((both * mask[None]).reshape(-1, TILE))
        one_hot = lax.broadcasted_iota(jnp.int32, (owned, TILE), 0) == (sets & (owned - 1))
        one_hot = jnp.where(one_hot, 1.0, 0.0).astype(BF16)
        net_scr[...] += mm(one_hot, jnp.concatenate(parts, axis=0), NT)

    def step(turn, carry):
        stages = [(slot, chunk) for slot in range(SLOTS) for chunk in chunks]
        pays, moment = {}, None
        for number in range(len(stages) + 1):
            if number < len(stages):
                slot, chunk = stages[number]
                if number % len(chunks) == 0:
                    load_rows(tile_at(SLOTS * turn + slot), load_ref, strike_ref, load_scr, slot)
                pays[number] = mm(states_scr[chunk, :], load_scr[slot])
            if number > 0:
                slot, chunk = stages[number - 1]
                part = chunk_moments(pays.pop(number - 1), chunk, wide_scr)
                moment = part if moment is None else moment + part
                if number % len(chunks) == 0:
                    add_tile(SLOTS * turn + slot, moment)
                    moment = None
        return carry

    lax.fori_loop(0, load_ref.shape[1] // (SLOTS * TILE), step, 0)
    wide = net_scr.shape[1] // (2 * groups)
    half = owned // 2
    for away, out in enumerate(outs):
        net = net_scr[:, 2 * wide * away : 2 * wide * (away + 1)]
        net = net[:, :wide] + net[:, wide:]
        out[...] = jnp.concatenate([net[:half], net[half:]], axis=1)


def inverse_kernel(factors, *refs):
    blocks, inverse_ref = refs[:-1], refs[-1]
    core = lax.axis_index("path") & 1
    wide = 2 * factors
    sub = lax.broadcasted_iota(jnp.int32, (wide, wide), 0)
    lane = lax.broadcasted_iota(jnp.int32, (wide, wide), 1)
    gram = jnp.zeros((wide, wide), F32)
    for block in path_blocks(blocks):
        basis = basis_rows(pick(core, *states_of(block, factors)))
        gram = gram + mm_full(basis * weights_of(block, factors), basis, NT)
    mat = gram
    for k in range(wide):
        row = mat[k : k + 1, :]
        col = mat[:, k : k + 1]
        pivot = 1.0 / mat[k : k + 1, k : k + 1]
        row = jnp.where(lane[:1] == k, 1.0, row) * pivot
        mat = jnp.where(sub == k, row, jnp.where(lane == k, 0.0, mat) - col * row)
    eye = jnp.where(sub == lane, 1.0, 0.0)
    mat = mat + mm_full(mat, eye - mm_full(gram, mat))
    zero = jnp.zeros_like(mat)
    upper = jnp.concatenate([mat, zero], axis=1)
    inverse_ref[...] = jnp.concatenate([upper, jnp.concatenate([zero, mat], axis=1)], axis=0)


def path_blocks(refs):
    for ref in refs:
        if len(ref.shape) == 2:
            yield ref
        else:
            for index in range(ref.shape[0]):
                yield ref.at[index]


def sum_kernel(*refs):
    total = refs[0][...]
    for ref in refs[1:-1]:
        total = total + ref[...]
    refs[-1][...] = total


def coeff_kernel(*refs):
    total = refs[0][...]
    for ref in refs[1:-2]:
        total = total + ref[...]
    refs[-1][...] = mm_full(total, refs[-2][...])


def exposure_kernel(factors, mine_ref, other_ref, limits_ref, *refs):
    blocks, (exposure_ref, expected_ref) = refs[:-2], refs[-2:]
    core = lax.axis_index("path") & 1
    wide = 2 * factors
    paths = blocks[0].shape[1]
    limits = 0.25 * limits_ref[...].astype(F32)
    mine, other = mine_ref[...], other_ref[...]
    coeffs = []
    for packed in (pick(core, mine, other), pick(core, other, mine)):
        hi, lo = split2(jnp.concatenate([packed[:, :wide], packed[:, wide:]], axis=0))
        coeffs.append(jnp.concatenate([hi, hi, lo], axis=1))
    sums = [jnp.zeros((limits.shape[0], 128), F32) for _ in coeffs]
    total = jnp.zeros((1, 1), F32)
    for number, block in enumerate(path_blocks(blocks)):
        weight_row = weights_of(block, factors)
        total = total + jnp.sum(weight_row, keepdims=True)
        for date, state in enumerate(states_of(block, factors)):
            hi, lo = split2(basis_rows(state))
            value = jnp.maximum(mm(coeffs[date], jnp.concatenate([hi, lo, hi], axis=0)) - limits, 0.0)
            if number == 0:
                exposure_ref[date] = value
            product = value * weight_row
            for c in range(paths // 128):
                sums[date] = sums[date] + product[:, c * 128 : (c + 1) * 128]
    for date, partial in enumerate(sums):
        expected_ref[date : date + 1, :] = jnp.sum(partial.T, axis=0, keepdims=True) / total


def swap(x, axis, away):
    return lax.ppermute(x, axis, [(i, i ^ away) for i in range(lax.axis_size(axis))])


def run(kernel, name, out, specs, args, mib, scratch=(), gflops=0.0):
    return pl.pallas_call(
        kernel,
        out_shape=out,
        in_specs=specs,
        out_specs=jax.tree.map(lambda _: VMEM, out),
        scratch_shapes=list(scratch),
        compiler_params=pltpu.CompilerParams(vmem_limit_bytes=int(mib * MIB)),
        cost_estimate=pl.CostEstimate(flops=int(gflops * 1e9), bytes_accessed=10**5, transcendentals=0),
        name=name,
    )(*args)


def body(
    start_state, shocks, loadings, strikes, notionals, trade_set, live_counts, weights, thresholds
):
    paths, factors = start_state.shape
    dates = shocks.shape[0]
    slots = loadings.shape[1]
    owned = thresholds.shape[0]
    groups = lax.axis_size("trade")
    ranks = lax.axis_size("path")
    wide = 2 * factors
    assert dates == 2

    shape = jax.ShapeDtypeStruct
    short, whole = run(
        pack_kernel, "pack_states",
        [shape(((dates - 1) * factors + factors + PAD, paths), F32), shape(((dates + 1) * factors + PAD, paths), F32)],
        [VMEM] * 3, (start_state.T, jnp.swapaxes(shocks, 1, 2), weights[None, :]), 58,
    )
    other = swap(whole, "path", 1)
    across = [swap(short, "path", 2 * away) for away in range(1, ranks // 2)]

    strike_row, notional_row, set_row = strikes[None, :], notionals[None, :], trade_set[None, :]
    nets = run(
        functools.partial(moment_kernel, groups), "net_moments",
        [shape((owned // 2, 2 * wide), F32)] * groups, [SMEM, VMEM, VMEM] + [ANY] * 4,
        (live_counts, whole, other, loadings, strike_row, notional_row, set_row), 52.75,
        [
            pltpu.VMEM((factors, slots), F32),
            pltpu.VMEM((1, slots), F32),
            pltpu.VMEM((1, slots), F32),
            pltpu.VMEM((1, slots), jnp.int32),
            pltpu.SemaphoreType.DMA((4,)),
            pltpu.VMEM((owned, 2 * wide * groups), F32),
            pltpu.VMEM((2 * paths, DEPTH), BF16),
            pltpu.VMEM((2 * wide, 2 * paths), BF16),
            pltpu.VMEM((SLOTS, DEPTH, TILE), BF16),
        ],
        20.0,
    )
    *across, net = lax.optimization_barrier((*across, nets[0]))
    others = swap(jnp.stack(across), "path", 1)
    got = [swap(nets[away], "trade", away) for away in range(1, groups)]
    blocks = (whole, other, *across, others)
    inverse = run(
        functools.partial(inverse_kernel, factors), "gram_inverse", shape((2 * wide, 2 * wide), F32),
        [VMEM] * len(blocks), blocks, 8, (), 6.0,
    )
    inverse, net = lax.optimization_barrier((inverse, net))
    part = run(
        sum_kernel, "group_sum", shape((owned // 2, 2 * wide), F32), [VMEM] * groups, [net] + got, 4
    )
    got = [swap(part, "path", 2 * away) for away in range(1, ranks // 2)]
    mine = run(
        coeff_kernel, "set_coeffs", shape((owned // 2, 2 * wide), F32), [VMEM] * (ranks // 2 + 1),
        [part] + got + [inverse], 4,
    )
    partner = swap(mine, "path", 1)
    exposure, expected = run(
        functools.partial(exposure_kernel, factors), "set_exposure",
        (shape((dates, owned, paths), F32), shape((dates, owned), F32)), [VMEM] * (3 + len(blocks)),
        (mine, partner, thresholds[:, None], *blocks), 16, (), 2.0,
    )
    return (exposure, expected)


def solution(mesh):
    placed = (
        P("path", None),
        P(None, "path", None),
        P(None, "trade"),
        P("trade"),
        P("trade"),
        P("trade"),
        P(),
        P("path"),
        P("trade"),
    )
    return jax.shard_map(
        body,
        mesh=mesh,
        in_specs=placed,
        out_specs=(P(None, "trade", "path"), P(None, "trade")),
        check_vma=False,
    )
```

```python
import functools

import jax
import jax.numpy as jnp
from jax import lax
from jax.experimental import pallas as pl
from jax.experimental.pallas import tpu as pltpu
from jax.sharding import PartitionSpec as P

HIGHEST_PREC = lax.Precision.HIGHEST
ROOT_HALF = 0.7071067811865476
F32 = jnp.float32
BF16 = jnp.bfloat16
TILE = 512
CHUNK = 256
SLOTS = 2
DEPTH = 256
PAD = 8
MIB = 1024 * 1024
NN = (((1,), (0,)), ((), ()))
NT = (((1,), (1,)), ((), ()))
VMEM = pl.BlockSpec(memory_space=pltpu.VMEM)
SMEM = pl.BlockSpec(memory_space=pltpu.SMEM)
HBM = pl.BlockSpec(memory_space=pltpu.HBM)


def mm(a, b, dims=NN):
    return lax.dot_general(a, b, dims, preferred_element_type=F32)


def mm_full(a, b, dims=NN):
    return lax.dot_general(a, b, dims, preferred_element_type=F32, precision=HIGHEST_PREC)


def split2(x):
    hi = x.astype(BF16)
    return hi, (x - hi.astype(F32)).astype(BF16)


def split3(x):
    hi = x.astype(BF16)
    rest = x - hi.astype(F32)
    mid = rest.astype(BF16)
    return hi, mid, (rest - mid.astype(F32)).astype(BF16)


def log2(n):
    assert n & (n - 1) == 0
    return n.bit_length() - 1


def basis_rows(state):
    return jnp.concatenate([state, (state * state - 1.0) * ROOT_HALF], axis=0)


def pick(core, first, second):
    return jnp.where(core == 0, first, second)


def states_of(ref, factors):
    state = ref[:factors, :]
    return state, 0.8 * state + 0.6 * ref[factors : 2 * factors, :]


def weights_of(ref, factors):
    return ref[2 * factors : 2 * factors + 1, :]


def pack_kernel(counts_ref, start_ref, shocks_ref, weights_ref, short_ref, whole_ref):
    factors, paths = start_ref.shape
    filled = counts_ref[lax.axis_index("trade")].astype(F32)
    spare = lax.broadcasted_iota(jnp.int32, (PAD, paths), 0) > 0
    for ref in (short_ref, whole_ref):
        ref[:factors, :] = start_ref[...]
        ref[factors : 2 * factors, :] = shocks_ref[0]
        ref[2 * factors : 2 * factors + PAD, :] = jnp.where(spare, filled, weights_ref[...].astype(F32))
    whole_ref[2 * factors + PAD :, :] = shocks_ref[1]


def prepare(number, start, shocks, weight_row, states_scr, wide_scr):
    core = lax.axis_index("path") & 1
    factors, paths = start.shape
    mine = pl.ds(number * paths, paths)
    second = 0.8 * start + 0.6 * shocks[0]
    third = 0.8 * second + 0.6 * shocks[1]
    hi, lo = split2(basis_rows(pick(core, start, second)) * weight_row)
    wide_scr[:, mine] = jnp.concatenate([hi, lo], axis=0)
    hi, mid, low = split3(pick(core, second, third))
    hi, mid, low = hi.astype(F32), mid.astype(F32), low.astype(F32)
    ones = jnp.where(lax.broadcasted_iota(jnp.int32, (DEPTH - 6 * factors, paths), 0) < 3, 1.0, 0.0)
    stacked = jnp.concatenate([hi, hi, mid, mid, hi, low, ones], axis=0)
    states_scr[mine, :] = stacked.T.astype(BF16)


def load_rows(cols, load_ref, strike_ref, load_scr, slot):
    factors = load_ref.shape[0]
    hi, mid, low = split3(load_ref[:, cols])
    for part, piece in enumerate((hi, mid, hi, mid, low, hi)):
        load_scr[slot, pl.ds(part * factors, factors), :] = piece
    s_hi, s_mid, s_low = split3(-strike_ref[:, cols])
    rows = lax.broadcasted_iota(jnp.int32, (16, TILE), 0)
    strike_rows = jnp.where(rows == 1, s_mid.astype(F32), jnp.where(rows == 2, s_low.astype(F32), 0.0))
    strike_rows = jnp.where(rows == 0, s_hi.astype(F32), strike_rows)
    load_scr[slot, pl.ds(6 * factors, 16), :] = strike_rows.astype(BF16)


def chunk_moments(pay, rows, wide_scr):
    wide = wide_scr.shape[0] // 2
    hi, lo = split2(jnp.maximum(pay, 0.0))
    both = mm(wide_scr[:, rows], hi)
    return both[:wide] + (both[wide:] + mm(wide_scr[:wide, rows], lo))


def tile_at(index):
    return pl.ds(pl.multiple_of(index * TILE, TILE), TILE)


def copies(sources, targets, sems):
    return [pltpu.make_async_copy(src, dst, sems.at[i]) for i, (src, dst) in enumerate(zip(sources, targets))]


def moment_kernel(
    groups, own_ref, other_ref, load_hbm, strike_hbm, notional_hbm, set_hbm, *refs
):
    outs = refs[:groups]
    *staged, sems, net_scr, states_scr, wide_scr, load_scr = refs[groups:]
    load_ref, strike_ref, notional_ref, set_ref = staged
    moves = copies((load_hbm, strike_hbm, notional_hbm, set_hbm), staged, sems)
    for move in moves:
        move.start()
    group = lax.axis_index("trade")
    factors = load_ref.shape[0]
    filled = other_ref[2 * factors + 1 : 2 * factors + 2, :1].astype(jnp.int32)
    owned = net_scr.shape[0]
    bits = log2(owned)
    rows = 16
    load_scr[...] = jnp.zeros_like(load_scr)
    net_scr[...] = jnp.zeros_like(net_scr)
    for number, ref in enumerate((own_ref, other_ref)):
        shocks = (ref[factors : 2 * factors, :], ref[2 * factors + PAD :, :])
        prepare(number, ref[:factors, :], shocks, weights_of(ref, factors), states_scr, wide_scr)
    for move in moves:
        move.wait()

    chunks = [pl.ds(start, CHUNK) for start in range(0, states_scr.shape[0], CHUNK)]

    def add_tile(index, moment):
        cols = tile_at(index)
        slot_ids = index * TILE + lax.broadcasted_iota(jnp.int32, (1, TILE), 1)
        hi, lo = split2(moment * jnp.where(slot_ids < filled, notional_ref[:, cols], 0.0))
        both = jnp.concatenate([hi, lo], axis=0)
        both = both.reshape(both.shape[0] // rows, rows, TILE)
        sets = set_ref[:, cols]
        to_group = jnp.broadcast_to((sets >> bits) ^ group, (rows, TILE))
        parts = []
        for away in range(groups):
            mask = jnp.where(to_group == away, 1.0, 0.0).astype(BF16)
            parts.append((both * mask[None]).reshape(-1, TILE))
        one_hot = lax.broadcasted_iota(jnp.int32, (owned, TILE), 0) == (sets & (owned - 1))
        one_hot = jnp.where(one_hot, 1.0, 0.0).astype(BF16)
        net_scr[...] += mm(one_hot, jnp.concatenate(parts, axis=0), NT)

    def step(turn, carry):
        stages = [(slot, chunk) for slot in range(SLOTS) for chunk in chunks]
        pays, moment = {}, None
        for number in range(len(stages) + 1):
            if number < len(stages):
                slot, chunk = stages[number]
                if number % len(chunks) == 0:
                    load_rows(tile_at(SLOTS * turn + slot), load_ref, strike_ref, load_scr, slot)
                pays[number] = mm(states_scr[chunk, :], load_scr[slot])
            if number > 0:
                slot, chunk = stages[number - 1]
                part = chunk_moments(pays.pop(number - 1), chunk, wide_scr)
                moment = part if moment is None else moment + part
                if number % len(chunks) == 0:
                    add_tile(SLOTS * turn + slot, moment)
                    moment = None
        return carry

    lax.fori_loop(0, load_ref.shape[1] // (SLOTS * TILE), step, 0)
    wide = net_scr.shape[1] // (2 * groups)
    half = owned // 2
    for away, out in enumerate(outs):
        net = net_scr[:, 2 * wide * away : 2 * wide * (away + 1)]
        net = net[:, :wide] + net[:, wide:]
        out[...] = jnp.concatenate([net[:half], net[half:]], axis=1)


def inverse_kernel(factors, *refs):
    blocks, inverse_ref = refs[:-1], refs[-1]
    core = lax.axis_index("path") & 1
    wide = 2 * factors
    sub = lax.broadcasted_iota(jnp.int32, (wide, wide), 0)
    lane = lax.broadcasted_iota(jnp.int32, (wide, wide), 1)
    gram = jnp.zeros((wide, wide), F32)
    for block in path_blocks(blocks):
        basis = basis_rows(pick(core, *states_of(block, factors)))
        gram = gram + mm_full(basis * weights_of(block, factors), basis, NT)
    mat = gram
    for k in range(0, wide, 2):
        top, low = mat[k : k + 1, :], mat[k + 1 : k + 2, :]
        left, right = mat[:, k : k + 1], mat[:, k + 1 : k + 2]
        a, b = left[k : k + 1], right[k : k + 1]
        c, d = left[k + 1 : k + 2], right[k + 1 : k + 2]
        scale = 1.0 / (a * d - b * c)
        top = jnp.where(lane[:1] == k, 1.0, jnp.where(lane[:1] == k + 1, 0.0, top))
        low = jnp.where(lane[:1] == k, 0.0, jnp.where(lane[:1] == k + 1, 1.0, low))
        top, low = (d * top - b * low) * scale, (a * low - c * top) * scale
        rest = jnp.where((lane >> 1) == k // 2, 0.0, mat) - left * top - right * low
        mat = jnp.where(sub == k, top, jnp.where(sub == k + 1, low, rest))
    eye = jnp.where(sub == lane, 1.0, 0.0)
    mat = mat + mm_full(mat, eye - mm_full(gram, mat))
    zero = jnp.zeros_like(mat)
    upper = jnp.concatenate([mat, zero], axis=1)
    inverse_ref[...] = jnp.concatenate([upper, jnp.concatenate([zero, mat], axis=1)], axis=0)


def path_blocks(refs):
    for ref in refs:
        if len(ref.shape) == 2:
            yield ref
        else:
            for index in range(ref.shape[0]):
                yield ref.at[index]


def sum_kernel(*refs):
    total = refs[0][...]
    for ref in refs[1:-1]:
        total = total + ref[...]
    refs[-1][...] = total


def coeff_kernel(*refs):
    total = refs[0][...]
    for ref in refs[1:-2]:
        total = total + ref[...]
    refs[-1][...] = mm_full(total, refs[-2][...])


def exposure_kernel(factors, mine_ref, other_ref, limits_ref, *refs):
    blocks, (exposure_ref, expected_ref) = refs[:-2], refs[-2:]
    core = lax.axis_index("path") & 1
    wide = 2 * factors
    paths = blocks[0].shape[1]
    limits = 0.25 * limits_ref[...].astype(F32)
    mine, other = mine_ref[...], other_ref[...]
    coeffs = []
    for packed in (pick(core, mine, other), pick(core, other, mine)):
        hi, lo = split2(jnp.concatenate([packed[:, :wide], packed[:, wide:]], axis=0))
        coeffs.append(jnp.concatenate([hi, hi, lo], axis=1))
    sums = [jnp.zeros((limits.shape[0], 128), F32) for _ in coeffs]
    total = jnp.zeros((1, 1), F32)
    for number, block in enumerate(path_blocks(blocks)):
        weight_row = weights_of(block, factors)
        total = total + jnp.sum(weight_row, keepdims=True)
        for date, state in enumerate(states_of(block, factors)):
            hi, lo = split2(basis_rows(state))
            value = jnp.maximum(mm(coeffs[date], jnp.concatenate([hi, lo, hi], axis=0)) - limits, 0.0)
            if number == 0:
                exposure_ref[date] = value
            product = value * weight_row
            for c in range(paths // 128):
                sums[date] = sums[date] + product[:, c * 128 : (c + 1) * 128]
    for date, partial in enumerate(sums):
        expected_ref[date : date + 1, :] = jnp.sum(partial.T, axis=0, keepdims=True) / total


def swap(x, axis, away):
    return lax.ppermute(x, axis, [(i, i ^ away) for i in range(lax.axis_size(axis))])


def run(kernel, name, out, specs, args, mib, scratch=(), gflops=0.0):
    return pl.pallas_call(
        kernel,
        out_shape=out,
        in_specs=specs,
        out_specs=jax.tree.map(lambda _: VMEM, out),
        scratch_shapes=list(scratch),
        compiler_params=pltpu.CompilerParams(vmem_limit_bytes=int(mib * MIB)),
        cost_estimate=pl.CostEstimate(flops=int(gflops * 1e9), bytes_accessed=10**5, transcendentals=0),
        name=name,
    )(*args)


def body(
    start_state, shocks, loadings, strikes, notionals, trade_set, live_counts, weights, thresholds
):
    paths, factors = start_state.shape
    dates = shocks.shape[0]
    slots = loadings.shape[1]
    owned = thresholds.shape[0]
    groups = lax.axis_size("trade")
    ranks = lax.axis_size("path")
    wide = 2 * factors
    assert dates == 2

    shape = jax.ShapeDtypeStruct
    start_t, shocks_t, weights_row = start_state.T, jnp.swapaxes(shocks, 1, 2), weights[None, :]
    short, whole = run(
        pack_kernel, "pack_states",
        [shape(((dates - 1) * factors + factors + PAD, paths), F32), shape(((dates + 1) * factors + PAD, paths), F32)],
        [SMEM] + [VMEM] * 3, (live_counts, start_t, shocks_t, weights_row), 58,
    )
    other = swap(whole, "path", 1)
    across = [swap(short, "path", 2 * away) for away in range(1, ranks // 2)]

    strike_row, notional_row, set_row = strikes[None, :], notionals[None, :], trade_set[None, :]
    nets = run(
        functools.partial(moment_kernel, groups), "net_moments",
        [shape((owned // 2, 2 * wide), F32)] * groups, [VMEM] * 2 + [HBM] * 4,
        (whole, other, loadings, strike_row, notional_row, set_row), 52.75,
        [
            pltpu.VMEM((factors, slots), F32),
            pltpu.VMEM((1, slots), F32),
            pltpu.VMEM((1, slots), F32),
            pltpu.VMEM((1, slots), jnp.int32),
            pltpu.SemaphoreType.DMA((4,)),
            pltpu.VMEM((owned, 2 * wide * groups), F32),
            pltpu.VMEM((2 * paths, DEPTH), BF16),
            pltpu.VMEM((2 * wide, 2 * paths), BF16),
            pltpu.VMEM((SLOTS, DEPTH, TILE), BF16),
        ],
        20.0,
    )
    *across, net = lax.optimization_barrier((*across, nets[0]))
    others = swap(jnp.stack(across), "path", 1)
    got = [swap(nets[away], "trade", away) for away in range(1, groups)]
    blocks = (whole, other, *across, others)
    inverse = run(
        functools.partial(inverse_kernel, factors), "gram_inverse", shape((2 * wide, 2 * wide), F32),
        [VMEM] * len(blocks), blocks, 8, (), 6.0,
    )
    inverse, net = lax.optimization_barrier((inverse, net))
    part = run(
        sum_kernel, "group_sum", shape((owned // 2, 2 * wide), F32), [VMEM] * groups, [net] + got, 4
    )
    got = [swap(part, "path", 2 * away) for away in range(1, ranks // 2)]
    mine = run(
        coeff_kernel, "set_coeffs", shape((owned // 2, 2 * wide), F32), [VMEM] * (ranks // 2 + 1),
        [part] + got + [inverse], 4,
    )
    partner = swap(mine, "path", 1)
    exposure, expected = run(
        functools.partial(exposure_kernel, factors), "set_exposure",
        (shape((dates, owned, paths), F32), shape((dates, owned), F32)), [VMEM] * (3 + len(blocks)),
        (mine, partner, thresholds[:, None], *blocks), 16, (), 2.0,
    )
    return (exposure, expected)


def solution(mesh):
    placed = (
        P("path", None),
        P(None, "path", None),
        P(None, "trade"),
        P("trade"),
        P("trade"),
        P("trade"),
        P(),
        P("path"),
        P("trade"),
    )
    return jax.shard_map(
        body,
        mesh=mesh,
        in_specs=placed,
        out_specs=(P(None, "trade", "path"), P(None, "trade")),
        check_vma=False,
    )
```

```python
import functools

import jax
import jax.numpy as jnp
from jax import lax
from jax.experimental import pallas as pl
from jax.experimental.pallas import tpu as pltpu
from jax.sharding import PartitionSpec as P

HIGHEST_PREC = lax.Precision.HIGHEST
ROOT_HALF = 0.7071067811865476
F32 = jnp.float32
BF16 = jnp.bfloat16
TILE = 512
CHUNK = 512
SLOTS = 4
FIRST_PIVOTS = 36
DEPTH = 256
PAD = 8
MIB = 1024 * 1024
NN = (((1,), (0,)), ((), ()))
NT = (((1,), (1,)), ((), ()))
VMEM = pl.BlockSpec(memory_space=pltpu.VMEM)
SMEM = pl.BlockSpec(memory_space=pltpu.SMEM)
HBM = pl.BlockSpec(memory_space=pltpu.HBM)


def mm(a, b, dims=NN):
    return lax.dot_general(a, b, dims, preferred_element_type=F32)


def mm_full(a, b, dims=NN):
    return lax.dot_general(a, b, dims, preferred_element_type=F32, precision=HIGHEST_PREC)


def split2(x):
    hi = x.astype(BF16)
    return hi, (x - hi.astype(F32)).astype(BF16)


def split3(x):
    hi = x.astype(BF16)
    rest = x - hi.astype(F32)
    mid = rest.astype(BF16)
    return hi, mid, (rest - mid.astype(F32)).astype(BF16)


def log2(n):
    assert n & (n - 1) == 0
    return n.bit_length() - 1


def basis_rows(state):
    return jnp.concatenate([state, (state * state - 1.0) * ROOT_HALF], axis=0)


def pick(core, first, second):
    return jnp.where(core == 0, first, second)


def states_of(ref, factors):
    state = ref[:factors, :]
    return state, 0.8 * state + 0.6 * ref[factors : 2 * factors, :]


def weights_of(ref, factors):
    return ref[2 * factors : 2 * factors + 1, :]


def pack_kernel(counts_ref, start_ref, shocks_ref, weights_ref, short_ref, whole_ref):
    factors, paths = start_ref.shape
    filled = counts_ref[lax.axis_index("trade")].astype(F32)
    spare = lax.broadcasted_iota(jnp.int32, (PAD, paths), 0) > 0
    for ref in (short_ref, whole_ref):
        ref[:factors, :] = start_ref[...]
        ref[factors : 2 * factors, :] = shocks_ref[0]
        ref[2 * factors : 2 * factors + PAD, :] = jnp.where(spare, filled, weights_ref[...].astype(F32))
    whole_ref[2 * factors + PAD :, :] = shocks_ref[1]


def prepare(number, start, shocks, weight_row, states_scr, wide_scr):
    core = lax.axis_index("path") & 1
    factors, paths = start.shape
    mine = pl.ds(number * paths, paths)
    second = 0.8 * start + 0.6 * shocks[0]
    third = 0.8 * second + 0.6 * shocks[1]
    hi, lo = split2(basis_rows(pick(core, start, second)) * weight_row)
    wide_scr[:, mine] = jnp.concatenate([hi, lo], axis=0)
    hi, mid, low = split3(pick(core, second, third))
    hi, mid, low = hi.astype(F32), mid.astype(F32), low.astype(F32)
    ones = jnp.where(lax.broadcasted_iota(jnp.int32, (DEPTH - 6 * factors, paths), 0) < 3, 1.0, 0.0)
    stacked = jnp.concatenate([hi, hi, mid, mid, hi, low, ones], axis=0)
    states_scr[mine, :] = stacked.T.astype(BF16)


def load_rows(cols, load_ref, strike_ref, load_scr, slot):
    factors = load_ref.shape[0]
    hi, mid, low = split3(load_ref[:, cols])
    for part, piece in enumerate((hi, mid, hi, mid, low, hi)):
        load_scr[slot, pl.ds(part * factors, factors), :] = piece
    s_hi, s_mid, s_low = split3(-strike_ref[:, cols])
    rows = lax.broadcasted_iota(jnp.int32, (16, TILE), 0)
    strike_rows = jnp.where(rows == 1, s_mid.astype(F32), jnp.where(rows == 2, s_low.astype(F32), 0.0))
    strike_rows = jnp.where(rows == 0, s_hi.astype(F32), strike_rows)
    load_scr[slot, pl.ds(6 * factors, 16), :] = strike_rows.astype(BF16)


def chunk_moments(pay, rows, wide_scr):
    wide = wide_scr.shape[0] // 2
    hi, lo = split2(jnp.maximum(pay, 0.0))
    both = mm(wide_scr[:, rows], hi)
    return both[:wide] + (both[wide:] + mm(wide_scr[:wide, rows], lo))


def tile_at(index):
    return pl.ds(pl.multiple_of(index * TILE, TILE), TILE)


def copies(sources, targets, sems):
    return [pltpu.make_async_copy(src, dst, sems.at[i]) for i, (src, dst) in enumerate(zip(sources, targets))]


def moment_kernel(
    groups, own_ref, other_ref, load_hbm, strike_hbm, notional_hbm, set_hbm, *refs
):
    outs = refs[:groups]
    *staged, sems, net_scr, states_scr, wide_scr, load_scr = refs[groups:]
    load_ref, strike_ref, notional_ref, set_ref = staged
    moves = copies((load_hbm, strike_hbm, notional_hbm, set_hbm), staged, sems)
    for move in moves:
        move.start()
    group = lax.axis_index("trade")
    factors = load_ref.shape[0]
    filled = other_ref[2 * factors + 1 : 2 * factors + 2, :1].astype(jnp.int32)
    owned = net_scr.shape[0]
    bits = log2(owned)
    rows = 16
    load_scr[...] = jnp.zeros_like(load_scr)
    net_scr[...] = jnp.zeros_like(net_scr)
    for number, ref in enumerate((own_ref, other_ref)):
        shocks = (ref[factors : 2 * factors, :], ref[2 * factors + PAD :, :])
        prepare(number, ref[:factors, :], shocks, weights_of(ref, factors), states_scr, wide_scr)
    for move in moves:
        move.wait()

    chunks = [pl.ds(start, CHUNK) for start in range(0, states_scr.shape[0], CHUNK)]

    def add_tile(index, moment):
        cols = tile_at(index)
        slot_ids = index * TILE + lax.broadcasted_iota(jnp.int32, (1, TILE), 1)
        hi, lo = split2(moment * jnp.where(slot_ids < filled, notional_ref[:, cols], 0.0))
        both = jnp.concatenate([hi, lo], axis=0)
        both = both.reshape(both.shape[0] // rows, rows, TILE)
        sets = set_ref[:, cols]
        to_group = jnp.broadcast_to((sets >> bits) ^ group, (rows, TILE))
        parts = []
        for away in range(groups):
            mask = jnp.where(to_group == away, 1.0, 0.0).astype(BF16)
            parts.append((both * mask[None]).reshape(-1, TILE))
        one_hot = lax.broadcasted_iota(jnp.int32, (owned, TILE), 0) == (sets & (owned - 1))
        one_hot = jnp.where(one_hot, 1.0, 0.0).astype(BF16)
        net_scr[...] += mm(one_hot, jnp.concatenate(parts, axis=0), NT)

    def step(turn, carry):
        stages = [(slot, chunk) for slot in range(SLOTS) for chunk in chunks]
        pays, moment = {}, None
        for number in range(len(stages) + 1):
            if number < len(stages):
                slot, chunk = stages[number]
                if number % len(chunks) == 0:
                    load_rows(tile_at(SLOTS * turn + slot), load_ref, strike_ref, load_scr, slot)
                pays[number] = mm(states_scr[chunk, :], load_scr[slot])
            if number > 0:
                slot, chunk = stages[number - 1]
                part = chunk_moments(pays.pop(number - 1), chunk, wide_scr)
                moment = part if moment is None else moment + part
                if number % len(chunks) == 0:
                    add_tile(SLOTS * turn + slot, moment)
                    moment = None
        return carry

    lax.fori_loop(0, load_ref.shape[1] // (SLOTS * TILE), step, 0)
    wide = net_scr.shape[1] // (2 * groups)
    half = owned // 2
    for away, out in enumerate(outs):
        net = net_scr[:, 2 * wide * away : 2 * wide * (away + 1)]
        net = net[:, :wide] + net[:, wide:]
        out[...] = jnp.concatenate([net[:half], net[half:]], axis=1)


def eliminate(mat, pivots):
    sub = lax.broadcasted_iota(jnp.int32, mat.shape, 0)
    lane = lax.broadcasted_iota(jnp.int32, mat.shape, 1)
    for k in pivots:
        row = mat[k : k + 1, :]
        col = mat[:, k : k + 1]
        pivot = 1.0 / mat[k : k + 1, k : k + 1]
        row = jnp.where(lane[:1] == k, 1.0, row) * pivot
        mat = jnp.where(sub == k, row, jnp.where(lane == k, 0.0, mat) - col * row)
    return mat


def gram_kernel(factors, *refs):
    blocks, gram_ref, mat_ref = refs[:-2], refs[-2], refs[-1]
    core = lax.axis_index("path") & 1
    wide = 2 * factors
    gram = jnp.zeros((wide, wide), F32)
    for block in path_blocks(blocks):
        basis = basis_rows(pick(core, *states_of(block, factors)))
        gram = gram + mm_full(basis * weights_of(block, factors), basis, NT)
    gram_ref[...] = gram
    mat_ref[...] = eliminate(gram, range(FIRST_PIVOTS))


def inverse_kernel(gram_ref, mat_ref, inverse_ref):
    gram = gram_ref[...]
    wide = gram.shape[0]
    mat = eliminate(mat_ref[...], range(FIRST_PIVOTS, wide))
    sub = lax.broadcasted_iota(jnp.int32, (wide, wide), 0)
    lane = lax.broadcasted_iota(jnp.int32, (wide, wide), 1)
    mat = mat + mm_full(mat, jnp.where(sub == lane, 1.0, 0.0) - mm_full(gram, mat))
    zero = jnp.zeros_like(mat)
    upper = jnp.concatenate([mat, zero], axis=1)
    inverse_ref[...] = jnp.concatenate([upper, jnp.concatenate([zero, mat], axis=1)], axis=0)


def path_blocks(refs):
    for ref in refs:
        if len(ref.shape) == 2:
            yield ref
        else:
            for index in range(ref.shape[0]):
                yield ref.at[index]


def sum_kernel(*refs):
    total = refs[0][...]
    for ref in refs[1:-1]:
        total = total + ref[...]
    refs[-1][...] = total


def coeff_kernel(*refs):
    total = refs[0][...]
    for ref in refs[1:-2]:
        total = total + ref[...]
    refs[-1][...] = mm_full(total, refs[-2][...])


def exposure_kernel(factors, mine_ref, other_ref, limits_ref, *refs):
    blocks, (exposure_ref, expected_ref) = refs[:-2], refs[-2:]
    core = lax.axis_index("path") & 1
    wide = 2 * factors
    paths = blocks[0].shape[1]
    limits = 0.25 * limits_ref[...].astype(F32)
    mine, other = mine_ref[...], other_ref[...]
    coeffs = []
    for packed in (pick(core, mine, other), pick(core, other, mine)):
        hi, lo = split2(jnp.concatenate([packed[:, :wide], packed[:, wide:]], axis=0))
        coeffs.append(jnp.concatenate([hi, hi, lo], axis=1))
    sums = [jnp.zeros((limits.shape[0], 128), F32) for _ in coeffs]
    total = jnp.zeros((1, 1), F32)
    for number, block in enumerate(path_blocks(blocks)):
        weight_row = weights_of(block, factors)
        total = total + jnp.sum(weight_row, keepdims=True)
        for date, state in enumerate(states_of(block, factors)):
            hi, lo = split2(basis_rows(state))
            value = jnp.maximum(mm(coeffs[date], jnp.concatenate([hi, lo, hi], axis=0)) - limits, 0.0)
            if number == 0:
                exposure_ref[date] = value
            product = value * weight_row
            for c in range(paths // 128):
                sums[date] = sums[date] + product[:, c * 128 : (c + 1) * 128]
    for date, partial in enumerate(sums):
        expected_ref[date : date + 1, :] = jnp.sum(partial.T, axis=0, keepdims=True) / total


def swap(x, axis, away):
    return lax.ppermute(x, axis, [(i, i ^ away) for i in range(lax.axis_size(axis))])


def run(kernel, name, out, specs, args, mib, scratch=(), gflops=0.0):
    return pl.pallas_call(
        kernel,
        out_shape=out,
        in_specs=specs,
        out_specs=jax.tree.map(lambda _: VMEM, out),
        scratch_shapes=list(scratch),
        compiler_params=pltpu.CompilerParams(vmem_limit_bytes=int(mib * MIB)),
        cost_estimate=pl.CostEstimate(flops=int(gflops * 1e9), bytes_accessed=10**5, transcendentals=0),
        name=name,
    )(*args)


def body(
    start_state, shocks, loadings, strikes, notionals, trade_set, live_counts, weights, thresholds
):
    paths, factors = start_state.shape
    dates = shocks.shape[0]
    slots = loadings.shape[1]
    owned = thresholds.shape[0]
    groups = lax.axis_size("trade")
    ranks = lax.axis_size("path")
    wide = 2 * factors
    assert dates == 2

    shape = jax.ShapeDtypeStruct
    start_t, shocks_t, weights_row = start_state.T, jnp.swapaxes(shocks, 1, 2), weights[None, :]
    short, whole = run(
        pack_kernel, "pack_states",
        [shape(((dates - 1) * factors + factors + PAD, paths), F32), shape(((dates + 1) * factors + PAD, paths), F32)],
        [SMEM] + [VMEM] * 3, (live_counts, start_t, shocks_t, weights_row), 58,
    )
    other = swap(whole, "path", 1)
    across = [swap(short, "path", 2 * away) for away in range(1, ranks // 2)]

    strike_row, notional_row, set_row = strikes[None, :], notionals[None, :], trade_set[None, :]
    nets = run(
        functools.partial(moment_kernel, groups), "net_moments",
        [shape((owned // 2, 2 * wide), F32)] * groups, [VMEM] * 2 + [HBM] * 4,
        (whole, other, loadings, strike_row, notional_row, set_row), 52.75,
        [
            pltpu.VMEM((factors, slots), F32),
            pltpu.VMEM((1, slots), F32),
            pltpu.VMEM((1, slots), F32),
            pltpu.VMEM((1, slots), jnp.int32),
            pltpu.SemaphoreType.DMA((4,)),
            pltpu.VMEM((owned, 2 * wide * groups), F32),
            pltpu.VMEM((2 * paths, DEPTH), BF16),
            pltpu.VMEM((2 * wide, 2 * paths), BF16),
            pltpu.VMEM((SLOTS, DEPTH, TILE), BF16),
        ],
        20.0,
    )
    *across, net = lax.optimization_barrier((*across, nets[0]))
    others = swap(jnp.stack(across), "path", 1)
    got = [swap(nets[away], "trade", away) for away in range(1, groups)]
    blocks = (whole, other, *across, others)
    gram, mat = run(
        functools.partial(gram_kernel, factors), "gram_first_pivots", [shape((wide, wide), F32)] * 2,
        [VMEM] * len(blocks), blocks, 8, (), 5.0,
    )
    mat, net = lax.optimization_barrier((mat, net))
    inverse = run(
        inverse_kernel, "gram_inverse", shape((2 * wide, 2 * wide), F32), [VMEM] * 2, (gram, mat), 8, (), 3.0
    )
    part = run(
        sum_kernel, "group_sum", shape((owned // 2, 2 * wide), F32), [VMEM] * groups, [net] + got, 4
    )
    got = [swap(part, "path", 2 * away) for away in range(1, ranks // 2)]
    mine = run(
        coeff_kernel, "set_coeffs", shape((owned // 2, 2 * wide), F32), [VMEM] * (ranks // 2 + 1),
        [part] + got + [inverse], 4,
    )
    partner = swap(mine, "path", 1)
    exposure, expected = run(
        functools.partial(exposure_kernel, factors), "set_exposure",
        (shape((dates, owned, paths), F32), shape((dates, owned), F32)), [VMEM] * (3 + len(blocks)),
        (mine, partner, thresholds[:, None], *blocks), 16, (), 2.0,
    )
    return (exposure, expected)


def solution(mesh):
    placed = (
        P("path", None),
        P(None, "path", None),
        P(None, "trade"),
        P("trade"),
        P("trade"),
        P("trade"),
        P(),
        P("path"),
        P("trade"),
    )
    return jax.shard_map(
        body,
        mesh=mesh,
        in_specs=placed,
        out_specs=(P(None, "trade", "path"), P(None, "trade")),
        check_vma=False,
    )
```

```python
import functools

import jax
import jax.numpy as jnp
from jax import lax
from jax.experimental import pallas as pl
from jax.experimental.pallas import tpu as pltpu
from jax.sharding import PartitionSpec as P

HIGHEST_PREC = lax.Precision.HIGHEST
ROOT_HALF = 0.7071067811865476
F32 = jnp.float32
BF16 = jnp.bfloat16
TILE = 512
CHUNK = 512
SLOTS = 8
FIRST_PIVOTS = 36
DEPTH = 256
PAD = 8
MIB = 1024 * 1024
NN = (((1,), (0,)), ((), ()))
NT = (((1,), (1,)), ((), ()))
VMEM = pl.BlockSpec(memory_space=pltpu.VMEM)
SMEM = pl.BlockSpec(memory_space=pltpu.SMEM)
HBM = pl.BlockSpec(memory_space=pltpu.HBM)


def mm(a, b, dims=NN):
    return lax.dot_general(a, b, dims, preferred_element_type=F32)


def mm_full(a, b, dims=NN):
    return lax.dot_general(a, b, dims, preferred_element_type=F32, precision=HIGHEST_PREC)


def split2(x):
    hi = x.astype(BF16)
    return hi, (x - hi.astype(F32)).astype(BF16)


def split3(x):
    hi = x.astype(BF16)
    rest = x - hi.astype(F32)
    mid = rest.astype(BF16)
    return hi, mid, (rest - mid.astype(F32)).astype(BF16)


def log2(n):
    assert n & (n - 1) == 0
    return n.bit_length() - 1


def basis_rows(state):
    return jnp.concatenate([state, (state * state - 1.0) * ROOT_HALF], axis=0)


def pick(core, first, second):
    return jnp.where(core == 0, first, second)


def states_of(ref, factors):
    state = ref[:factors, :]
    return state, 0.8 * state + 0.6 * ref[factors : 2 * factors, :]


def weights_of(ref, factors):
    return ref[2 * factors : 2 * factors + 1, :]


def pack_kernel(counts_ref, start_ref, shocks_ref, weights_ref, short_ref, whole_ref):
    factors, paths = start_ref.shape
    filled = counts_ref[lax.axis_index("trade")].astype(F32)
    spare = lax.broadcasted_iota(jnp.int32, (PAD, paths), 0) > 0
    for ref in (short_ref, whole_ref):
        ref[:factors, :] = start_ref[...]
        ref[factors : 2 * factors, :] = shocks_ref[0]
        ref[2 * factors : 2 * factors + PAD, :] = jnp.where(spare, filled, weights_ref[...].astype(F32))
    whole_ref[2 * factors + PAD :, :] = shocks_ref[1]


def prepare(number, start, shocks, weight_row, states_scr, wide_scr):
    core = lax.axis_index("path") & 1
    factors, paths = start.shape
    mine = pl.ds(number * paths, paths)
    second = 0.8 * start + 0.6 * shocks[0]
    third = 0.8 * second + 0.6 * shocks[1]
    hi, lo = split2(basis_rows(pick(core, start, second)) * weight_row)
    wide_scr[:, mine] = jnp.concatenate([hi, lo], axis=0)
    hi, mid, low = split3(pick(core, second, third))
    hi, mid, low = hi.astype(F32), mid.astype(F32), low.astype(F32)
    ones = jnp.where(lax.broadcasted_iota(jnp.int32, (DEPTH - 6 * factors, paths), 0) < 3, 1.0, 0.0)
    stacked = jnp.concatenate([hi, hi, mid, mid, hi, low, ones], axis=0)
    states_scr[mine, :] = stacked.T.astype(BF16)


def load_rows(cols, load_ref, strike_ref, load_scr, slot):
    factors = load_ref.shape[0]
    hi, mid, low = split3(load_ref[:, cols])
    for part, piece in enumerate((hi, mid, hi, mid, low, hi)):
        load_scr[slot, pl.ds(part * factors, factors), :] = piece
    s_hi, s_mid, s_low = split3(-strike_ref[:, cols])
    rows = lax.broadcasted_iota(jnp.int32, (16, TILE), 0)
    strike_rows = jnp.where(rows == 1, s_mid.astype(F32), jnp.where(rows == 2, s_low.astype(F32), 0.0))
    strike_rows = jnp.where(rows == 0, s_hi.astype(F32), strike_rows)
    load_scr[slot, pl.ds(6 * factors, 16), :] = strike_rows.astype(BF16)


def chunk_moments(pay, rows, wide_scr):
    wide = wide_scr.shape[0] // 2
    hi, lo = split2(jnp.maximum(pay, 0.0))
    both = mm(wide_scr[:, rows], hi)
    return both[:wide] + (both[wide:] + mm(wide_scr[:wide, rows], lo))


def tile_at(index):
    return pl.ds(pl.multiple_of(index * TILE, TILE), TILE)


def copies(sources, targets, sems):
    return [pltpu.make_async_copy(src, dst, sems.at[i]) for i, (src, dst) in enumerate(zip(sources, targets))]


def moment_kernel(
    groups, start_ref, shocks_ref, weights_ref, other_ref, load_hbm, strike_hbm, notional_hbm, set_hbm, *refs
):
    outs = refs[:groups]
    *staged, sems, net_scr, states_scr, wide_scr, load_scr = refs[groups:]
    load_ref, strike_ref, notional_ref, set_ref = staged
    moves = copies((load_hbm, strike_hbm, notional_hbm, set_hbm), staged, sems)
    for move in moves:
        move.start()
    group = lax.axis_index("trade")
    factors = load_ref.shape[0]
    filled = other_ref[2 * factors + 1 : 2 * factors + 2, :1].astype(jnp.int32)
    owned = net_scr.shape[0]
    bits = log2(owned)
    rows = 16
    load_scr[...] = jnp.zeros_like(load_scr)
    net_scr[...] = jnp.zeros_like(net_scr)
    prepare(0, start_ref[...], shocks_ref[...], weights_ref[...].astype(F32), states_scr, wide_scr)
    shocks = (other_ref[factors : 2 * factors, :], other_ref[2 * factors + PAD :, :])
    prepare(1, other_ref[:factors, :], shocks, weights_of(other_ref, factors), states_scr, wide_scr)
    for move in moves:
        move.wait()

    chunks = [pl.ds(start, CHUNK) for start in range(0, states_scr.shape[0], CHUNK)]

    def add_tile(index, moment):
        cols = tile_at(index)
        slot_ids = index * TILE + lax.broadcasted_iota(jnp.int32, (1, TILE), 1)
        hi, lo = split2(moment * jnp.where(slot_ids < filled, notional_ref[:, cols], 0.0))
        both = jnp.concatenate([hi, lo], axis=0)
        both = both.reshape(both.shape[0] // rows, rows, TILE)
        sets = set_ref[:, cols]
        to_group = jnp.broadcast_to((sets >> bits) ^ group, (rows, TILE))
        parts = []
        for away in range(groups):
            mask = jnp.where(to_group == away, 1.0, 0.0).astype(BF16)
            parts.append((both * mask[None]).reshape(-1, TILE))
        one_hot = lax.broadcasted_iota(jnp.int32, (owned, TILE), 0) == (sets & (owned - 1))
        one_hot = jnp.where(one_hot, 1.0, 0.0).astype(BF16)
        net_scr[...] += mm(one_hot, jnp.concatenate(parts, axis=0), NT)

    def step(turn, carry):
        stages = [(slot, chunk) for slot in range(SLOTS) for chunk in chunks]
        pays, moment = {}, None
        for number in range(len(stages) + 1):
            if number < len(stages):
                slot, chunk = stages[number]
                if number % len(chunks) == 0:
                    load_rows(tile_at(SLOTS * turn + slot), load_ref, strike_ref, load_scr, slot)
                pays[number] = mm(states_scr[chunk, :], load_scr[slot])
            if number > 0:
                slot, chunk = stages[number - 1]
                part = chunk_moments(pays.pop(number - 1), chunk, wide_scr)
                moment = part if moment is None else moment + part
                if number % len(chunks) == 0:
                    add_tile(SLOTS * turn + slot, moment)
                    moment = None
        return carry

    lax.fori_loop(0, load_ref.shape[1] // (SLOTS * TILE), step, 0)
    wide = net_scr.shape[1] // (2 * groups)
    half = owned // 2
    for away, out in enumerate(outs):
        net = net_scr[:, 2 * wide * away : 2 * wide * (away + 1)]
        net = net[:, :wide] + net[:, wide:]
        out[...] = jnp.concatenate([net[:half], net[half:]], axis=1)


def eliminate(mat, pivots):
    sub = lax.broadcasted_iota(jnp.int32, mat.shape, 0)
    lane = lax.broadcasted_iota(jnp.int32, mat.shape, 1)
    for k in pivots:
        row = mat[k : k + 1, :]
        col = mat[:, k : k + 1]
        pivot = 1.0 / mat[k : k + 1, k : k + 1]
        row = jnp.where(lane[:1] == k, 1.0, row) * pivot
        mat = jnp.where(sub == k, row, jnp.where(lane == k, 0.0, mat) - col * row)
    return mat


def gram_kernel(factors, *refs):
    *blocks, thresholds_ref, gram_ref, mat_ref, limits_ref = refs
    limits = 0.25 * thresholds_ref[...].astype(F32)
    limits_ref[...] = jnp.broadcast_to(limits, (limits_ref.shape[1], limits.shape[1])).T
    core = lax.axis_index("path") & 1
    wide = 2 * factors
    gram = jnp.zeros((wide, wide), F32)
    for block in path_blocks(blocks):
        basis = basis_rows(pick(core, *states_of(block, factors)))
        gram = gram + mm_full(basis * weights_of(block, factors), basis, NT)
    gram_ref[...] = gram
    mat_ref[...] = eliminate(gram, range(FIRST_PIVOTS))


def inverse_kernel(gram_ref, mat_ref, inverse_ref):
    gram = gram_ref[...]
    wide = gram.shape[0]
    mat = eliminate(mat_ref[...], range(FIRST_PIVOTS, wide))
    sub = lax.broadcasted_iota(jnp.int32, (wide, wide), 0)
    lane = lax.broadcasted_iota(jnp.int32, (wide, wide), 1)
    mat = mat + mm_full(mat, jnp.where(sub == lane, 1.0, 0.0) - mm_full(gram, mat))
    zero = jnp.zeros_like(mat)
    upper = jnp.concatenate([mat, zero], axis=1)
    inverse_ref[...] = jnp.concatenate([upper, jnp.concatenate([zero, mat], axis=1)], axis=0)


def path_blocks(refs):
    for ref in refs:
        if len(ref.shape) == 2:
            yield ref
        else:
            for index in range(ref.shape[0]):
                yield ref.at[index]


def sum_kernel(*refs):
    total = refs[0][...]
    for ref in refs[1:-1]:
        total = total + ref[...]
    refs[-1][...] = total


def coeff_kernel(*refs):
    total = refs[0][...]
    for ref in refs[1:-2]:
        total = total + ref[...]
    refs[-1][...] = mm_full(total, refs[-2][...])


def exposure_kernel(factors, own, coeff_ref, limits_ref, *refs):
    date = (lax.axis_index("path") & 1) ^ (0 if own else 1)
    *blocks, exposure_hbm, expected_ref, value_scr, sem = refs
    if not own:
        *blocks, first_ref, _ = blocks
    wide = 2 * factors
    paths = blocks[0].shape[1]
    limits = limits_ref[:, :1]
    packed = coeff_ref[...]
    hi, lo = split2(jnp.concatenate([packed[:, :wide], packed[:, wide:]], axis=0))
    coeffs = jnp.concatenate([hi, hi, lo], axis=1)
    move = pltpu.make_async_copy(value_scr, exposure_hbm.at[date], sem)
    sums = jnp.zeros((limits.shape[0], 128), F32)
    total = jnp.zeros((1, 1), F32)
    for number, block in enumerate(path_blocks(blocks)):
        weight_row = weights_of(block, factors)
        total = total + jnp.sum(weight_row, keepdims=True)
        hi, lo = split2(basis_rows(pick(date, *states_of(block, factors))))
        value = jnp.maximum(mm(coeffs, jnp.concatenate([hi, lo, hi], axis=0)) - limits, 0.0)
        if number == 0:
            value_scr[...] = value
            move.start()
        product = value * weight_row
        for c in range(paths // 128):
            sums = sums + product[:, c * 128 : (c + 1) * 128]
    mine = jnp.sum(sums.T, axis=0, keepdims=True) / total
    if own:
        expected_ref[...] = mine
    else:
        other = first_ref[...]
        expected_ref[...] = jnp.concatenate([pick(date, mine, other), pick(date, other, mine)], axis=0)
    move.wait()


def swap(x, axis, away):
    return lax.ppermute(x, axis, [(i, i ^ away) for i in range(lax.axis_size(axis))])


def run(kernel, name, out, specs, args, mib, scratch=(), gflops=0.0, out_specs=None, aliases=None):
    return pl.pallas_call(
        kernel,
        out_shape=out,
        in_specs=specs,
        out_specs=out_specs or jax.tree.map(lambda _: VMEM, out),
        input_output_aliases=aliases or {},
        scratch_shapes=list(scratch),
        compiler_params=pltpu.CompilerParams(vmem_limit_bytes=int(mib * MIB)),
        cost_estimate=pl.CostEstimate(flops=int(gflops * 1e9), bytes_accessed=10**5, transcendentals=0),
        name=name,
    )(*args)


def body(
    start_state, shocks, loadings, strikes, notionals, trade_set, live_counts, weights, thresholds
):
    paths, factors = start_state.shape
    dates = shocks.shape[0]
    slots = loadings.shape[1]
    owned = thresholds.shape[0]
    groups = lax.axis_size("trade")
    ranks = lax.axis_size("path")
    wide = 2 * factors
    assert dates == 2

    shape = jax.ShapeDtypeStruct
    start_t, shocks_t, weights_row = start_state.T, jnp.swapaxes(shocks, 1, 2), weights[None, :]
    short, whole = run(
        pack_kernel, "pack_states",
        [shape(((dates - 1) * factors + factors + PAD, paths), F32), shape(((dates + 1) * factors + PAD, paths), F32)],
        [SMEM] + [VMEM] * 3, (live_counts, start_t, shocks_t, weights_row), 58, (), 20.0,
    )
    other = swap(whole, "path", 1)
    across = [swap(short, "path", 2 * away) for away in range(1, ranks // 2)]

    strike_row, notional_row, set_row = strikes[None, :], notionals[None, :], trade_set[None, :]
    nets = run(
        functools.partial(moment_kernel, groups), "net_moments",
        [shape((owned // 2, 2 * wide), F32)] * groups, [VMEM] * 4 + [HBM] * 4,
        (start_t, shocks_t, weights_row, other, loadings, strike_row, notional_row, set_row), 52.75,
        [
            pltpu.VMEM((factors, slots), F32),
            pltpu.VMEM((1, slots), F32),
            pltpu.VMEM((1, slots), F32),
            pltpu.VMEM((1, slots), jnp.int32),
            pltpu.SemaphoreType.DMA((4,)),
            pltpu.VMEM((owned, 2 * wide * groups), F32),
            pltpu.VMEM((2 * paths, DEPTH), BF16),
            pltpu.VMEM((2 * wide, 2 * paths), BF16),
            pltpu.VMEM((SLOTS, DEPTH, TILE), BF16),
        ],
        20.0,
    )
    *across, net = lax.optimization_barrier((*across, nets[0]))
    others = swap(jnp.stack(across), "path", 1)
    got = [swap(nets[away], "trade", away) for away in range(1, groups)]
    blocks = (short, other, *across, others)
    gram, mat, limits = run(
        functools.partial(gram_kernel, factors), "gram_first_pivots",
        [shape((wide, wide), F32)] * 2 + [shape((owned, 128), F32)],
        [VMEM] * (len(blocks) + 1), (*blocks, thresholds[None, :]), 8, (), 5.0,
    )
    mat, net = lax.optimization_barrier((mat, net))
    inverse = run(
        inverse_kernel, "gram_inverse", shape((2 * wide, 2 * wide), F32), [VMEM] * 2, (gram, mat), 8, (), 3.0
    )
    part = run(
        sum_kernel, "group_sum", shape((owned // 2, 2 * wide), F32), [VMEM] * groups, [net] + got, 4
    )
    got = [swap(part, "path", 2 * away) for away in range(1, ranks // 2)]
    mine = run(
        coeff_kernel, "set_coeffs", shape((owned // 2, 2 * wide), F32), [VMEM] * (ranks // 2 + 1),
        [part] + got + [inverse], 4,
    )
    partner = swap(mine, "path", 1)
    scratch = [pltpu.VMEM((owned, paths), F32), pltpu.SemaphoreType.DMA]
    exposure, first = run(
        functools.partial(exposure_kernel, factors, True), "own_date_exposure",
        (shape((dates, owned, paths), F32), shape((1, owned), F32)), [VMEM] * (2 + len(blocks)),
        (mine, limits, *blocks), 16, scratch, 2.0, (HBM, VMEM),
    )
    exposure, expected = run(
        functools.partial(exposure_kernel, factors, False), "other_date_exposure",
        (shape((dates, owned, paths), F32), shape((dates, owned), F32)), [VMEM] * (3 + len(blocks)) + [HBM],
        (partner, limits, *blocks, first, exposure), 16, scratch, 2.0, (HBM, VMEM), {3 + len(blocks): 0},
    )
    return (exposure, expected)


def solution(mesh):
    placed = (
        P("path", None),
        P(None, "path", None),
        P(None, "trade"),
        P("trade"),
        P("trade"),
        P("trade"),
        P(),
        P("path"),
        P("trade"),
    )
    return jax.shard_map(
        body,
        mesh=mesh,
        in_specs=placed,
        out_specs=(P(None, "trade", "path"), P(None, "trade")),
        check_vma=False,
    )
```

```python
import functools

import jax
import jax.numpy as jnp
from jax import lax
from jax.experimental import pallas as pl
from jax.experimental.pallas import tpu as pltpu
from jax.sharding import PartitionSpec as P

HIGHEST_PREC = lax.Precision.HIGHEST
ROOT_HALF = 0.7071067811865476
F32 = jnp.float32
BF16 = jnp.bfloat16
TILE = 512
CHUNK = 512
SLOTS = 4
FIRST_PIVOTS = 36
DEPTH = 256
PAD = 8
MIB = 1024 * 1024
NN = (((1,), (0,)), ((), ()))
NT = (((1,), (1,)), ((), ()))
VMEM = pl.BlockSpec(memory_space=pltpu.VMEM)
SMEM = pl.BlockSpec(memory_space=pltpu.SMEM)
HBM = pl.BlockSpec(memory_space=pltpu.HBM)


def mm(a, b, dims=NN):
    return lax.dot_general(a, b, dims, preferred_element_type=F32)


def mm_full(a, b, dims=NN):
    return lax.dot_general(a, b, dims, preferred_element_type=F32, precision=HIGHEST_PREC)


def split2(x):
    hi = x.astype(BF16)
    return hi, (x - hi.astype(F32)).astype(BF16)


def split3(x):
    hi = x.astype(BF16)
    rest = x - hi.astype(F32)
    mid = rest.astype(BF16)
    return hi, mid, (rest - mid.astype(F32)).astype(BF16)


def log2(n):
    assert n & (n - 1) == 0
    return n.bit_length() - 1


def basis_rows(state):
    return jnp.concatenate([state, (state * state - 1.0) * ROOT_HALF], axis=0)


def pick(core, first, second):
    return jnp.where(core == 0, first, second)


def states_of(ref, factors):
    state = ref[:factors, :]
    return state, 0.8 * state + 0.6 * ref[factors : 2 * factors, :]


def weights_of(ref, factors):
    return ref[2 * factors : 2 * factors + 1, :]


def pack_kernel(counts_ref, start_ref, shocks_ref, weights_ref, short_ref, whole_ref):
    factors, paths = start_ref.shape
    filled = counts_ref[lax.axis_index("trade")].astype(F32)
    spare = lax.broadcasted_iota(jnp.int32, (PAD, paths), 0) > 0
    for ref in (short_ref, whole_ref):
        ref[:factors, :] = start_ref[...]
        ref[factors : 2 * factors, :] = shocks_ref[0]
        ref[2 * factors : 2 * factors + PAD, :] = jnp.where(spare, filled, weights_ref[...].astype(F32))
    whole_ref[2 * factors + PAD :, :] = shocks_ref[1]


def prepare(number, start, shocks, weight_row, states_scr, wide_scr):
    core = lax.axis_index("path") & 1
    factors, paths = start.shape
    mine = pl.ds(number * paths, paths)
    second = 0.8 * start + 0.6 * shocks[0]
    third = 0.8 * second + 0.6 * shocks[1]
    hi, lo = split2(basis_rows(pick(core, start, second)) * weight_row)
    wide_scr[:, mine] = jnp.concatenate([hi, lo], axis=0)
    hi, mid, low = split3(pick(core, second, third))
    hi, mid, low = hi.astype(F32), mid.astype(F32), low.astype(F32)
    ones = jnp.where(lax.broadcasted_iota(jnp.int32, (DEPTH - 6 * factors, paths), 0) < 3, 1.0, 0.0)
    stacked = jnp.concatenate([hi, hi, mid, mid, hi, low, ones], axis=0)
    states_scr[mine, :] = stacked.T.astype(BF16)


def load_rows(cols, load_ref, strike_ref, load_scr, slot):
    factors = load_ref.shape[0]
    hi, mid, low = split3(load_ref[:, cols])
    for part, piece in enumerate((hi, mid, hi, mid, low, hi)):
        load_scr[slot, pl.ds(part * factors, factors), :] = piece
    s_hi, s_mid, s_low = split3(-strike_ref[:, cols])
    rows = lax.broadcasted_iota(jnp.int32, (16, TILE), 0)
    strike_rows = jnp.where(rows == 1, s_mid.astype(F32), jnp.where(rows == 2, s_low.astype(F32), 0.0))
    strike_rows = jnp.where(rows == 0, s_hi.astype(F32), strike_rows)
    load_scr[slot, pl.ds(6 * factors, 16), :] = strike_rows.astype(BF16)


def chunk_moments(pay, rows, wide_scr):
    wide = wide_scr.shape[0] // 2
    hi, lo = split2(jnp.maximum(pay, 0.0))
    both = mm(wide_scr[:, rows], hi)
    return both[:wide] + (both[wide:] + mm(wide_scr[:wide, rows], lo))


def tile_at(index):
    return pl.ds(pl.multiple_of(index * TILE, TILE), TILE)


def copies(sources, targets, sems):
    return [pltpu.make_async_copy(src, dst, sems.at[i]) for i, (src, dst) in enumerate(zip(sources, targets))]


def moment_kernel(
    groups, start_ref, shocks_ref, weights_ref, other_ref, load_hbm, strike_hbm, notional_hbm, set_hbm, *refs
):
    outs = refs[:groups]
    *staged, sems, net_scr, states_scr, wide_scr, load_scr = refs[groups:]
    load_ref, strike_ref, notional_ref, set_ref = staged
    moves = copies((load_hbm, strike_hbm, notional_hbm, set_hbm), staged, sems)
    for move in moves:
        move.start()
    group = lax.axis_index("trade")
    factors = load_ref.shape[0]
    filled = other_ref[2 * factors + 1 : 2 * factors + 2, :1].astype(jnp.int32)
    owned = net_scr.shape[0]
    bits = log2(owned)
    rows = 16
    load_scr[...] = jnp.zeros_like(load_scr)
    net_scr[...] = jnp.zeros_like(net_scr)
    prepare(0, start_ref[...], shocks_ref[...], weights_ref[...].astype(F32), states_scr, wide_scr)
    shocks = (other_ref[factors : 2 * factors, :], other_ref[2 * factors + PAD :, :])
    prepare(1, other_ref[:factors, :], shocks, weights_of(other_ref, factors), states_scr, wide_scr)
    for move in moves:
        move.wait()

    chunks = [pl.ds(start, CHUNK) for start in range(0, states_scr.shape[0], CHUNK)]

    def add_tile(index, moment):
        cols = tile_at(index)
        slot_ids = index * TILE + lax.broadcasted_iota(jnp.int32, (1, TILE), 1)
        hi, lo = split2(moment * jnp.where(slot_ids < filled, notional_ref[:, cols], 0.0))
        both = jnp.concatenate([hi, lo], axis=0)
        both = both.reshape(both.shape[0] // rows, rows, TILE)
        sets = set_ref[:, cols]
        to_group = jnp.broadcast_to((sets >> bits) ^ group, (rows, TILE))
        parts = []
        for away in range(groups):
            mask = jnp.where(to_group == away, 1.0, 0.0).astype(BF16)
            parts.append((both * mask[None]).reshape(-1, TILE))
        one_hot = lax.broadcasted_iota(jnp.int32, (owned, TILE), 0) == (sets & (owned - 1))
        one_hot = jnp.where(one_hot, 1.0, 0.0).astype(BF16)
        net_scr[...] += mm(one_hot, jnp.concatenate(parts, axis=0), NT)

    def step(turn, carry):
        stages = [(slot, chunk) for slot in range(SLOTS) for chunk in chunks]
        pays, moment = {}, None
        for number in range(len(stages) + 1):
            if number < len(stages):
                slot, chunk = stages[number]
                if number % len(chunks) == 0:
                    load_rows(tile_at(SLOTS * turn + slot), load_ref, strike_ref, load_scr, slot)
                pays[number] = mm(states_scr[chunk, :], load_scr[slot])
            if number > 0:
                slot, chunk = stages[number - 1]
                part = chunk_moments(pays.pop(number - 1), chunk, wide_scr)
                moment = part if moment is None else moment + part
                if number % len(chunks) == 0:
                    add_tile(SLOTS * turn + slot, moment)
                    moment = None
        return carry

    lax.fori_loop(0, (jnp.max(filled) + SLOTS * TILE - 1) // (SLOTS * TILE), step, 0)
    wide = net_scr.shape[1] // (2 * groups)
    half = owned // 2
    for away, out in enumerate(outs):
        net = net_scr[:, 2 * wide * away : 2 * wide * (away + 1)]
        net = net[:, :wide] + net[:, wide:]
        out[...] = jnp.concatenate([net[:half], net[half:]], axis=1)


def eliminate(mat, pivots):
    sub = lax.broadcasted_iota(jnp.int32, mat.shape, 0)
    lane = lax.broadcasted_iota(jnp.int32, mat.shape, 1)
    for k in pivots:
        row = mat[k : k + 1, :]
        col = mat[:, k : k + 1]
        pivot = 1.0 / mat[k : k + 1, k : k + 1]
        row = jnp.where(lane[:1] == k, 1.0, row) * pivot
        mat = jnp.where(sub == k, row, jnp.where(lane == k, 0.0, mat) - col * row)
    return mat


def gram_kernel(factors, *refs):
    *blocks, thresholds_ref, gram_ref, mat_ref, limits_ref = refs
    limits = 0.25 * thresholds_ref[...].astype(F32)
    limits_ref[...] = jnp.broadcast_to(limits, (limits_ref.shape[1], limits.shape[1])).T
    core = lax.axis_index("path") & 1
    wide = 2 * factors
    gram = jnp.zeros((wide, wide), F32)
    for block in path_blocks(blocks):
        basis = basis_rows(pick(core, *states_of(block, factors)))
        gram = gram + mm_full(basis * weights_of(block, factors), basis, NT)
    gram_ref[...] = gram
    mat_ref[...] = eliminate(gram, range(FIRST_PIVOTS))


def inverse_kernel(gram_ref, mat_ref, inverse_ref):
    gram = gram_ref[...]
    wide = gram.shape[0]
    mat = eliminate(mat_ref[...], range(FIRST_PIVOTS, wide))
    sub = lax.broadcasted_iota(jnp.int32, (wide, wide), 0)
    lane = lax.broadcasted_iota(jnp.int32, (wide, wide), 1)
    mat = mat + mm_full(mat, jnp.where(sub == lane, 1.0, 0.0) - mm_full(gram, mat))
    zero = jnp.zeros_like(mat)
    upper = jnp.concatenate([mat, zero], axis=1)
    inverse_ref[...] = jnp.concatenate([upper, jnp.concatenate([zero, mat], axis=1)], axis=0)


def path_blocks(refs):
    for ref in refs:
        if len(ref.shape) == 2:
            yield ref
        else:
            for index in range(ref.shape[0]):
                yield ref.at[index]


def sum_kernel(*refs):
    total = refs[0][...]
    for ref in refs[1:-1]:
        total = total + ref[...]
    refs[-1][...] = total


def coeff_kernel(*refs):
    total = refs[0][...]
    for ref in refs[1:-2]:
        total = total + ref[...]
    refs[-1][...] = mm_full(total, refs[-2][...])


def exposure_kernel(factors, mine_ref, other_ref, limits_ref, *refs):
    *blocks, exposure_hbm, expected_ref, value_scr, sems = refs
    core = lax.axis_index("path") & 1
    wide = 2 * factors
    paths = blocks[0].shape[1]
    limits = limits_ref[:, :1]
    results, moves = [], []
    total = jnp.zeros((1, 1), F32)
    for block in path_blocks(blocks):
        total = total + jnp.sum(weights_of(block, factors), keepdims=True)
    for turn, ref in enumerate((mine_ref, other_ref)):
        date = core ^ turn
        packed = ref[...]
        hi, lo = split2(jnp.concatenate([packed[:, :wide], packed[:, wide:]], axis=0))
        coeffs = jnp.concatenate([hi, hi, lo], axis=1)
        sums = jnp.zeros((limits.shape[0], 128), F32)
        for number, block in enumerate(path_blocks(blocks)):
            hi, lo = split2(basis_rows(pick(date, *states_of(block, factors))))
            value = jnp.maximum(mm(coeffs, jnp.concatenate([hi, lo, hi], axis=0)) - limits, 0.0)
            if number == 0:
                value_scr[turn] = value
                moves.append(pltpu.make_async_copy(value_scr.at[turn], exposure_hbm.at[date], sems.at[turn]))
                moves[turn].start()
            product = value * weights_of(block, factors)
            for c in range(paths // 128):
                sums = sums + product[:, c * 128 : (c + 1) * 128]
        results.append(jnp.sum(sums.T, axis=0, keepdims=True) / total)
    mine, other = results
    expected_ref[...] = jnp.concatenate([pick(core, mine, other), pick(core, other, mine)], axis=0)
    for move in moves:
        move.wait()


def swap(x, axis, away):
    return lax.ppermute(x, axis, [(i, i ^ away) for i in range(lax.axis_size(axis))])


def run(kernel, name, out, specs, args, mib, scratch=(), gflops=0.0, out_specs=None):
    return pl.pallas_call(
        kernel,
        out_shape=out,
        in_specs=specs,
        out_specs=out_specs or jax.tree.map(lambda _: VMEM, out),
        scratch_shapes=list(scratch),
        compiler_params=pltpu.CompilerParams(vmem_limit_bytes=int(mib * MIB)),
        cost_estimate=pl.CostEstimate(flops=int(gflops * 1e9), bytes_accessed=10**5, transcendentals=0),
        name=name,
    )(*args)


def body(
    start_state, shocks, loadings, strikes, notionals, trade_set, live_counts, weights, thresholds
):
    paths, factors = start_state.shape
    dates = shocks.shape[0]
    slots = loadings.shape[1]
    owned = thresholds.shape[0]
    groups = lax.axis_size("trade")
    ranks = lax.axis_size("path")
    wide = 2 * factors
    assert dates == 2

    shape = jax.ShapeDtypeStruct
    start_t, shocks_t, weights_row = start_state.T, jnp.swapaxes(shocks, 1, 2), weights[None, :]
    short, whole = run(
        pack_kernel, "pack_states",
        [shape(((dates - 1) * factors + factors + PAD, paths), F32), shape(((dates + 1) * factors + PAD, paths), F32)],
        [SMEM] + [VMEM] * 3, (live_counts, start_t, shocks_t, weights_row), 58, (), 20.0,
    )
    other = swap(whole, "path", 1)
    across = [swap(short, "path", 2 * away) for away in range(1, ranks // 2)]

    strike_row, notional_row, set_row = strikes[None, :], notionals[None, :], trade_set[None, :]
    nets = run(
        functools.partial(moment_kernel, groups), "net_moments",
        [shape((owned // 2, 2 * wide), F32)] * groups, [VMEM] * 4 + [HBM] * 4,
        (start_t, shocks_t, weights_row, other, loadings, strike_row, notional_row, set_row), 52.75,
        [
            pltpu.VMEM((factors, slots), F32),
            pltpu.VMEM((1, slots), F32),
            pltpu.VMEM((1, slots), F32),
            pltpu.VMEM((1, slots), jnp.int32),
            pltpu.SemaphoreType.DMA((4,)),
            pltpu.VMEM((owned, 2 * wide * groups), F32),
            pltpu.VMEM((2 * paths, DEPTH), BF16),
            pltpu.VMEM((2 * wide, 2 * paths), BF16),
            pltpu.VMEM((SLOTS, DEPTH, TILE), BF16),
        ],
        20.0,
    )
    *across, net = lax.optimization_barrier((*across, nets[0]))
    others = swap(jnp.stack(across), "path", 1)
    got = [swap(nets[away], "trade", away) for away in range(1, groups)]
    blocks = (short, other, *across, others)
    gram, mat, limits = run(
        functools.partial(gram_kernel, factors), "gram_first_pivots",
        [shape((wide, wide), F32)] * 2 + [shape((owned, 128), F32)],
        [VMEM] * (len(blocks) + 1), (*blocks, thresholds[None, :]), 8, (), 5.0,
    )
    mat, net = lax.optimization_barrier((mat, net))
    inverse = run(
        inverse_kernel, "gram_inverse", shape((2 * wide, 2 * wide), F32), [VMEM] * 2, (gram, mat), 8, (), 3.0
    )
    part = run(
        sum_kernel, "group_sum", shape((owned // 2, 2 * wide), F32), [VMEM] * groups, [net] + got, 4
    )
    got = [swap(part, "path", 2 * away) for away in range(1, ranks // 2)]
    mine = run(
        coeff_kernel, "set_coeffs", shape((owned // 2, 2 * wide), F32), [VMEM] * (ranks // 2 + 1),
        [part] + got + [inverse], 4,
    )
    partner = swap(mine, "path", 1)
    exposure, expected = run(
        functools.partial(exposure_kernel, factors), "set_exposure",
        (shape((dates, owned, paths), F32), shape((dates, owned), F32)), [VMEM] * (3 + len(blocks)),
        (mine, partner, limits, *blocks), 16,
        [pltpu.VMEM((dates, owned, paths), F32), pltpu.SemaphoreType.DMA((dates,))], 2.0, (HBM, VMEM),
    )
    return (exposure, expected)


def solution(mesh):
    placed = (
        P("path", None),
        P(None, "path", None),
        P(None, "trade"),
        P("trade"),
        P("trade"),
        P("trade"),
        P(),
        P("path"),
        P("trade"),
    )
    return jax.shard_map(
        body,
        mesh=mesh,
        in_specs=placed,
        out_specs=(P(None, "trade", "path"), P(None, "trade")),
        check_vma=False,
    )
```

```python
import functools

import jax
import jax.numpy as jnp
from jax import lax
from jax.experimental import pallas as pl
from jax.experimental.pallas import tpu as pltpu
from jax.sharding import PartitionSpec as P

HIGHEST_PREC = lax.Precision.HIGHEST
ROOT_HALF = 0.7071067811865476
F32 = jnp.float32
BF16 = jnp.bfloat16
TILE = 512
CHUNK = 1024
SLOTS = 4
FIRST_PIVOTS = 36
DEPTH = 256
PAD = 8
MIB = 1024 * 1024
NN = (((1,), (0,)), ((), ()))
NT = (((1,), (1,)), ((), ()))
VMEM = pl.BlockSpec(memory_space=pltpu.VMEM)
SMEM = pl.BlockSpec(memory_space=pltpu.SMEM)
HBM = pl.BlockSpec(memory_space=pltpu.HBM)


def mm(a, b, dims=NN):
    return lax.dot_general(a, b, dims, preferred_element_type=F32)


def mm_full(a, b, dims=NN):
    return lax.dot_general(a, b, dims, preferred_element_type=F32, precision=HIGHEST_PREC)


def split2(x):
    hi = x.astype(BF16)
    return hi, (x - hi.astype(F32)).astype(BF16)


def split3(x):
    hi = x.astype(BF16)
    rest = x - hi.astype(F32)
    mid = rest.astype(BF16)
    return hi, mid, (rest - mid.astype(F32)).astype(BF16)


def log2(n):
    assert n & (n - 1) == 0
    return n.bit_length() - 1


def basis_rows(state):
    return jnp.concatenate([state, (state * state - 1.0) * ROOT_HALF], axis=0)


def pick(core, first, second):
    return jnp.where(core == 0, first, second)


def states_of(ref, factors):
    state = ref[:factors, :]
    return state, 0.8 * state + 0.6 * ref[factors : 2 * factors, :]


def weights_of(ref, factors):
    return ref[2 * factors : 2 * factors + 1, :]


def pack_kernel(counts_ref, start_ref, shocks_ref, weights_ref, short_ref, whole_ref):
    factors, paths = start_ref.shape
    filled = counts_ref[lax.axis_index("trade")].astype(F32)
    spare = lax.broadcasted_iota(jnp.int32, (PAD, paths), 0) > 0
    for ref in (short_ref, whole_ref):
        ref[:factors, :] = start_ref[...]
        ref[factors : 2 * factors, :] = shocks_ref[0]
        ref[2 * factors : 2 * factors + PAD, :] = jnp.where(spare, filled, weights_ref[...].astype(F32))
    whole_ref[2 * factors + PAD :, :] = shocks_ref[1]


def prepare(number, start, shocks, weight_row, states_scr, wide_scr):
    core = lax.axis_index("path") & 1
    factors, paths = start.shape
    mine = pl.ds(number * paths, paths)
    second = 0.8 * start + 0.6 * shocks[0]
    third = 0.8 * second + 0.6 * shocks[1]
    hi, lo = split2(basis_rows(pick(core, start, second)) * weight_row)
    wide_scr[:, mine] = jnp.concatenate([hi, lo], axis=0)
    hi, mid, low = split3(pick(core, second, third))
    hi, mid, low = hi.astype(F32), mid.astype(F32), low.astype(F32)
    ones = jnp.where(lax.broadcasted_iota(jnp.int32, (DEPTH - 6 * factors, paths), 0) < 3, 1.0, 0.0)
    stacked = jnp.concatenate([hi, hi, mid, mid, hi, low, ones], axis=0)
    states_scr[mine, :] = stacked.T.astype(BF16)


def load_rows(cols, load_ref, strike_ref, load_scr, slot):
    factors = load_ref.shape[0]
    hi, mid, low = split3(load_ref[:, cols])
    for part, piece in enumerate((hi, mid, hi, mid, low, hi)):
        load_scr[slot, pl.ds(part * factors, factors), :] = piece
    s_hi, s_mid, s_low = split3(-strike_ref[:, cols])
    rows = lax.broadcasted_iota(jnp.int32, (16, TILE), 0)
    strike_rows = jnp.where(rows == 1, s_mid.astype(F32), jnp.where(rows == 2, s_low.astype(F32), 0.0))
    strike_rows = jnp.where(rows == 0, s_hi.astype(F32), strike_rows)
    load_scr[slot, pl.ds(6 * factors, 16), :] = strike_rows.astype(BF16)


def chunk_moments(pay, rows, wide_scr):
    wide = wide_scr.shape[0] // 2
    hi, lo = split2(jnp.maximum(pay, 0.0))
    both = mm(wide_scr[:, rows], hi)
    return both[:wide] + (both[wide:] + mm(wide_scr[:wide, rows], lo))


def tile_at(index):
    return pl.ds(pl.multiple_of(index * TILE, TILE), TILE)


def copies(sources, targets, sems):
    return [pltpu.make_async_copy(src, dst, sems.at[i]) for i, (src, dst) in enumerate(zip(sources, targets))]


def moment_kernel(
    groups, start_ref, shocks_ref, weights_ref, other_ref, load_hbm, strike_hbm, notional_hbm, set_hbm, *refs
):
    outs = refs[:groups]
    *staged, sems, net_scr, states_scr, wide_scr, load_scr, part_scr, hot_scr = refs[groups:]
    load_ref, strike_ref, notional_ref, set_ref = staged
    moves = copies((load_hbm, strike_hbm, notional_hbm, set_hbm), staged, sems)
    for move in moves:
        move.start()
    group = lax.axis_index("trade")
    factors = load_ref.shape[0]
    filled = other_ref[2 * factors + 1 : 2 * factors + 2, :1].astype(jnp.int32)
    owned = net_scr.shape[0]
    bits = log2(owned)
    rows = 16
    load_scr[...] = jnp.zeros_like(load_scr)
    for ref in (net_scr, part_scr, hot_scr):
        ref[...] = jnp.zeros_like(ref)
    prepare(0, start_ref[...], shocks_ref[...], weights_ref[...].astype(F32), states_scr, wide_scr)
    shocks = (other_ref[factors : 2 * factors, :], other_ref[2 * factors + PAD :, :])
    prepare(1, other_ref[:factors, :], shocks, weights_of(other_ref, factors), states_scr, wide_scr)
    for move in moves:
        move.wait()

    chunks = [pl.ds(start, CHUNK) for start in range(0, states_scr.shape[0], CHUNK)]

    def keep_tile(index, slot, moment):
        cols = tile_at(index)
        slot_ids = index * TILE + lax.broadcasted_iota(jnp.int32, (1, TILE), 1)
        hi, lo = split2(moment * jnp.where(slot_ids < filled, notional_ref[:, cols], 0.0))
        both = jnp.concatenate([hi, lo], axis=0)
        both = both.reshape(both.shape[0] // rows, rows, TILE)
        sets = set_ref[:, cols]
        to_group = jnp.broadcast_to((sets >> bits) ^ group, (rows, TILE))
        place = slice(slot * TILE, (slot + 1) * TILE)
        for away in range(groups):
            mask = jnp.where(to_group == away, 1.0, 0.0).astype(BF16)
            size = both.shape[0] * rows
            part_scr[away * size : (away + 1) * size, place] = (both * mask[None]).reshape(-1, TILE)
        one_hot = lax.broadcasted_iota(jnp.int32, (owned, TILE), 0) == (sets & (owned - 1))
        hot_scr[:, place] = jnp.where(one_hot, 1.0, 0.0).astype(BF16)

    def add_tiles():
        net_scr[...] += mm(hot_scr[...], part_scr[...], NT)

    def step(turn, carry):
        add_tiles()
        stages = [(slot, chunk) for slot in range(SLOTS) for chunk in chunks]
        pays, moment = {}, None
        for number in range(len(stages) + 1):
            if number < len(stages):
                slot, chunk = stages[number]
                if number % len(chunks) == 0:
                    load_rows(tile_at(SLOTS * turn + slot), load_ref, strike_ref, load_scr, slot)
                pays[number] = mm(states_scr[chunk, :], load_scr[slot])
            if number > 0:
                slot, chunk = stages[number - 1]
                part = chunk_moments(pays.pop(number - 1), chunk, wide_scr)
                moment = part if moment is None else moment + part
                if number % len(chunks) == 0:
                    keep_tile(SLOTS * turn + slot, slot, moment)
                    moment = None
        return carry

    lax.fori_loop(0, (jnp.max(filled) + SLOTS * TILE - 1) // (SLOTS * TILE), step, 0)
    add_tiles()
    wide = net_scr.shape[1] // (2 * groups)
    half = owned // 2
    for away, out in enumerate(outs):
        net = net_scr[:, 2 * wide * away : 2 * wide * (away + 1)]
        net = net[:, :wide] + net[:, wide:]
        out[...] = jnp.concatenate([net[:half], net[half:]], axis=1)


def eliminate(mat, pivots):
    sub = lax.broadcasted_iota(jnp.int32, mat.shape, 0)
    lane = lax.broadcasted_iota(jnp.int32, mat.shape, 1)
    for k in pivots:
        row = mat[k : k + 1, :]
        col = mat[:, k : k + 1]
        pivot = 1.0 / mat[k : k + 1, k : k + 1]
        row = jnp.where(lane[:1] == k, 1.0, row) * pivot
        mat = jnp.where(sub == k, row, jnp.where(lane == k, 0.0, mat) - col * row)
    return mat


def gram_kernel(factors, *refs):
    *blocks, thresholds_ref, gram_ref, mat_ref, limits_ref = refs
    limits = 0.25 * thresholds_ref[...].astype(F32)
    limits_ref[...] = jnp.broadcast_to(limits, (limits_ref.shape[1], limits.shape[1])).T
    core = lax.axis_index("path") & 1
    wide = 2 * factors
    gram = jnp.zeros((wide, wide), F32)
    for block in path_blocks(blocks):
        basis = basis_rows(pick(core, *states_of(block, factors)))
        gram = gram + mm_full(basis * weights_of(block, factors), basis, NT)
    gram_ref[...] = gram
    mat_ref[...] = eliminate(gram, range(FIRST_PIVOTS))


def inverse_kernel(gram_ref, mat_ref, inverse_ref):
    gram = gram_ref[...]
    wide = gram.shape[0]
    mat = eliminate(mat_ref[...], range(FIRST_PIVOTS, wide))
    sub = lax.broadcasted_iota(jnp.int32, (wide, wide), 0)
    lane = lax.broadcasted_iota(jnp.int32, (wide, wide), 1)
    mat = mat + mm_full(mat, jnp.where(sub == lane, 1.0, 0.0) - mm_full(gram, mat))
    zero = jnp.zeros_like(mat)
    upper = jnp.concatenate([mat, zero], axis=1)
    inverse_ref[...] = jnp.concatenate([upper, jnp.concatenate([zero, mat], axis=1)], axis=0)


def path_blocks(refs):
    for ref in refs:
        if len(ref.shape) == 2:
            yield ref
        else:
            for index in range(ref.shape[0]):
                yield ref.at[index]


def sum_kernel(*refs):
    total = refs[0][...]
    for ref in refs[1:-1]:
        total = total + ref[...]
    refs[-1][...] = total


def coeff_kernel(*refs):
    total = refs[0][...]
    for ref in refs[1:-2]:
        total = total + ref[...]
    refs[-1][...] = mm_full(total, refs[-2][...])


def exposure_kernel(factors, mine_ref, other_ref, limits_ref, *refs):
    *blocks, exposure_hbm, expected_ref, value_scr, sems = refs
    core = lax.axis_index("path") & 1
    wide = 2 * factors
    paths = blocks[0].shape[1]
    limits = limits_ref[:, :1]
    mine, other = mine_ref[...], other_ref[...]
    coeffs = []
    for packed in (pick(core, mine, other), pick(core, other, mine)):
        hi, lo = split2(jnp.concatenate([packed[:, :wide], packed[:, wide:]], axis=0))
        coeffs.append(jnp.concatenate([hi, hi, lo], axis=1))
    sums = [jnp.zeros((limits.shape[0], 128), F32) for _ in coeffs]
    total = jnp.zeros((1, 1), F32)
    moves = []
    for number, block in enumerate(path_blocks(blocks)):
        weight_row = weights_of(block, factors)
        total = total + jnp.sum(weight_row, keepdims=True)
        for date, state in enumerate(states_of(block, factors)):
            hi, lo = split2(basis_rows(state))
            value = jnp.maximum(mm(coeffs[date], jnp.concatenate([hi, lo, hi], axis=0)) - limits, 0.0)
            if number == 0:
                value_scr[date] = value
                moves.append(pltpu.make_async_copy(value_scr.at[date], exposure_hbm.at[date], sems.at[date]))
                moves[date].start()
            product = value * weight_row
            for c in range(paths // 128):
                sums[date] = sums[date] + product[:, c * 128 : (c + 1) * 128]
    for date, partial in enumerate(sums):
        expected_ref[date : date + 1, :] = jnp.sum(partial.T, axis=0, keepdims=True) / total
    for move in moves:
        move.wait()


def swap(x, axis, away):
    return lax.ppermute(x, axis, [(i, i ^ away) for i in range(lax.axis_size(axis))])


def run(kernel, name, out, specs, args, mib, scratch=(), gflops=0.0, out_specs=None):
    return pl.pallas_call(
        kernel,
        out_shape=out,
        in_specs=specs,
        out_specs=out_specs or jax.tree.map(lambda _: VMEM, out),
        scratch_shapes=list(scratch),
        compiler_params=pltpu.CompilerParams(vmem_limit_bytes=int(mib * MIB)),
        cost_estimate=pl.CostEstimate(flops=int(gflops * 1e9), bytes_accessed=10**5, transcendentals=0),
        name=name,
    )(*args)


def body(
    start_state, shocks, loadings, strikes, notionals, trade_set, live_counts, weights, thresholds
):
    paths, factors = start_state.shape
    dates = shocks.shape[0]
    slots = loadings.shape[1]
    owned = thresholds.shape[0]
    groups = lax.axis_size("trade")
    ranks = lax.axis_size("path")
    wide = 2 * factors
    assert dates == 2

    shape = jax.ShapeDtypeStruct
    start_t, shocks_t, weights_row = start_state.T, jnp.swapaxes(shocks, 1, 2), weights[None, :]
    short, whole = run(
        pack_kernel, "pack_states",
        [shape(((dates - 1) * factors + factors + PAD, paths), F32), shape(((dates + 1) * factors + PAD, paths), F32)],
        [SMEM] + [VMEM] * 3, (live_counts, start_t, shocks_t, weights_row), 58, (), 20.0,
    )
    other = swap(whole, "path", 1)
    across = [swap(short, "path", 2 * away) for away in range(1, ranks // 2)]

    strike_row, notional_row, set_row = strikes[None, :], notionals[None, :], trade_set[None, :]
    nets = run(
        functools.partial(moment_kernel, groups), "net_moments",
        [shape((owned // 2, 2 * wide), F32)] * groups, [VMEM] * 4 + [HBM] * 4,
        (start_t, shocks_t, weights_row, other, loadings, strike_row, notional_row, set_row), 52.75,
        [
            pltpu.VMEM((factors, slots), F32),
            pltpu.VMEM((1, slots), F32),
            pltpu.VMEM((1, slots), F32),
            pltpu.VMEM((1, slots), jnp.int32),
            pltpu.SemaphoreType.DMA((4,)),
            pltpu.VMEM((owned, 2 * wide * groups), F32),
            pltpu.VMEM((2 * paths, DEPTH), BF16),
            pltpu.VMEM((2 * wide, 2 * paths), BF16),
            pltpu.VMEM((SLOTS, DEPTH, TILE), BF16),
            pltpu.VMEM((2 * wide * groups, SLOTS * TILE), BF16),
            pltpu.VMEM((owned, SLOTS * TILE), BF16),
        ],
        20.0,
    )
    *across, net = lax.optimization_barrier((*across, nets[0]))
    others = swap(jnp.stack(across), "path", 1)
    got = [swap(nets[away], "trade", away) for away in range(1, groups)]
    blocks = (short, other, *across, others)
    gram, mat, limits = run(
        functools.partial(gram_kernel, factors), "gram_first_pivots",
        [shape((wide, wide), F32)] * 2 + [shape((owned, 128), F32)],
        [VMEM] * (len(blocks) + 1), (*blocks, thresholds[None, :]), 8, (), 5.0,
    )
    mat, net = lax.optimization_barrier((mat, net))
    inverse = run(
        inverse_kernel, "gram_inverse", shape((2 * wide, 2 * wide), F32), [VMEM] * 2, (gram, mat), 8, (), 3.0
    )
    part = run(
        sum_kernel, "group_sum", shape((owned // 2, 2 * wide), F32), [VMEM] * groups, [net] + got, 4
    )
    got = [swap(part, "path", 2 * away) for away in range(1, ranks // 2)]
    mine = run(
        coeff_kernel, "set_coeffs", shape((owned // 2, 2 * wide), F32), [VMEM] * (ranks // 2 + 1),
        [part] + got + [inverse], 4,
    )
    partner = swap(mine, "path", 1)
    exposure, expected = run(
        functools.partial(exposure_kernel, factors), "set_exposure",
        (shape((dates, owned, paths), F32), shape((dates, owned), F32)), [VMEM] * (3 + len(blocks)),
        (mine, partner, limits, *blocks), 16,
        [pltpu.VMEM((dates, owned, paths), F32), pltpu.SemaphoreType.DMA((dates,))], 2.0, (HBM, VMEM),
    )
    return (exposure, expected)


def solution(mesh):
    placed = (
        P("path", None),
        P(None, "path", None),
        P(None, "trade"),
        P("trade"),
        P("trade"),
        P("trade"),
        P(),
        P("path"),
        P("trade"),
    )
    return jax.shard_map(
        body,
        mesh=mesh,
        in_specs=placed,
        out_specs=(P(None, "trade", "path"), P(None, "trade")),
        check_vma=False,
    )
```

```python
import functools

import jax
import jax.numpy as jnp
from jax import lax
from jax.experimental import pallas as pl
from jax.experimental.pallas import tpu as pltpu
from jax.sharding import PartitionSpec as P

HIGHEST_PREC = lax.Precision.HIGHEST
ROOT_HALF = 0.7071067811865476
F32 = jnp.float32
BF16 = jnp.bfloat16
TILE = 512
CHUNK = 1024
SLOTS = 4
FIRST_PIVOTS = 36
DEPTH = 256
PAD = 8
MIB = 1024 * 1024
NN = (((1,), (0,)), ((), ()))
NT = (((1,), (1,)), ((), ()))
VMEM = pl.BlockSpec(memory_space=pltpu.VMEM)
SMEM = pl.BlockSpec(memory_space=pltpu.SMEM)
HBM = pl.BlockSpec(memory_space=pltpu.HBM)


def mm(a, b, dims=NN):
    return lax.dot_general(a, b, dims, preferred_element_type=F32)


def mm_full(a, b, dims=NN):
    return lax.dot_general(a, b, dims, preferred_element_type=F32, precision=HIGHEST_PREC)


def split2(x):
    hi = x.astype(BF16)
    return hi, (x - hi.astype(F32)).astype(BF16)


def split3(x):
    hi = x.astype(BF16)
    rest = x - hi.astype(F32)
    mid = rest.astype(BF16)
    return hi, mid, (rest - mid.astype(F32)).astype(BF16)


def log2(n):
    assert n & (n - 1) == 0
    return n.bit_length() - 1


def basis_rows(state):
    return jnp.concatenate([state, (state * state - 1.0) * ROOT_HALF], axis=0)


def pick(core, first, second):
    return jnp.where(core == 0, first, second)


def states_of(ref, factors):
    state = ref[:factors, :]
    return state, 0.8 * state + 0.6 * ref[factors : 2 * factors, :]


def weights_of(ref, factors):
    return ref[2 * factors : 2 * factors + 1, :]


def pack_kernel(counts_ref, start_ref, shocks_ref, weights_ref, short_ref, whole_ref):
    factors, paths = start_ref.shape
    filled = counts_ref[lax.axis_index("trade")].astype(F32)
    spare = lax.broadcasted_iota(jnp.int32, (PAD, paths), 0) > 0
    for ref in (short_ref, whole_ref):
        ref[:factors, :] = start_ref[...]
        ref[factors : 2 * factors, :] = shocks_ref[0]
        ref[2 * factors : 2 * factors + PAD, :] = jnp.where(spare, filled, weights_ref[...].astype(F32))
    whole_ref[2 * factors + PAD :, :] = shocks_ref[1]


def prepare(number, start, shocks, weight_row, states_scr, wide_scr):
    core = lax.axis_index("path") & 1
    factors, paths = start.shape
    mine = pl.ds(number * paths, paths)
    second = 0.8 * start + 0.6 * shocks[0]
    third = 0.8 * second + 0.6 * shocks[1]
    hi, lo = split2(basis_rows(pick(core, start, second)) * weight_row)
    wide_scr[:, mine] = jnp.concatenate([hi, lo], axis=0)
    hi, mid, low = split3(pick(core, second, third))
    hi, mid, low = hi.astype(F32), mid.astype(F32), low.astype(F32)
    ones = jnp.where(lax.broadcasted_iota(jnp.int32, (DEPTH - 6 * factors, paths), 0) < 3, 1.0, 0.0)
    stacked = jnp.concatenate([hi, hi, mid, mid, hi, low, ones], axis=0)
    states_scr[mine, :] = stacked.T.astype(BF16)


def load_rows(cols, load_ref, strike_ref, load_scr, slot):
    factors = load_ref.shape[0]
    hi, mid, low = split3(load_ref[:, cols])
    for part, piece in enumerate((hi, mid, hi, mid, low, hi)):
        load_scr[slot, pl.ds(part * factors, factors), :] = piece
    s_hi, s_mid, s_low = split3(-strike_ref[:, cols])
    rows = lax.broadcasted_iota(jnp.int32, (16, TILE), 0)
    strike_rows = jnp.where(rows == 1, s_mid.astype(F32), jnp.where(rows == 2, s_low.astype(F32), 0.0))
    strike_rows = jnp.where(rows == 0, s_hi.astype(F32), strike_rows)
    load_scr[slot, pl.ds(6 * factors, 16), :] = strike_rows.astype(BF16)


def chunk_moments(pay, rows, wide_scr):
    wide = wide_scr.shape[0] // 2
    hi, lo = split2(jnp.maximum(pay, 0.0))
    both = mm(wide_scr[:, rows], hi)
    return both[:wide] + (both[wide:] + mm(wide_scr[:wide, rows], lo))


def tile_at(index):
    return pl.ds(pl.multiple_of(index * TILE, TILE), TILE)


def copies(sources, targets, sems):
    return [pltpu.make_async_copy(src, dst, sems.at[i]) for i, (src, dst) in enumerate(zip(sources, targets))]


def moment_kernel(
    groups, start_ref, shocks_ref, weights_ref, other_ref, load_hbm, strike_hbm, notional_hbm, set_hbm, *refs
):
    outs = refs[:groups]
    *staged, sems, net_scr, states_scr, wide_scr, load_scr, part_scr, hot_scr = refs[groups:]
    load_ref, strike_ref, notional_ref, set_ref = staged
    moves = copies((load_hbm, strike_hbm, notional_hbm, set_hbm), staged, sems)
    for move in moves:
        move.start()
    group = lax.axis_index("trade")
    factors = load_ref.shape[0]
    filled = other_ref[2 * factors + 1 : 2 * factors + 2, :1].astype(jnp.int32)
    owned = net_scr.shape[1]
    bits = log2(owned)
    rows = 16
    load_scr[...] = jnp.zeros_like(load_scr)
    for ref in (net_scr, part_scr, hot_scr):
        ref[...] = jnp.zeros_like(ref)
    prepare(0, start_ref[...], shocks_ref[...], weights_ref[...].astype(F32), states_scr, wide_scr)
    shocks = (other_ref[factors : 2 * factors, :], other_ref[2 * factors + PAD :, :])
    prepare(1, other_ref[:factors, :], shocks, weights_of(other_ref, factors), states_scr, wide_scr)
    for move in moves:
        move.wait()

    chunks = [pl.ds(start, CHUNK) for start in range(0, states_scr.shape[0], CHUNK)]

    def keep_tile(index, slot, moment):
        cols = tile_at(index)
        slot_ids = index * TILE + lax.broadcasted_iota(jnp.int32, (1, TILE), 1)
        hi, lo = split2(moment * jnp.where(slot_ids < filled, notional_ref[:, cols], 0.0))
        both = jnp.concatenate([hi, lo], axis=0)
        both = both.reshape(both.shape[0] // rows, rows, TILE)
        sets = set_ref[:, cols]
        to_group = jnp.broadcast_to((sets >> bits) ^ group, (rows, TILE))
        place = slice(slot * TILE, (slot + 1) * TILE)
        for away in range(groups):
            mask = jnp.where(to_group == away, 1.0, 0.0).astype(BF16)
            size = both.shape[0] * rows
            part_scr[away * size : (away + 1) * size, place] = (both * mask[None]).reshape(-1, TILE)
        one_hot = lax.broadcasted_iota(jnp.int32, (owned, TILE), 0) == (sets & (owned - 1))
        hot_scr[:, place] = jnp.where(one_hot, 1.0, 0.0).astype(BF16)

    def add_tiles():
        net_scr[...] += mm(part_scr[...], hot_scr[...], NT)

    def step(turn, carry):
        add_tiles()
        stages = [(slot, chunk) for slot in range(SLOTS) for chunk in chunks]
        pays, moment = {}, None
        for number in range(len(stages) + 1):
            if number < len(stages):
                slot, chunk = stages[number]
                if number % len(chunks) == 0:
                    load_rows(tile_at(SLOTS * turn + slot), load_ref, strike_ref, load_scr, slot)
                pays[number] = mm(states_scr[chunk, :], load_scr[slot])
            if number > 0:
                slot, chunk = stages[number - 1]
                part = chunk_moments(pays.pop(number - 1), chunk, wide_scr)
                moment = part if moment is None else moment + part
                if number % len(chunks) == 0:
                    keep_tile(SLOTS * turn + slot, slot, moment)
                    moment = None
        return carry

    lax.fori_loop(0, (jnp.max(filled) + SLOTS * TILE - 1) // (SLOTS * TILE), step, 0)
    add_tiles()
    wide = net_scr.shape[0] // (2 * groups)
    half = owned // 2
    for away, out in enumerate(outs):
        at = 2 * wide * away
        net = net_scr[at : at + wide, :] + net_scr[at + wide : at + 2 * wide, :]
        out[...] = jnp.concatenate([net[:, :half], net[:, half:]], axis=0).T


def eliminate(mat, pivots):
    sub = lax.broadcasted_iota(jnp.int32, mat.shape, 0)
    lane = lax.broadcasted_iota(jnp.int32, mat.shape, 1)
    for k in pivots:
        row = mat[k : k + 1, :]
        col = mat[:, k : k + 1]
        pivot = 1.0 / mat[k : k + 1, k : k + 1]
        row = jnp.where(lane[:1] == k, 1.0, row) * pivot
        mat = jnp.where(sub == k, row, jnp.where(lane == k, 0.0, mat) - col * row)
    return mat


def gram_kernel(factors, *refs):
    *blocks, thresholds_ref, gram_ref, mat_ref, limits_ref = refs
    limits = 0.25 * thresholds_ref[...].astype(F32)
    limits_ref[...] = jnp.broadcast_to(limits, (limits_ref.shape[1], limits.shape[1])).T
    core = lax.axis_index("path") & 1
    wide = 2 * factors
    gram = jnp.zeros((wide, wide), F32)
    for block in path_blocks(blocks):
        basis = basis_rows(pick(core, *states_of(block, factors)))
        gram = gram + mm_full(basis * weights_of(block, factors), basis, NT)
    gram_ref[...] = gram
    mat_ref[...] = eliminate(gram, range(FIRST_PIVOTS))


def inverse_kernel(gram_ref, mat_ref, inverse_ref):
    gram = gram_ref[...]
    wide = gram.shape[0]
    mat = eliminate(mat_ref[...], range(FIRST_PIVOTS, wide))
    sub = lax.broadcasted_iota(jnp.int32, (wide, wide), 0)
    lane = lax.broadcasted_iota(jnp.int32, (wide, wide), 1)
    mat = mat + mm_full(mat, jnp.where(sub == lane, 1.0, 0.0) - mm_full(gram, mat))
    zero = jnp.zeros_like(mat)
    upper = jnp.concatenate([mat, zero], axis=1)
    inverse_ref[...] = jnp.concatenate([upper, jnp.concatenate([zero, mat], axis=1)], axis=0)


def path_blocks(refs):
    for ref in refs:
        if len(ref.shape) == 2:
            yield ref
        else:
            for index in range(ref.shape[0]):
                yield ref.at[index]


def sum_kernel(*refs):
    total = refs[0][...]
    for ref in refs[1:-1]:
        total = total + ref[...]
    refs[-1][...] = total


def coeff_kernel(*refs):
    total = refs[0][...]
    for ref in refs[1:-2]:
        total = total + ref[...]
    refs[-1][...] = mm_full(total, refs[-2][...])


def exposure_kernel(factors, mine_ref, other_ref, limits_ref, *refs):
    *blocks, exposure_hbm, expected_ref, value_scr, sems = refs
    core = lax.axis_index("path") & 1
    wide = 2 * factors
    paths = blocks[0].shape[1]
    limits = limits_ref[:, :1]
    mine, other = mine_ref[...], other_ref[...]
    coeffs = []
    for packed in (pick(core, mine, other), pick(core, other, mine)):
        hi, lo = split2(jnp.concatenate([packed[:, :wide], packed[:, wide:]], axis=0))
        coeffs.append(jnp.concatenate([hi, hi, lo], axis=1))
    sums = [jnp.zeros((limits.shape[0], 128), F32) for _ in coeffs]
    total = jnp.zeros((1, 1), F32)
    moves = []
    for number, block in enumerate(path_blocks(blocks)):
        weight_row = weights_of(block, factors)
        total = total + jnp.sum(weight_row, keepdims=True)
        for date, state in enumerate(states_of(block, factors)):
            hi, lo = split2(basis_rows(state))
            value = jnp.maximum(mm(coeffs[date], jnp.concatenate([hi, lo, hi], axis=0)) - limits, 0.0)
            if number == 0:
                value_scr[date] = value
                moves.append(pltpu.make_async_copy(value_scr.at[date], exposure_hbm.at[date], sems.at[date]))
                moves[date].start()
            product = value * weight_row
            for c in range(paths // 128):
                sums[date] = sums[date] + product[:, c * 128 : (c + 1) * 128]
    for date, partial in enumerate(sums):
        expected_ref[date : date + 1, :] = jnp.sum(partial.T, axis=0, keepdims=True) / total
    for move in moves:
        move.wait()


def swap(x, axis, away):
    return lax.ppermute(x, axis, [(i, i ^ away) for i in range(lax.axis_size(axis))])


def run(kernel, name, out, specs, args, mib, scratch=(), gflops=0.0, out_specs=None):
    return pl.pallas_call(
        kernel,
        out_shape=out,
        in_specs=specs,
        out_specs=out_specs or jax.tree.map(lambda _: VMEM, out),
        scratch_shapes=list(scratch),
        compiler_params=pltpu.CompilerParams(vmem_limit_bytes=int(mib * MIB)),
        cost_estimate=pl.CostEstimate(flops=int(gflops * 1e9), bytes_accessed=10**5, transcendentals=0),
        name=name,
    )(*args)


def body(
    start_state, shocks, loadings, strikes, notionals, trade_set, live_counts, weights, thresholds
):
    paths, factors = start_state.shape
    dates = shocks.shape[0]
    slots = loadings.shape[1]
    owned = thresholds.shape[0]
    groups = lax.axis_size("trade")
    ranks = lax.axis_size("path")
    wide = 2 * factors
    assert dates == 2

    shape = jax.ShapeDtypeStruct
    start_t, shocks_t, weights_row = start_state.T, jnp.swapaxes(shocks, 1, 2), weights[None, :]
    short, whole = run(
        pack_kernel, "pack_states",
        [shape(((dates - 1) * factors + factors + PAD, paths), F32), shape(((dates + 1) * factors + PAD, paths), F32)],
        [SMEM] + [VMEM] * 3, (live_counts, start_t, shocks_t, weights_row), 58, (), 20.0,
    )
    other = swap(whole, "path", 1)
    across = [swap(short, "path", 2 * away) for away in range(1, ranks // 2)]

    strike_row, notional_row, set_row = strikes[None, :], notionals[None, :], trade_set[None, :]
    nets = run(
        functools.partial(moment_kernel, groups), "net_moments",
        [shape((owned // 2, 2 * wide), F32)] * groups, [VMEM] * 4 + [HBM] * 4,
        (start_t, shocks_t, weights_row, other, loadings, strike_row, notional_row, set_row), 52.75,
        [
            pltpu.VMEM((factors, slots), F32),
            pltpu.VMEM((1, slots), F32),
            pltpu.VMEM((1, slots), F32),
            pltpu.VMEM((1, slots), jnp.int32),
            pltpu.SemaphoreType.DMA((4,)),
            pltpu.VMEM((2 * wide * groups, owned), F32),
            pltpu.VMEM((2 * paths, DEPTH), BF16),
            pltpu.VMEM((2 * wide, 2 * paths), BF16),
            pltpu.VMEM((SLOTS, DEPTH, TILE), BF16),
            pltpu.VMEM((2 * wide * groups, SLOTS * TILE), BF16),
            pltpu.VMEM((owned, SLOTS * TILE), BF16),
        ],
        20.0,
    )
    *across, net = lax.optimization_barrier((*across, nets[0]))
    others = swap(jnp.stack(across), "path", 1)
    got = [swap(nets[away], "trade", away) for away in range(1, groups)]
    blocks = (short, other, *across, others)
    gram, mat, limits = run(
        functools.partial(gram_kernel, factors), "gram_first_pivots",
        [shape((wide, wide), F32)] * 2 + [shape((owned, 128), F32)],
        [VMEM] * (len(blocks) + 1), (*blocks, thresholds[None, :]), 8, (), 5.0,
    )
    mat, net = lax.optimization_barrier((mat, net))
    inverse = run(
        inverse_kernel, "gram_inverse", shape((2 * wide, 2 * wide), F32), [VMEM] * 2, (gram, mat), 8, (), 3.0
    )
    part = run(
        sum_kernel, "group_sum", shape((owned // 2, 2 * wide), F32), [VMEM] * groups, [net] + got, 4
    )
    got = [swap(part, "path", 2 * away) for away in range(1, ranks // 2)]
    mine = run(
        coeff_kernel, "set_coeffs", shape((owned // 2, 2 * wide), F32), [VMEM] * (ranks // 2 + 1),
        [part] + got + [inverse], 4,
    )
    partner = swap(mine, "path", 1)
    exposure, expected = run(
        functools.partial(exposure_kernel, factors), "set_exposure",
        (shape((dates, owned, paths), F32), shape((dates, owned), F32)), [VMEM] * (3 + len(blocks)),
        (mine, partner, limits, *blocks), 16,
        [pltpu.VMEM((dates, owned, paths), F32), pltpu.SemaphoreType.DMA((dates,))], 2.0, (HBM, VMEM),
    )
    return (exposure, expected)


def solution(mesh):
    placed = (
        P("path", None),
        P(None, "path", None),
        P(None, "trade"),
        P("trade"),
        P("trade"),
        P("trade"),
        P(),
        P("path"),
        P("trade"),
    )
    return jax.shard_map(
        body,
        mesh=mesh,
        in_specs=placed,
        out_specs=(P(None, "trade", "path"), P(None, "trade")),
        check_vma=False,
    )
```

```python
import functools

import jax
import jax.numpy as jnp
from jax import lax
from jax.experimental import pallas as pl
from jax.experimental.pallas import tpu as pltpu
from jax.sharding import PartitionSpec as P

HIGHEST_PREC = lax.Precision.HIGHEST
ROOT_HALF = 0.7071067811865476
F32 = jnp.float32
BF16 = jnp.bfloat16
F8 = jnp.float8_e5m2
SCALE = 256.0
TILE = 512
CHUNK = 1024
SLOTS = 4
FIRST_PIVOTS = 36
DEPTH = 256
PAD = 8
MIB = 1024 * 1024
NN = (((1,), (0,)), ((), ()))
NT = (((1,), (1,)), ((), ()))
VMEM = pl.BlockSpec(memory_space=pltpu.VMEM)
SMEM = pl.BlockSpec(memory_space=pltpu.SMEM)
HBM = pl.BlockSpec(memory_space=pltpu.HBM)


def mm(a, b, dims=NN):
    return lax.dot_general(a, b, dims, preferred_element_type=F32)


def mm_full(a, b, dims=NN):
    return lax.dot_general(a, b, dims, preferred_element_type=F32, precision=HIGHEST_PREC)


def split2(x):
    hi = x.astype(BF16)
    return hi, (x - hi.astype(F32)).astype(BF16)


def split3(x):
    hi = x.astype(BF16)
    rest = x - hi.astype(F32)
    mid = rest.astype(BF16)
    return hi, mid, (rest - mid.astype(F32)).astype(BF16)


def log2(n):
    assert n & (n - 1) == 0
    return n.bit_length() - 1


def basis_rows(state):
    return jnp.concatenate([state, (state * state - 1.0) * ROOT_HALF], axis=0)


def pick(core, first, second):
    return jnp.where(core == 0, first, second)


def states_of(ref, factors):
    state = ref[:factors, :]
    return state, 0.8 * state + 0.6 * ref[factors : 2 * factors, :]


def weights_of(ref, factors):
    return ref[2 * factors : 2 * factors + 1, :]


def pack_kernel(counts_ref, start_ref, shocks_ref, weights_ref, short_ref, whole_ref):
    factors, paths = start_ref.shape
    filled = counts_ref[lax.axis_index("trade")].astype(F32)
    spare = lax.broadcasted_iota(jnp.int32, (PAD, paths), 0) > 0
    for ref in (short_ref, whole_ref):
        ref[:factors, :] = start_ref[...]
        ref[factors : 2 * factors, :] = shocks_ref[0]
        ref[2 * factors : 2 * factors + PAD, :] = jnp.where(spare, filled, weights_ref[...].astype(F32))
    whole_ref[2 * factors + PAD :, :] = shocks_ref[1]


def prepare(number, start, shocks, weight_row, states_scr, wide_scr, few_scr):
    core = lax.axis_index("path") & 1
    factors, paths = start.shape
    mine = pl.ds(number * paths, paths)
    second = 0.8 * start + 0.6 * shocks[0]
    third = 0.8 * second + 0.6 * shocks[1]
    weighted = basis_rows(pick(core, start, second)) * weight_row
    few_scr[:, mine] = weighted.astype(F8)
    hi, lo = split2(weighted)
    wide_scr[:, mine] = jnp.concatenate([hi, lo], axis=0)
    hi, mid, low = split3(SCALE * pick(core, second, third))
    hi, mid, low = hi.astype(F32), mid.astype(F32), low.astype(F32)
    ones = jnp.where(lax.broadcasted_iota(jnp.int32, (DEPTH - 6 * factors, paths), 0) < 3, 1.0, 0.0)
    stacked = jnp.concatenate([hi, hi, mid, mid, hi, low, ones], axis=0)
    states_scr[mine, :] = stacked.T.astype(BF16)


def load_rows(cols, load_ref, strike_ref, load_scr, slot):
    factors = load_ref.shape[0]
    hi, mid, low = split3(load_ref[:, cols])
    for part, piece in enumerate((hi, mid, hi, mid, low, hi)):
        load_scr[slot, pl.ds(part * factors, factors), :] = piece
    s_hi, s_mid, s_low = split3(-SCALE * strike_ref[:, cols])
    rows = lax.broadcasted_iota(jnp.int32, (16, TILE), 0)
    strike_rows = jnp.where(rows == 1, s_mid.astype(F32), jnp.where(rows == 2, s_low.astype(F32), 0.0))
    strike_rows = jnp.where(rows == 0, s_hi.astype(F32), strike_rows)
    load_scr[slot, pl.ds(6 * factors, 16), :] = strike_rows.astype(BF16)


def chunk_moments(pay, rows, wide_scr, few_scr):
    wide = wide_scr.shape[0] // 2
    cash = jnp.maximum(pay, 0.0)
    hi = cash.astype(BF16)
    lo = (cash - hi.astype(F32)).astype(F8)
    both = mm(wide_scr[:, rows], hi)
    return both[:wide] + (both[wide:] + mm(few_scr[:, rows], lo))


def tile_at(index):
    return pl.ds(pl.multiple_of(index * TILE, TILE), TILE)


def copies(sources, targets, sems):
    return [pltpu.make_async_copy(src, dst, sems.at[i]) for i, (src, dst) in enumerate(zip(sources, targets))]


def moment_kernel(
    groups, start_ref, shocks_ref, weights_ref, other_ref, load_hbm, strike_hbm, notional_hbm, set_hbm, *refs
):
    outs = refs[:groups]
    *staged, sems, net_scr, states_scr, wide_scr, few_scr, load_scr, part_scr, hot_scr = refs[groups:]
    load_ref, strike_ref, notional_ref, set_ref = staged
    moves = copies((load_hbm, strike_hbm, notional_hbm, set_hbm), staged, sems)
    for move in moves:
        move.start()
    group = lax.axis_index("trade")
    factors = load_ref.shape[0]
    filled = other_ref[2 * factors + 1 : 2 * factors + 2, :1].astype(jnp.int32)
    owned = net_scr.shape[1]
    bits = log2(owned)
    rows = 16
    load_scr[...] = jnp.zeros_like(load_scr)
    for ref in (net_scr, part_scr, hot_scr):
        ref[...] = jnp.zeros_like(ref)
    prepare(0, start_ref[...], shocks_ref[...], weights_ref[...].astype(F32), states_scr, wide_scr, few_scr)
    shocks = (other_ref[factors : 2 * factors, :], other_ref[2 * factors + PAD :, :])
    prepare(1, other_ref[:factors, :], shocks, weights_of(other_ref, factors), states_scr, wide_scr, few_scr)
    for move in moves:
        move.wait()

    chunks = [pl.ds(start, CHUNK) for start in range(0, states_scr.shape[0], CHUNK)]

    def keep_tile(index, slot, moment):
        cols = tile_at(index)
        slot_ids = index * TILE + lax.broadcasted_iota(jnp.int32, (1, TILE), 1)
        hi, lo = split2(moment * jnp.where(slot_ids < filled, notional_ref[:, cols] * (1.0 / SCALE), 0.0))
        both = jnp.concatenate([hi, lo], axis=0)
        both = both.reshape(both.shape[0] // rows, rows, TILE)
        sets = set_ref[:, cols]
        to_group = jnp.broadcast_to((sets >> bits) ^ group, (rows, TILE))
        place = slice(slot * TILE, (slot + 1) * TILE)
        for away in range(groups):
            mask = jnp.where(to_group == away, 1.0, 0.0).astype(BF16)
            size = both.shape[0] * rows
            part_scr[away * size : (away + 1) * size, place] = (both * mask[None]).reshape(-1, TILE)
        one_hot = lax.broadcasted_iota(jnp.int32, (owned, TILE), 0) == (sets & (owned - 1))
        hot_scr[:, place] = jnp.where(one_hot, 1.0, 0.0).astype(BF16)

    def add_tiles():
        net_scr[...] += mm(part_scr[...], hot_scr[...], NT)

    def step(turn, carry):
        add_tiles()
        stages = [(slot, chunk) for slot in range(SLOTS) for chunk in chunks]
        pays, moment = {}, None
        for number in range(len(stages) + 1):
            if number < len(stages):
                slot, chunk = stages[number]
                if number % len(chunks) == 0:
                    load_rows(tile_at(SLOTS * turn + slot), load_ref, strike_ref, load_scr, slot)
                pays[number] = mm(states_scr[chunk, :], load_scr[slot])
            if number > 0:
                slot, chunk = stages[number - 1]
                part = chunk_moments(pays.pop(number - 1), chunk, wide_scr, few_scr)
                moment = part if moment is None else moment + part
                if number % len(chunks) == 0:
                    keep_tile(SLOTS * turn + slot, slot, moment)
                    moment = None
        return carry

    lax.fori_loop(0, (jnp.max(filled) + SLOTS * TILE - 1) // (SLOTS * TILE), step, 0)
    add_tiles()
    wide = net_scr.shape[0] // (2 * groups)
    half = owned // 2
    for away, out in enumerate(outs):
        at = 2 * wide * away
        net = net_scr[at : at + wide, :] + net_scr[at + wide : at + 2 * wide, :]
        out[...] = jnp.concatenate([net[:, :half], net[:, half:]], axis=0).T


def eliminate(mat, pivots):
    sub = lax.broadcasted_iota(jnp.int32, mat.shape, 0)
    lane = lax.broadcasted_iota(jnp.int32, mat.shape, 1)
    for k in pivots:
        row = mat[k : k + 1, :]
        col = mat[:, k : k + 1]
        pivot = 1.0 / mat[k : k + 1, k : k + 1]
        row = jnp.where(lane[:1] == k, 1.0, row) * pivot
        mat = jnp.where(sub == k, row, jnp.where(lane == k, 0.0, mat) - col * row)
    return mat


def gram_kernel(factors, *refs):
    *blocks, thresholds_ref, gram_ref, mat_ref, limits_ref = refs
    limits = 0.25 * thresholds_ref[...].astype(F32)
    limits_ref[...] = jnp.broadcast_to(limits, (limits_ref.shape[1], limits.shape[1])).T
    core = lax.axis_index("path") & 1
    wide = 2 * factors
    gram = jnp.zeros((wide, wide), F32)
    for block in path_blocks(blocks):
        basis = basis_rows(pick(core, *states_of(block, factors)))
        gram = gram + mm_full(basis * weights_of(block, factors), basis, NT)
    gram_ref[...] = gram
    mat_ref[...] = eliminate(gram, range(FIRST_PIVOTS))


def inverse_kernel(gram_ref, mat_ref, inverse_ref):
    gram = gram_ref[...]
    wide = gram.shape[0]
    mat = eliminate(mat_ref[...], range(FIRST_PIVOTS, wide))
    sub = lax.broadcasted_iota(jnp.int32, (wide, wide), 0)
    lane = lax.broadcasted_iota(jnp.int32, (wide, wide), 1)
    mat = mat + mm_full(mat, jnp.where(sub == lane, 1.0, 0.0) - mm_full(gram, mat))
    zero = jnp.zeros_like(mat)
    upper = jnp.concatenate([mat, zero], axis=1)
    inverse_ref[...] = jnp.concatenate([upper, jnp.concatenate([zero, mat], axis=1)], axis=0)


def path_blocks(refs):
    for ref in refs:
        if len(ref.shape) == 2:
            yield ref
        else:
            for index in range(ref.shape[0]):
                yield ref.at[index]


def sum_kernel(*refs):
    total = refs[0][...]
    for ref in refs[1:-1]:
        total = total + ref[...]
    refs[-1][...] = total


def coeff_kernel(*refs):
    total = refs[0][...]
    for ref in refs[1:-2]:
        total = total + ref[...]
    refs[-1][...] = mm_full(total, refs[-2][...])


def exposure_kernel(factors, mine_ref, other_ref, limits_ref, *refs):
    *blocks, exposure_hbm, expected_ref, value_scr, sems = refs
    core = lax.axis_index("path") & 1
    wide = 2 * factors
    paths = blocks[0].shape[1]
    limits = limits_ref[:, :1]
    mine, other = mine_ref[...], other_ref[...]
    coeffs = []
    for packed in (pick(core, mine, other), pick(core, other, mine)):
        hi, lo = split2(jnp.concatenate([packed[:, :wide], packed[:, wide:]], axis=0))
        coeffs.append(jnp.concatenate([hi, hi, lo], axis=1))
    sums = [jnp.zeros((limits.shape[0], 128), F32) for _ in coeffs]
    total = jnp.zeros((1, 1), F32)
    moves = []
    for number, block in enumerate(path_blocks(blocks)):
        weight_row = weights_of(block, factors)
        total = total + jnp.sum(weight_row, keepdims=True)
        for date, state in enumerate(states_of(block, factors)):
            hi, lo = split2(basis_rows(state))
            value = jnp.maximum(mm(coeffs[date], jnp.concatenate([hi, lo, hi], axis=0)) - limits, 0.0)
            if number == 0:
                value_scr[date] = value
                moves.append(pltpu.make_async_copy(value_scr.at[date], exposure_hbm.at[date], sems.at[date]))
                moves[date].start()
            product = value * weight_row
            for c in range(paths // 128):
                sums[date] = sums[date] + product[:, c * 128 : (c + 1) * 128]
    for date, partial in enumerate(sums):
        expected_ref[date : date + 1, :] = jnp.sum(partial.T, axis=0, keepdims=True) / total
    for move in moves:
        move.wait()


def swap(x, axis, away):
    return lax.ppermute(x, axis, [(i, i ^ away) for i in range(lax.axis_size(axis))])


def run(kernel, name, out, specs, args, mib, scratch=(), gflops=0.0, out_specs=None):
    return pl.pallas_call(
        kernel,
        out_shape=out,
        in_specs=specs,
        out_specs=out_specs or jax.tree.map(lambda _: VMEM, out),
        scratch_shapes=list(scratch),
        compiler_params=pltpu.CompilerParams(vmem_limit_bytes=int(mib * MIB)),
        cost_estimate=pl.CostEstimate(flops=int(gflops * 1e9), bytes_accessed=10**5, transcendentals=0),
        name=name,
    )(*args)


def body(
    start_state, shocks, loadings, strikes, notionals, trade_set, live_counts, weights, thresholds
):
    paths, factors = start_state.shape
    dates = shocks.shape[0]
    slots = loadings.shape[1]
    owned = thresholds.shape[0]
    groups = lax.axis_size("trade")
    ranks = lax.axis_size("path")
    wide = 2 * factors
    assert dates == 2

    shape = jax.ShapeDtypeStruct
    start_t, shocks_t, weights_row = start_state.T, jnp.swapaxes(shocks, 1, 2), weights[None, :]
    short, whole = run(
        pack_kernel, "pack_states",
        [shape(((dates - 1) * factors + factors + PAD, paths), F32), shape(((dates + 1) * factors + PAD, paths), F32)],
        [SMEM] + [VMEM] * 3, (live_counts, start_t, shocks_t, weights_row), 58, (), 20.0,
    )
    other = swap(whole, "path", 1)
    across = [swap(short, "path", 2 * away) for away in range(1, ranks // 2)]

    strike_row, notional_row, set_row = strikes[None, :], notionals[None, :], trade_set[None, :]
    nets = run(
        functools.partial(moment_kernel, groups), "net_moments",
        [shape((owned // 2, 2 * wide), F32)] * groups, [VMEM] * 4 + [HBM] * 4,
        (start_t, shocks_t, weights_row, other, loadings, strike_row, notional_row, set_row), 52.75,
        [
            pltpu.VMEM((factors, slots), F32),
            pltpu.VMEM((1, slots), F32),
            pltpu.VMEM((1, slots), F32),
            pltpu.VMEM((1, slots), jnp.int32),
            pltpu.SemaphoreType.DMA((4,)),
            pltpu.VMEM((2 * wide * groups, owned), F32),
            pltpu.VMEM((2 * paths, DEPTH), BF16),
            pltpu.VMEM((2 * wide, 2 * paths), BF16),
            pltpu.VMEM((wide, 2 * paths), F8),
            pltpu.VMEM((SLOTS, DEPTH, TILE), BF16),
            pltpu.VMEM((2 * wide * groups, SLOTS * TILE), BF16),
            pltpu.VMEM((owned, SLOTS * TILE), BF16),
        ],
        20.0,
    )
    *across, net = lax.optimization_barrier((*across, nets[0]))
    others = swap(jnp.stack(across), "path", 1)
    got = [swap(nets[away], "trade", away) for away in range(1, groups)]
    blocks = (short, other, *across, others)
    gram, mat, limits = run(
        functools.partial(gram_kernel, factors), "gram_first_pivots",
        [shape((wide, wide), F32)] * 2 + [shape((owned, 128), F32)],
        [VMEM] * (len(blocks) + 1), (*blocks, thresholds[None, :]), 8, (), 5.0,
    )
    mat, net = lax.optimization_barrier((mat, net))
    inverse = run(
        inverse_kernel, "gram_inverse", shape((2 * wide, 2 * wide), F32), [VMEM] * 2, (gram, mat), 8, (), 3.0
    )
    part = run(
        sum_kernel, "group_sum", shape((owned // 2, 2 * wide), F32), [VMEM] * groups, [net] + got, 4
    )
    got = [swap(part, "path", 2 * away) for away in range(1, ranks // 2)]
    mine = run(
        coeff_kernel, "set_coeffs", shape((owned // 2, 2 * wide), F32), [VMEM] * (ranks // 2 + 1),
        [part] + got + [inverse], 4,
    )
    partner = swap(mine, "path", 1)
    exposure, expected = run(
        functools.partial(exposure_kernel, factors), "set_exposure",
        (shape((dates, owned, paths), F32), shape((dates, owned), F32)), [VMEM] * (3 + len(blocks)),
        (mine, partner, limits, *blocks), 16,
        [pltpu.VMEM((dates, owned, paths), F32), pltpu.SemaphoreType.DMA((dates,))], 2.0, (HBM, VMEM),
    )
    return (exposure, expected)


def solution(mesh):
    placed = (
        P("path", None),
        P(None, "path", None),
        P(None, "trade"),
        P("trade"),
        P("trade"),
        P("trade"),
        P(),
        P("path"),
        P("trade"),
    )
    return jax.shard_map(
        body,
        mesh=mesh,
        in_specs=placed,
        out_specs=(P(None, "trade", "path"), P(None, "trade")),
        check_vma=False,
    )
```

```python
import functools

import jax
import jax.numpy as jnp
from jax import lax
from jax.experimental import pallas as pl
from jax.experimental.pallas import tpu as pltpu
from jax.sharding import PartitionSpec as P

HIGHEST_PREC = lax.Precision.HIGHEST
ROOT_HALF = 0.7071067811865476
F32 = jnp.float32
BF16 = jnp.bfloat16
F8 = jnp.float8_e5m2
SCALE = 256.0
TILE = 512
CHUNK = 1024
SLOTS = 4
FIRST_PIVOTS = 36
DEPTH = 256
PAD = 8
MIB = 1024 * 1024
NN = (((1,), (0,)), ((), ()))
NT = (((1,), (1,)), ((), ()))
VMEM = pl.BlockSpec(memory_space=pltpu.VMEM)
SMEM = pl.BlockSpec(memory_space=pltpu.SMEM)
HBM = pl.BlockSpec(memory_space=pltpu.HBM)


def mm(a, b, dims=NN):
    return lax.dot_general(a, b, dims, preferred_element_type=F32)


def mm_full(a, b, dims=NN):
    return lax.dot_general(a, b, dims, preferred_element_type=F32, precision=HIGHEST_PREC)


def split2(x):
    hi = x.astype(BF16)
    return hi, (x - hi.astype(F32)).astype(BF16)


def split3(x):
    hi = x.astype(BF16)
    rest = x - hi.astype(F32)
    mid = rest.astype(BF16)
    return hi, mid, (rest - mid.astype(F32)).astype(BF16)


def log2(n):
    assert n & (n - 1) == 0
    return n.bit_length() - 1


def basis_rows(state):
    return jnp.concatenate([state, (state * state - 1.0) * ROOT_HALF], axis=0)


def pick(core, first, second):
    return jnp.where(core == 0, first, second)


def states_of(ref, factors):
    state = ref[:factors, :]
    return state, 0.8 * state + 0.6 * ref[factors : 2 * factors, :]


def weights_of(ref, factors):
    return ref[2 * factors : 2 * factors + 1, :]


def pack_kernel(counts_ref, start_ref, shocks_ref, weights_ref, short_ref, whole_ref):
    factors, paths = start_ref.shape
    filled = counts_ref[lax.axis_index("trade")].astype(F32)
    spare = lax.broadcasted_iota(jnp.int32, (PAD, paths), 0) > 0
    for ref in (short_ref, whole_ref):
        ref[:factors, :] = start_ref[...]
        ref[factors : 2 * factors, :] = shocks_ref[0]
        ref[2 * factors : 2 * factors + PAD, :] = jnp.where(spare, filled, weights_ref[...].astype(F32))
    whole_ref[2 * factors + PAD :, :] = shocks_ref[1]


def prepare(number, start, shocks, weight_row, states_scr, wide_scr, few_scr):
    core = lax.axis_index("path") & 1
    factors, paths = start.shape
    mine = pl.ds(number * paths, paths)
    second = 0.8 * start + 0.6 * shocks[0]
    third = 0.8 * second + 0.6 * shocks[1]
    weighted = basis_rows(pick(core, start, second)) * weight_row
    few_scr[:, mine] = weighted.astype(F8)
    hi, lo = split2(weighted)
    wide_scr[:, mine] = jnp.concatenate([hi, lo], axis=0)
    hi, mid, low = split3(SCALE * pick(core, second, third))
    ones = jnp.where(lax.broadcasted_iota(jnp.int32, (DEPTH - 6 * factors, paths), 0) < 3, 1.0, 0.0)
    stacked = jnp.concatenate([hi, hi, mid, mid, hi, low, ones.astype(BF16)], axis=0)
    states_scr[mine, :] = stacked.T


def load_rows(cols, load_ref, strike_ref, load_scr, slot):
    factors = load_ref.shape[0]
    hi, mid, low = split3(load_ref[:, cols])
    for part, piece in enumerate((hi, mid, hi, mid, low, hi)):
        load_scr[slot, pl.ds(part * factors, factors), :] = piece
    s_hi, s_mid, s_low = split3(-SCALE * strike_ref[:, cols])
    rows = lax.broadcasted_iota(jnp.int32, (16, TILE), 0)
    strike_rows = jnp.where(rows == 1, s_mid.astype(F32), jnp.where(rows == 2, s_low.astype(F32), 0.0))
    strike_rows = jnp.where(rows == 0, s_hi.astype(F32), strike_rows)
    load_scr[slot, pl.ds(6 * factors, 16), :] = strike_rows.astype(BF16)


def chunk_moments(pay, rows, wide_scr, few_scr):
    wide = wide_scr.shape[0] // 2
    cash = jnp.maximum(pay, 0.0)
    hi = cash.astype(BF16)
    lo = (cash - hi.astype(F32)).astype(F8)
    both = mm(wide_scr[:, rows], hi)
    return both[:wide] + (both[wide:] + mm(few_scr[:, rows], lo))


def tile_at(index):
    return pl.ds(pl.multiple_of(index * TILE, TILE), TILE)


def copies(sources, targets, sems):
    return [pltpu.make_async_copy(src, dst, sems.at[i]) for i, (src, dst) in enumerate(zip(sources, targets))]


def moment_kernel(
    groups, start_ref, shocks_ref, weights_ref, other_ref, load_hbm, strike_hbm, notional_hbm, set_hbm, *refs
):
    outs = refs[:groups]
    *staged, sems, net_scr, states_scr, wide_scr, few_scr, load_scr, part_scr, hot_scr = refs[groups:]
    load_ref, strike_ref, notional_ref, set_ref = staged
    moves = copies((load_hbm, strike_hbm, notional_hbm, set_hbm), staged, sems)
    for move in moves:
        move.start()
    group = lax.axis_index("trade")
    factors = load_ref.shape[0]
    filled = other_ref[2 * factors + 1 : 2 * factors + 2, :1].astype(jnp.int32)
    owned = net_scr.shape[1]
    bits = log2(owned)
    rows = 16
    load_scr[...] = jnp.zeros_like(load_scr)
    net_scr[...] = jnp.zeros_like(net_scr)
    prepare(0, start_ref[...], shocks_ref[...], weights_ref[...].astype(F32), states_scr, wide_scr, few_scr)
    shocks = (other_ref[factors : 2 * factors, :], other_ref[2 * factors + PAD :, :])
    prepare(1, other_ref[:factors, :], shocks, weights_of(other_ref, factors), states_scr, wide_scr, few_scr)
    for move in moves:
        move.wait()

    chunks = [pl.ds(start, CHUNK) for start in range(0, states_scr.shape[0], CHUNK)]

    def keep_tile(index, slot, moment):
        cols = tile_at(index)
        slot_ids = index * TILE + lax.broadcasted_iota(jnp.int32, (1, TILE), 1)
        hi, lo = split2(moment * jnp.where(slot_ids < filled, notional_ref[:, cols] * (1.0 / SCALE), 0.0))
        both = jnp.concatenate([hi, lo], axis=0)
        both = both.reshape(both.shape[0] // rows, rows, TILE)
        sets = set_ref[:, cols]
        to_group = jnp.broadcast_to((sets >> bits) ^ group, (rows, TILE))
        place = slice(slot * TILE, (slot + 1) * TILE)
        for away in range(groups):
            mask = jnp.where(to_group == away, 1.0, 0.0).astype(BF16)
            size = both.shape[0] * rows
            part_scr[away * size : (away + 1) * size, place] = (both * mask[None]).reshape(-1, TILE)
        one_hot = lax.broadcasted_iota(jnp.int32, (owned, TILE), 0) == (sets & (owned - 1))
        hot_scr[:, place] = jnp.where(one_hot, 1.0, 0.0).astype(BF16)

    def add_tiles():
        net_scr[...] += mm(part_scr[...], hot_scr[...], NT)

    def step(turn, carry):
        if carry is not None:
            add_tiles()
        stages = [(slot, chunk) for slot in range(SLOTS) for chunk in chunks]
        pays, moment = {}, None
        for number in range(len(stages) + 1):
            if number < len(stages):
                slot, chunk = stages[number]
                if number % len(chunks) == 0:
                    load_rows(tile_at(SLOTS * turn + slot), load_ref, strike_ref, load_scr, slot)
                pays[number] = mm(states_scr[chunk, :], load_scr[slot])
            if number > 0:
                slot, chunk = stages[number - 1]
                part = chunk_moments(pays.pop(number - 1), chunk, wide_scr, few_scr)
                moment = part if moment is None else moment + part
                if number % len(chunks) == 0:
                    keep_tile(SLOTS * turn + slot, slot, moment)
                    moment = None
        return carry

    step(0, None)
    lax.fori_loop(1, (jnp.max(filled) + SLOTS * TILE - 1) // (SLOTS * TILE), step, 0)
    add_tiles()
    wide = net_scr.shape[0] // (2 * groups)
    half = owned // 2
    for away, out in enumerate(outs):
        at = 2 * wide * away
        net = net_scr[at : at + wide, :] + net_scr[at + wide : at + 2 * wide, :]
        out[...] = jnp.concatenate([net[:, :half], net[:, half:]], axis=0).T


def eliminate(mat, pivots):
    sub = lax.broadcasted_iota(jnp.int32, mat.shape, 0)
    lane = lax.broadcasted_iota(jnp.int32, mat.shape, 1)
    for k in pivots:
        row = mat[k : k + 1, :]
        col = mat[:, k : k + 1]
        pivot = 1.0 / mat[k : k + 1, k : k + 1]
        row = jnp.where(lane[:1] == k, 1.0, row) * pivot
        mat = jnp.where(sub == k, row, jnp.where(lane == k, 0.0, mat) - col * row)
    return mat


def gram_kernel(factors, *refs):
    *blocks, thresholds_ref, gram_ref, mat_ref, limits_ref = refs
    limits = 0.25 * thresholds_ref[...].astype(F32)
    limits_ref[...] = jnp.broadcast_to(limits, (limits_ref.shape[1], limits.shape[1])).T
    core = lax.axis_index("path") & 1
    wide = 2 * factors
    gram = jnp.zeros((wide, wide), F32)
    for block in path_blocks(blocks):
        basis = basis_rows(pick(core, *states_of(block, factors)))
        gram = gram + mm_full(basis * weights_of(block, factors), basis, NT)
    gram_ref[...] = gram
    mat_ref[...] = eliminate(gram, range(FIRST_PIVOTS))


def inverse_kernel(gram_ref, mat_ref, inverse_ref):
    gram = gram_ref[...]
    wide = gram.shape[0]
    mat = eliminate(mat_ref[...], range(FIRST_PIVOTS, wide))
    sub = lax.broadcasted_iota(jnp.int32, (wide, wide), 0)
    lane = lax.broadcasted_iota(jnp.int32, (wide, wide), 1)
    mat = mat + mm_full(mat, jnp.where(sub == lane, 1.0, 0.0) - mm_full(gram, mat))
    zero = jnp.zeros_like(mat)
    upper = jnp.concatenate([mat, zero], axis=1)
    inverse_ref[...] = jnp.concatenate([upper, jnp.concatenate([zero, mat], axis=1)], axis=0)


def path_blocks(refs):
    for ref in refs:
        if len(ref.shape) == 2:
            yield ref
        else:
            for index in range(ref.shape[0]):
                yield ref.at[index]


def sum_kernel(*refs):
    total = refs[0][...]
    for ref in refs[1:-1]:
        total = total + ref[...]
    refs[-1][...] = total


def coeff_kernel(*refs):
    total = refs[0][...]
    for ref in refs[1:-2]:
        total = total + ref[...]
    refs[-1][...] = mm_full(total, refs[-2][...])


def exposure_kernel(factors, mine_ref, other_ref, limits_ref, *refs):
    *blocks, exposure_hbm, expected_ref, value_scr, sems = refs
    core = lax.axis_index("path") & 1
    wide = 2 * factors
    paths = blocks[0].shape[1]
    limits = limits_ref[:, :1]
    mine, other = mine_ref[...], other_ref[...]
    coeffs = []
    for packed in (pick(core, mine, other), pick(core, other, mine)):
        hi, lo = split2(jnp.concatenate([packed[:, :wide], packed[:, wide:]], axis=0))
        coeffs.append(jnp.concatenate([hi, hi, lo], axis=1))
    sums = [jnp.zeros((limits.shape[0], 128), F32) for _ in coeffs]
    total = jnp.zeros((1, 1), F32)
    moves = []
    for number, block in enumerate(path_blocks(blocks)):
        weight_row = weights_of(block, factors)
        total = total + jnp.sum(weight_row, keepdims=True)
        for date, state in enumerate(states_of(block, factors)):
            hi, lo = split2(basis_rows(state))
            value = jnp.maximum(mm(coeffs[date], jnp.concatenate([hi, lo, hi], axis=0)) - limits, 0.0)
            if number == 0:
                value_scr[date] = value
                moves.append(pltpu.make_async_copy(value_scr.at[date], exposure_hbm.at[date], sems.at[date]))
                moves[date].start()
            product = value * weight_row
            for c in range(paths // 128):
                sums[date] = sums[date] + product[:, c * 128 : (c + 1) * 128]
    for date, partial in enumerate(sums):
        expected_ref[date : date + 1, :] = jnp.sum(partial.T, axis=0, keepdims=True) / total
    for move in moves:
        move.wait()


def swap(x, axis, away):
    return lax.ppermute(x, axis, [(i, i ^ away) for i in range(lax.axis_size(axis))])


def run(kernel, name, out, specs, args, mib, scratch=(), gflops=0.0, out_specs=None):
    return pl.pallas_call(
        kernel,
        out_shape=out,
        in_specs=specs,
        out_specs=out_specs or jax.tree.map(lambda _: VMEM, out),
        scratch_shapes=list(scratch),
        compiler_params=pltpu.CompilerParams(vmem_limit_bytes=int(mib * MIB)),
        cost_estimate=pl.CostEstimate(flops=int(gflops * 1e9), bytes_accessed=10**5, transcendentals=0),
        name=name,
    )(*args)


def body(
    start_state, shocks, loadings, strikes, notionals, trade_set, live_counts, weights, thresholds
):
    paths, factors = start_state.shape
    dates = shocks.shape[0]
    slots = loadings.shape[1]
    owned = thresholds.shape[0]
    groups = lax.axis_size("trade")
    ranks = lax.axis_size("path")
    wide = 2 * factors
    assert dates == 2

    shape = jax.ShapeDtypeStruct
    start_t, shocks_t, weights_row = start_state.T, jnp.swapaxes(shocks, 1, 2), weights[None, :]
    short, whole = run(
        pack_kernel, "pack_states",
        [shape(((dates - 1) * factors + factors + PAD, paths), F32), shape(((dates + 1) * factors + PAD, paths), F32)],
        [SMEM] + [VMEM] * 3, (live_counts, start_t, shocks_t, weights_row), 58, (), 20.0,
    )
    other = swap(whole, "path", 1)
    across = [swap(short, "path", 2 * away) for away in range(1, ranks // 2)]

    strike_row, notional_row, set_row = strikes[None, :], notionals[None, :], trade_set[None, :]
    nets = run(
        functools.partial(moment_kernel, groups), "net_moments",
        [shape((owned // 2, 2 * wide), F32)] * groups, [VMEM] * 4 + [HBM] * 4,
        (start_t, shocks_t, weights_row, other, loadings, strike_row, notional_row, set_row), 52.75,
        [
            pltpu.VMEM((factors, slots), F32),
            pltpu.VMEM((1, slots), F32),
            pltpu.VMEM((1, slots), F32),
            pltpu.VMEM((1, slots), jnp.int32),
            pltpu.SemaphoreType.DMA((4,)),
            pltpu.VMEM((2 * wide * groups, owned), F32),
            pltpu.VMEM((2 * paths, DEPTH), BF16),
            pltpu.VMEM((2 * wide, 2 * paths), BF16),
            pltpu.VMEM((wide, 2 * paths), F8),
            pltpu.VMEM((SLOTS, DEPTH, TILE), BF16),
            pltpu.VMEM((2 * wide * groups, SLOTS * TILE), BF16),
            pltpu.VMEM((owned, SLOTS * TILE), BF16),
        ],
        20.0,
    )
    *across, net = lax.optimization_barrier((*across, nets[0]))
    others = swap(jnp.stack(across), "path", 1)
    got = [swap(nets[away], "trade", away) for away in range(1, groups)]
    blocks = (short, other, *across, others)
    gram, mat, limits = run(
        functools.partial(gram_kernel, factors), "gram_first_pivots",
        [shape((wide, wide), F32)] * 2 + [shape((owned, 128), F32)],
        [VMEM] * (len(blocks) + 1), (*blocks, thresholds[None, :]), 8, (), 5.0,
    )
    mat, net = lax.optimization_barrier((mat, net))
    inverse = run(
        inverse_kernel, "gram_inverse", shape((2 * wide, 2 * wide), F32), [VMEM] * 2, (gram, mat), 8, (), 3.0
    )
    part = run(
        sum_kernel, "group_sum", shape((owned // 2, 2 * wide), F32), [VMEM] * groups, [net] + got, 4
    )
    got = [swap(part, "path", 2 * away) for away in range(1, ranks // 2)]
    mine = run(
        coeff_kernel, "set_coeffs", shape((owned // 2, 2 * wide), F32), [VMEM] * (ranks // 2 + 1),
        [part] + got + [inverse], 4,
    )
    partner = swap(mine, "path", 1)
    exposure, expected = run(
        functools.partial(exposure_kernel, factors), "set_exposure",
        (shape((dates, owned, paths), F32), shape((dates, owned), F32)), [VMEM] * (3 + len(blocks)),
        (mine, partner, limits, *blocks), 16,
        [pltpu.VMEM((dates, owned, paths), F32), pltpu.SemaphoreType.DMA((dates,))], 2.0, (HBM, VMEM),
    )
    return (exposure, expected)


def solution(mesh):
    placed = (
        P("path", None),
        P(None, "path", None),
        P(None, "trade"),
        P("trade"),
        P("trade"),
        P("trade"),
        P(),
        P("path"),
        P("trade"),
    )
    return jax.shard_map(
        body,
        mesh=mesh,
        in_specs=placed,
        out_specs=(P(None, "trade", "path"), P(None, "trade")),
        check_vma=False,
    )
```

```python
import functools

import jax
import jax.numpy as jnp
from jax import lax
from jax.experimental import pallas as pl
from jax.experimental.pallas import tpu as pltpu
from jax.sharding import PartitionSpec as P

HIGHEST_PREC = lax.Precision.HIGHEST
ROOT_HALF = 0.7071067811865476
F32 = jnp.float32
BF16 = jnp.bfloat16
F8 = jnp.float8_e5m2
SCALE = 256.0
TILE = 512
CHUNK = 1024
SLOTS = 8
FIRST_PIVOTS = 36
DEPTH = 256
PAD = 8
MIB = 1024 * 1024
NN = (((1,), (0,)), ((), ()))
NT = (((1,), (1,)), ((), ()))
VMEM = pl.BlockSpec(memory_space=pltpu.VMEM)
SMEM = pl.BlockSpec(memory_space=pltpu.SMEM)
HBM = pl.BlockSpec(memory_space=pltpu.HBM)


def mm(a, b, dims=NN):
    return lax.dot_general(a, b, dims, preferred_element_type=F32)


def mm_full(a, b, dims=NN):
    return lax.dot_general(a, b, dims, preferred_element_type=F32, precision=HIGHEST_PREC)


def split2(x):
    hi = x.astype(BF16)
    return hi, (x - hi.astype(F32)).astype(BF16)


def split3(x):
    hi = x.astype(BF16)
    rest = x - hi.astype(F32)
    mid = rest.astype(BF16)
    return hi, mid, (rest - mid.astype(F32)).astype(BF16)


def log2(n):
    assert n & (n - 1) == 0
    return n.bit_length() - 1


def basis_rows(state):
    return jnp.concatenate([state, (state * state - 1.0) * ROOT_HALF], axis=0)


def pick(core, first, second):
    return jnp.where(core == 0, first, second)


def states_of(ref, factors):
    state = ref[:factors, :]
    return state, 0.8 * state + 0.6 * ref[factors : 2 * factors, :]


def weights_of(ref, factors):
    return ref[2 * factors : 2 * factors + 1, :]


def pack_kernel(counts_ref, start_ref, shocks_ref, weights_ref, short_ref, whole_ref):
    factors, paths = start_ref.shape
    filled = counts_ref[lax.axis_index("trade")].astype(F32)
    spare = lax.broadcasted_iota(jnp.int32, (PAD, paths), 0) > 0
    for ref in (short_ref, whole_ref):
        ref[:factors, :] = start_ref[...]
        ref[factors : 2 * factors, :] = shocks_ref[0]
        ref[2 * factors : 2 * factors + PAD, :] = jnp.where(spare, filled, weights_ref[...].astype(F32))
    whole_ref[2 * factors + PAD :, :] = shocks_ref[1]


def prepare(number, start, shocks, weight_row, states_scr, wide_scr, few_scr):
    core = lax.axis_index("path") & 1
    factors, paths = start.shape
    mine = pl.ds(number * paths, paths)
    second = 0.8 * start + 0.6 * shocks[0]
    third = 0.8 * second + 0.6 * shocks[1]
    weighted = basis_rows(pick(core, start, second)) * weight_row
    few_scr[:, mine] = weighted.astype(F8)
    hi, lo = split2(weighted)
    wide_scr[:, mine] = jnp.concatenate([hi, lo], axis=0)
    hi, mid, low = split3(SCALE * pick(core, second, third))
    hi, mid, low = hi.astype(F32), mid.astype(F32), low.astype(F32)
    ones = jnp.where(lax.broadcasted_iota(jnp.int32, (DEPTH - 6 * factors, paths), 0) < 3, 1.0, 0.0)
    stacked = jnp.concatenate([hi, hi, mid, mid, hi, low, ones], axis=0)
    states_scr[mine, :] = stacked.T.astype(BF16)


def load_rows(cols, load_ref, strike_ref, load_scr, slot):
    factors = load_ref.shape[0]
    hi, mid, low = split3(load_ref[:, cols])
    for part, piece in enumerate((hi, mid, hi, mid, low, hi)):
        load_scr[slot, pl.ds(part * factors, factors), :] = piece
    s_hi, s_mid, s_low = split3(-SCALE * strike_ref[:, cols])
    rows = lax.broadcasted_iota(jnp.int32, (16, TILE), 0)
    strike_rows = jnp.where(rows == 1, s_mid.astype(F32), jnp.where(rows == 2, s_low.astype(F32), 0.0))
    strike_rows = jnp.where(rows == 0, s_hi.astype(F32), strike_rows)
    load_scr[slot, pl.ds(6 * factors, 16), :] = strike_rows.astype(BF16)


def chunk_moments(pay, rows, wide_scr, few_scr):
    wide = wide_scr.shape[0] // 2
    cash = jnp.maximum(pay, 0.0)
    hi = cash.astype(BF16)
    lo = (cash - hi.astype(F32)).astype(F8)
    both = mm(wide_scr[:, rows], hi)
    return both[:wide] + (both[wide:] + mm(few_scr[:, rows], lo))


def tile_at(index):
    return pl.ds(pl.multiple_of(index * TILE, TILE), TILE)


def copies(sources, targets, sems):
    return [pltpu.make_async_copy(src, dst, sems.at[i]) for i, (src, dst) in enumerate(zip(sources, targets))]


def moment_kernel(
    groups, start_ref, shocks_ref, weights_ref, other_ref, load_hbm, strike_hbm, notional_hbm, set_hbm, *refs
):
    outs = refs[:groups]
    *staged, sems, net_scr, states_scr, wide_scr, few_scr, load_scr, part_scr, hot_scr = refs[groups:]
    load_ref, strike_ref, notional_ref, set_ref = staged
    moves = copies((load_hbm, strike_hbm, notional_hbm, set_hbm), staged, sems)
    for move in moves:
        move.start()
    group = lax.axis_index("trade")
    factors = load_ref.shape[0]
    filled = other_ref[2 * factors + 1 : 2 * factors + 2, :1].astype(jnp.int32)
    owned = net_scr.shape[1]
    bits = log2(owned)
    rows = 16
    load_scr[...] = jnp.zeros_like(load_scr)
    for ref in (net_scr, part_scr, hot_scr):
        ref[...] = jnp.zeros_like(ref)
    prepare(0, start_ref[...], shocks_ref[...], weights_ref[...].astype(F32), states_scr, wide_scr, few_scr)
    shocks = (other_ref[factors : 2 * factors, :], other_ref[2 * factors + PAD :, :])
    prepare(1, other_ref[:factors, :], shocks, weights_of(other_ref, factors), states_scr, wide_scr, few_scr)
    for move in moves:
        move.wait()

    chunks = [pl.ds(start, CHUNK) for start in range(0, states_scr.shape[0], CHUNK)]

    def keep_tile(index, slot, moment):
        cols = tile_at(index)
        slot_ids = index * TILE + lax.broadcasted_iota(jnp.int32, (1, TILE), 1)
        hi, lo = split2(moment * jnp.where(slot_ids < filled, notional_ref[:, cols] * (1.0 / SCALE), 0.0))
        both = jnp.concatenate([hi, lo], axis=0)
        both = both.reshape(both.shape[0] // rows, rows, TILE)
        sets = set_ref[:, cols]
        to_group = jnp.broadcast_to((sets >> bits) ^ group, (rows, TILE))
        place = slice(slot * TILE, (slot + 1) * TILE)
        for away in range(groups):
            mask = jnp.where(to_group == away, 1.0, 0.0).astype(BF16)
            size = both.shape[0] * rows
            part_scr[away * size : (away + 1) * size, place] = (both * mask[None]).reshape(-1, TILE)
        one_hot = lax.broadcasted_iota(jnp.int32, (owned, TILE), 0) == (sets & (owned - 1))
        hot_scr[:, place] = jnp.where(one_hot, 1.0, 0.0).astype(BF16)

    def add_tiles():
        net_scr[...] += mm(part_scr[...], hot_scr[...], NT)

    def step(turn, carry):
        add_tiles()
        stages = [(slot, chunk) for slot in range(SLOTS) for chunk in chunks]
        pays, moment = {}, None
        for number in range(len(stages) + 1):
            if number < len(stages):
                slot, chunk = stages[number]
                if number % len(chunks) == 0:
                    load_rows(tile_at(SLOTS * turn + slot), load_ref, strike_ref, load_scr, slot)
                pays[number] = mm(states_scr[chunk, :], load_scr[slot])
            if number > 0:
                slot, chunk = stages[number - 1]
                part = chunk_moments(pays.pop(number - 1), chunk, wide_scr, few_scr)
                moment = part if moment is None else moment + part
                if number % len(chunks) == 0:
                    keep_tile(SLOTS * turn + slot, slot, moment)
                    moment = None
        return carry

    lax.fori_loop(0, (jnp.max(filled) + SLOTS * TILE - 1) // (SLOTS * TILE), step, 0)
    add_tiles()
    wide = net_scr.shape[0] // (2 * groups)
    half = owned // 2
    for away, out in enumerate(outs):
        at = 2 * wide * away
        net = net_scr[at : at + wide, :] + net_scr[at + wide : at + 2 * wide, :]
        out[...] = jnp.concatenate([net[:, :half], net[:, half:]], axis=0).T


def eliminate(mat, pivots):
    sub = lax.broadcasted_iota(jnp.int32, mat.shape, 0)
    lane = lax.broadcasted_iota(jnp.int32, mat.shape, 1)
    for k in pivots:
        row = mat[k : k + 1, :]
        col = mat[:, k : k + 1]
        pivot = 1.0 / mat[k : k + 1, k : k + 1]
        row = jnp.where(lane[:1] == k, 1.0, row) * pivot
        mat = jnp.where(sub == k, row, jnp.where(lane == k, 0.0, mat) - col * row)
    return mat


def gram_kernel(factors, *refs):
    *blocks, thresholds_ref, gram_ref, mat_ref, limits_ref = refs
    limits = 0.25 * thresholds_ref[...].astype(F32)
    limits_ref[...] = jnp.broadcast_to(limits, (limits_ref.shape[1], limits.shape[1])).T
    core = lax.axis_index("path") & 1
    wide = 2 * factors
    gram = jnp.zeros((wide, wide), F32)
    for block in path_blocks(blocks):
        basis = basis_rows(pick(core, *states_of(block, factors)))
        gram = gram + mm_full(basis * weights_of(block, factors), basis, NT)
    gram_ref[...] = gram
    mat_ref[...] = eliminate(gram, range(FIRST_PIVOTS))


def inverse_kernel(gram_ref, mat_ref, inverse_ref):
    gram = gram_ref[...]
    wide = gram.shape[0]
    mat = eliminate(mat_ref[...], range(FIRST_PIVOTS, wide))
    sub = lax.broadcasted_iota(jnp.int32, (wide, wide), 0)
    lane = lax.broadcasted_iota(jnp.int32, (wide, wide), 1)
    mat = mat + mm_full(mat, jnp.where(sub == lane, 1.0, 0.0) - mm_full(gram, mat))
    zero = jnp.zeros_like(mat)
    upper = jnp.concatenate([mat, zero], axis=1)
    inverse_ref[...] = jnp.concatenate([upper, jnp.concatenate([zero, mat], axis=1)], axis=0)


def path_blocks(refs):
    for ref in refs:
        if len(ref.shape) == 2:
            yield ref
        else:
            for index in range(ref.shape[0]):
                yield ref.at[index]


def sum_kernel(*refs):
    total = refs[0][...]
    for ref in refs[1:-1]:
        total = total + ref[...]
    refs[-1][...] = total


def coeff_kernel(*refs):
    total = refs[0][...]
    for ref in refs[1:-2]:
        total = total + ref[...]
    refs[-1][...] = mm_full(total, refs[-2][...])


def exposure_kernel(factors, mine_ref, other_ref, limits_ref, *refs):
    *blocks, exposure_hbm, expected_ref, value_scr, sems = refs
    core = lax.axis_index("path") & 1
    wide = 2 * factors
    paths = blocks[0].shape[1]
    limits = limits_ref[:, :1]
    mine, other = mine_ref[...], other_ref[...]
    coeffs = []
    for packed in (pick(core, mine, other), pick(core, other, mine)):
        hi, lo = split2(jnp.concatenate([packed[:, :wide], packed[:, wide:]], axis=0))
        coeffs.append(jnp.concatenate([hi, hi, lo], axis=1))
    sums = [jnp.zeros((limits.shape[0], 128), F32) for _ in coeffs]
    total = jnp.zeros((1, 1), F32)
    moves = []
    for number, block in enumerate(path_blocks(blocks)):
        weight_row = weights_of(block, factors)
        total = total + jnp.sum(weight_row, keepdims=True)
        for date, state in enumerate(states_of(block, factors)):
            hi, lo = split2(basis_rows(state))
            value = jnp.maximum(mm(coeffs[date], jnp.concatenate([hi, lo, hi], axis=0)) - limits, 0.0)
            if number == 0:
                value_scr[date] = value
                moves.append(pltpu.make_async_copy(value_scr.at[date], exposure_hbm.at[date], sems.at[date]))
                moves[date].start()
            product = value * weight_row
            for c in range(paths // 128):
                sums[date] = sums[date] + product[:, c * 128 : (c + 1) * 128]
    for date, partial in enumerate(sums):
        expected_ref[date : date + 1, :] = jnp.sum(partial.T, axis=0, keepdims=True) / total
    for move in moves:
        move.wait()


def swap(x, axis, away):
    return lax.ppermute(x, axis, [(i, i ^ away) for i in range(lax.axis_size(axis))])


def run(kernel, name, out, specs, args, mib, scratch=(), gflops=0.0, out_specs=None):
    return pl.pallas_call(
        kernel,
        out_shape=out,
        in_specs=specs,
        out_specs=out_specs or jax.tree.map(lambda _: VMEM, out),
        scratch_shapes=list(scratch),
        compiler_params=pltpu.CompilerParams(vmem_limit_bytes=int(mib * MIB)),
        cost_estimate=pl.CostEstimate(flops=int(gflops * 1e9), bytes_accessed=10**5, transcendentals=0),
        name=name,
    )(*args)


def body(
    start_state, shocks, loadings, strikes, notionals, trade_set, live_counts, weights, thresholds
):
    paths, factors = start_state.shape
    dates = shocks.shape[0]
    slots = loadings.shape[1]
    owned = thresholds.shape[0]
    groups = lax.axis_size("trade")
    ranks = lax.axis_size("path")
    wide = 2 * factors
    assert dates == 2

    shape = jax.ShapeDtypeStruct
    start_t, shocks_t, weights_row = start_state.T, jnp.swapaxes(shocks, 1, 2), weights[None, :]
    short, whole = run(
        pack_kernel, "pack_states",
        [shape(((dates - 1) * factors + factors + PAD, paths), F32), shape(((dates + 1) * factors + PAD, paths), F32)],
        [SMEM] + [VMEM] * 3, (live_counts, start_t, shocks_t, weights_row), 58, (), 20.0,
    )
    other = swap(whole, "path", 1)
    across = [swap(short, "path", 2 * away) for away in range(1, ranks // 2)]

    strike_row, notional_row, set_row = strikes[None, :], notionals[None, :], trade_set[None, :]
    nets = run(
        functools.partial(moment_kernel, groups), "net_moments",
        [shape((owned // 2, 2 * wide), F32)] * groups, [VMEM] * 4 + [HBM] * 4,
        (start_t, shocks_t, weights_row, other, loadings, strike_row, notional_row, set_row), 52.75,
        [
            pltpu.VMEM((factors, slots), F32),
            pltpu.VMEM((1, slots), F32),
            pltpu.VMEM((1, slots), F32),
            pltpu.VMEM((1, slots), jnp.int32),
            pltpu.SemaphoreType.DMA((4,)),
            pltpu.VMEM((2 * wide * groups, owned), F32),
            pltpu.VMEM((2 * paths, DEPTH), BF16),
            pltpu.VMEM((2 * wide, 2 * paths), BF16),
            pltpu.VMEM((wide, 2 * paths), F8),
            pltpu.VMEM((SLOTS, DEPTH, TILE), BF16),
            pltpu.VMEM((2 * wide * groups, SLOTS * TILE), BF16),
            pltpu.VMEM((owned, SLOTS * TILE), BF16),
        ],
        20.0,
    )
    *across, net = lax.optimization_barrier((*across, nets[0]))
    others = swap(jnp.stack(across), "path", 1)
    got = [swap(nets[away], "trade", away) for away in range(1, groups)]
    blocks = (short, other, *across, others)
    gram, mat, limits = run(
        functools.partial(gram_kernel, factors), "gram_first_pivots",
        [shape((wide, wide), F32)] * 2 + [shape((owned, 128), F32)],
        [VMEM] * (len(blocks) + 1), (*blocks, thresholds[None, :]), 8, (), 5.0,
    )
    mat, net = lax.optimization_barrier((mat, net))
    inverse = run(
        inverse_kernel, "gram_inverse", shape((2 * wide, 2 * wide), F32), [VMEM] * 2, (gram, mat), 8, (), 3.0
    )
    part = run(
        sum_kernel, "group_sum", shape((owned // 2, 2 * wide), F32), [VMEM] * groups, [net] + got, 4
    )
    got = [swap(part, "path", 2 * away) for away in range(1, ranks // 2)]
    mine = run(
        coeff_kernel, "set_coeffs", shape((owned // 2, 2 * wide), F32), [VMEM] * (ranks // 2 + 1),
        [part] + got + [inverse], 4,
    )
    partner = swap(mine, "path", 1)
    exposure, expected = run(
        functools.partial(exposure_kernel, factors), "set_exposure",
        (shape((dates, owned, paths), F32), shape((dates, owned), F32)), [VMEM] * (3 + len(blocks)),
        (mine, partner, limits, *blocks), 16,
        [pltpu.VMEM((dates, owned, paths), F32), pltpu.SemaphoreType.DMA((dates,))], 2.0, (HBM, VMEM),
    )
    return (exposure, expected)


def solution(mesh):
    placed = (
        P("path", None),
        P(None, "path", None),
        P(None, "trade"),
        P("trade"),
        P("trade"),
        P("trade"),
        P(),
        P("path"),
        P("trade"),
    )
    return jax.shard_map(
        body,
        mesh=mesh,
        in_specs=placed,
        out_specs=(P(None, "trade", "path"), P(None, "trade")),
        check_vma=False,
    )
```
